32 devices in a mesh: sess: 8 (over z, x), act: 4 (over y, core).
Axes of the slice: x: 2, y: 2, z: 4, core: 2. Of those that a mesh axis runs over, the one named last changes fastest.
Arguments:
- hist: bfloat16 [4096, 131072], P('sess', 'act'), may hold values from 0.049804688 to 5
- tile_mask: int32 [32, 1024], P('sess', 'act'), may hold values 0 or 1
- planes: bfloat16 [131072, 1024], P('act', 'sess'), may hold values from -0.015625 to 0.015625
- pairs: int32 [128, 2], P('sess'), may hold values from 0 to 31
Outputs:
- scores: float32 [128, 128, 128], P(('sess', 'act'))
The draws below stay inside these ranges and needn't reach their ends.
All inputs are finite; a program needn't handle non-finite values. No bound on the sum of `tile_mask` on one device may be relied on, other than what follows from the above.
Results may differ from the reference program's by a relative error of at most 0.0003.
Values may be sent and summed in bfloat16 or wider, within the bound.
No kernel may reach another device: no remote copies, remote signals or barrier semaphores. Data moves between devices by JAX's collectives and lax.ppermute only.
A program may use at most 192 MiB of HBM per device.

```python
import math
import jax
import jax.numpy as jnp
from jax import lax

A = 131072
P_SIZE = 1024
BLK = 128
SESSIONS = 4096
NB = 32
NPAIR = 128


def set_ends(result, rng, least, high):
    extent = result.shape
    spot = [jax.random.randint(jax.random.fold_in(rng, axis), (), 0, extent[axis]) for axis in range(len(extent))]
    result = result.at[tuple(spot)].set(least)
    longest = extent.index(max(extent))
    spot[longest] = (spot[longest] + 1) % extent[longest]
    return result.at[tuple(spot)].set(high)


def block_scale(own_key, extent, split, low, high):
    level = 1.0
    for dim, shards_of in split:
        heights = jax.random.uniform(jax.random.fold_in(jax.random.fold_in(own_key, 6), dim), (shards_of,), jnp.float32, low / len(split), high / len(split))
        level = level * jnp.repeat(jnp.exp(heights), extent[dim] // shards_of).reshape((-1,) + (1,) * (len(extent) - 1 - dim))
    return level


def centred(rng, extent, spread, limit, split=(), held_as=jnp.bfloat16):
    result = jax.random.normal(rng, extent, jnp.float32) * spread
    if len(split) > 0:
        result = block_scale(rng, extent, split, -0.22, 0.18) * result
    return jnp.clip(result, min=-limit, max=limit).astype(held_as)


def setup_inputs(seed: int = 0) -> dict:
    splits = jax.random.split(jax.random.key(seed), 5)
    hist = jnp.clip(jnp.exp(math.log(5.0) - 4.609084 * jax.random.uniform(splits[0], (SESSIONS, A), jnp.float32) ** block_scale(splits[0], (SESSIONS, A), ((0, 8), (1, 4)), -0.2, 0.2)), 0.049804688, 5.0).astype(jnp.bfloat16)
    tile_mask = set_ends((jax.random.randint(splits[1], (NB, A // BLK), 0, 2) < 1).astype(jnp.int32), jax.random.fold_in(splits[1], 1), 0, 1)
    planes = centred(splits[2], (A, P_SIZE), A ** -0.5, 0.015625, ((0, 4), (1, 8)))
    pairs = set_ends(jax.random.randint(splits[3], (NPAIR, 2), 0, NB), jax.random.fold_in(splits[3], 1), 0, NB - 1).astype(jnp.int32)
    return dict(hist=hist, tile_mask=tile_mask, planes=planes, pairs=pairs)


def reference(hist, tile_mask, planes, pairs):
    nb = tile_mask.shape[0]
    ab = tile_mask.shape[1]
    shaped = hist.reshape(nb, BLK, ab, BLK)
    masked = (shaped * tile_mask.astype(jnp.bfloat16)[:, None, :, None]).reshape(hist.shape)
    wide = jnp.dot(masked, planes, preferred_element_type=jnp.float32)
    sq = lax.optimization_barrier(jnp.sum(wide * wide, axis=1))
    blocks = wide.reshape(nb, BLK, P_SIZE)
    norms = sq.reshape(nb, BLK)

    def one_pair(pair):
        left = blocks[pair[0]]
        right = blocks[pair[1]]
        dots = jnp.dot(left, right.T, precision=lax.Precision.HIGHEST)
        lscale = lax.rsqrt(norms[pair[0]] / P_SIZE + 1e-06)
        rscale = lax.rsqrt(norms[pair[1]] / P_SIZE + 1e-06)
        return dots / P_SIZE * lscale[:, None] * rscale[None, :]
    return lax.map(one_pair, pairs)
```

```python
import functools

import jax
import jax.numpy as jnp
import numpy as np
from jax import lax
from jax.sharding import Mesh, PartitionSpec as P

P_SIZE = 1024
DEPTH = 4
CORES = 2
CHUNKS = 4
PLANE = ("x", "y", "core")


def ring_order(count):
    return list(range(0, count, 2)) + list(range(1, count, 2))[::-1]


def ring_pairs(count):
    order = ring_order(count)
    return [(order[k], order[(k + 1) % count]) for k in range(count)]


def ring_source(z, step, count):
    order = np.array(ring_order(count))
    place = np.argsort(order)
    table = np.array([[order[(place[d] - s) % count] for s in range(count)] for d in range(count)], np.int32)
    return jnp.asarray(table)[z, step]


def body(hist, tile_mask, planes, pairs):
    rows, acts = hist.shape
    row_blocks, act_blocks = tile_mask.shape
    blk = rows // row_blocks
    own_planes = planes.shape[1]
    wide = lax.axis_size("x")
    deep = lax.axis_size("z")
    x, z = lax.axis_index("x"), lax.axis_index("z")
    span = acts // wide
    step = span // CHUNKS

    def masked_part(owner, chunk):
        start = owner * span + chunk * step
        part = lax.dynamic_slice_in_dim(hist, start, step, 1)
        mask = lax.dynamic_slice_in_dim(tile_mask, start // blk, step // blk, 1).astype(jnp.bfloat16)
        return (part.reshape(row_blocks, blk, step // blk, blk) * mask[:, None, :, None]).reshape(rows, step)

    def planes_part(owner, chunk):
        return lax.dynamic_slice_in_dim(planes, owner * span + chunk * step, step, 0)

    def turn(k):
        return [(d, (d + k) % wide) for d in range(wide)]

    groups = []
    for c in range(CHUNKS):
        parts = [planes_part(x, c)] + [
            lax.ppermute(planes_part((x + k) % wide, c), "x", turn(k)) for k in range(1, wide)
        ]
        whole = jnp.zeros((step, wide * own_planes), planes.dtype)
        for k, part in enumerate(parts):
            whole = lax.dynamic_update_slice_in_dim(whole, part, ((x - k) % wide) * own_planes, 1)
        groups.append(whole)

    hists = [
        [masked_part(x, c)]
        + [lax.ppermute(masked_part((x + k) % wide, c), "x", turn(k)) for k in range(1, wide)]
        for c in range(CHUNKS)
    ]

    order = (x - jnp.arange(wide)) % wide
    shares = []
    for s in range(deep):
        total = []
        for k in range(wide):
            one = 0.0
            for c in range(CHUNKS):
                one = one + jnp.dot(hists[c][k], groups[c], preferred_element_type=jnp.float32)
            total.append(one)
        total = jnp.stack(total)[order].reshape(wide * rows, wide * own_planes)
        shares.append(lax.psum_scatter(total, PLANE, scatter_dimension=1, tiled=True))
        if s < deep - 1:
            groups = [lax.ppermute(g, "z", ring_pairs(deep)) for g in groups]
    shares = jnp.stack(shares)[jnp.argsort(jnp.stack([ring_source(z, s, deep) for s in range(deep)]))]
    proj = jnp.moveaxis(shares, 0, 1).reshape(wide * rows, -1)

    everyone = lax.all_gather(proj, "z", axis=0, tiled=True)
    blocks = everyone.reshape(-1, blk, proj.shape[1])
    all_pairs = lax.all_gather(pairs, "x", axis=0, tiled=True)
    left_ids, right_ids = all_pairs[:, 0], all_pairs[:, 1]
    lefts, rights = blocks[left_ids], blocks[right_ids]
    dots = jnp.einsum("kuc,kvc->kuv", lefts, rights, precision=lax.Precision.HIGHEST)
    sq = jnp.sum(blocks * blocks, axis=2)
    sums = jnp.concatenate([dots, sq[left_ids][:, None], sq[right_ids][:, None]], axis=1)
    own = lax.psum_scatter(sums, PLANE, scatter_dimension=0, tiled=True)
    scale = lax.rsqrt(own[:, blk:] / P_SIZE + 1e-06)
    return own[:, :blk] / P_SIZE * scale[:, 0, :, None] * scale[:, 1, None, :]


def solution(mesh):
    sess, act = mesh.shape["sess"], mesh.shape["act"]
    fine = Mesh(
        mesh.devices.reshape(DEPTH, sess // DEPTH, act // CORES, CORES), ("z", "x", "y", "core")
    )
    sess_axes, act_axes = ("z", "x"), ("y", "core")
    placed = (
        P(sess_axes, act_axes), P(sess_axes, act_axes), P(act_axes, sess_axes), P(sess_axes, None)
    )
    return jax.shard_map(
        body, mesh=fine, in_specs=placed, out_specs=P(sess_axes + act_axes, None, None), check_vma=False
    )
```

```python
import functools

import jax
import jax.numpy as jnp
import numpy as np
from jax import lax
from jax.experimental import pallas as pl
from jax.experimental.pallas import tpu as pltpu
from jax.sharding import Mesh, PartitionSpec as P

P_SIZE = 1024
DEPTH = 4
CORES = 2

NEAR = ((0, 1), (1, 0), (2, 3), (3, 2))
INWARD = ((0, 1), (3, 2))
OUTWARD = ((1, 0), (2, 3))
MIDDLE = ((1, 2), (2, 1))
SOURCE = np.array([[0, 1, 2, 3], [1, 0, 2, 3], [2, 3, 1, 0], [3, 2, 1, 0]], np.int32)
PLACE = np.argsort(SOURCE, axis=1).astype(np.int32)

LENT = (5, 16)


def bounds(total, parts):
    return [total * k // parts for k in range(parts + 1)]


def room(tiles):
    return min(tiles, -(-(tiles // 2 + int(2.6 * tiles**0.5)) // 2) * 2)


def params(**kwargs):
    return pltpu.CompilerParams(**kwargs)


def pack_kernel(blk, row_blocks, columns, slots, info, hist, out, sem):
    base = info[0]

    def one_column(c, used):
        start = pl.multiple_of((base + c) * blk, blk)
        for b in range(row_blocks):
            take = jnp.logical_and(info[1 + c * row_blocks + b] != 0, used < slots)

            @pl.when(take)
            def _():
                pltpu.make_async_copy(
                    hist.at[pl.ds(b * blk, blk), pl.ds(start, blk)], out.at[used], sem
                ).start()

            used = used + take.astype(jnp.int32)
        return used

    used = lax.fori_loop(0, columns, one_column, jnp.int32(0))

    def one_wait(_, carry):
        pltpu.make_async_copy(hist.at[pl.ds(0, blk), pl.ds(0, blk)], out.at[0], sem).wait()
        return carry

    lax.fori_loop(0, used, one_wait, 0)


def pack(hist, mask, base, slots):
    row_blocks, columns = mask.shape
    blk = hist.shape[0] // row_blocks
    info = jnp.concatenate([jnp.reshape(base, (1,)).astype(jnp.int32), mask.T.reshape(-1)])
    return pl.pallas_call(
        functools.partial(pack_kernel, blk, row_blocks, columns, slots),
        out_shape=jax.ShapeDtypeStruct((slots, blk, blk), hist.dtype),
        in_specs=[pl.BlockSpec(memory_space=pltpu.SMEM), pl.BlockSpec(memory_space=pl.ANY)],
        out_specs=pl.BlockSpec(memory_space=pl.ANY),
        scratch_shapes=[pltpu.SemaphoreType.DMA],
        cost_estimate=pl.CostEstimate(flops=0, bytes_accessed=2 * slots * blk * blk * 2, transcendentals=0),
        name="pack_tiles",
    )(info, hist)


def spread_kernel(blk, row_blocks, parts, slots, info, source, *refs):
    outs, (zeros, sem) = refs[: len(parts)], refs[len(parts) :]
    zeros[...] = jnp.zeros_like(zeros)
    base = info[0]
    used = jnp.int32(0)
    first = 0
    for out, columns in zip(outs, parts):

        def one_column(c, used, out=out, first=first):
            start = pl.multiple_of((base + first + c) * blk, blk)
            place = pl.multiple_of(c * blk, blk)
            for b in range(row_blocks):
                there = info[1 + (first + c) * row_blocks + b] != 0
                if slots is not None:
                    there = jnp.logical_and(there, used < slots)
                target = out.at[pl.ds(b * blk, blk), pl.ds(place, blk)]

                @pl.when(there)
                def _():
                    if slots is None:
                        tile = source.at[pl.ds(b * blk, blk), pl.ds(start, blk)]
                    else:
                        tile = source.at[used]
                    pltpu.make_async_copy(tile, target, sem).start()

                @pl.when(jnp.logical_not(there))
                def _():
                    pltpu.make_async_copy(zeros, target, sem).start()

                used = used + there.astype(jnp.int32)
            return used

        used = lax.fori_loop(0, columns, one_column, used)
        first += columns
    for out in outs:
        pltpu.make_async_copy(out, out, sem).wait()


def spread(source, mask, base, parts):
    row_blocks = mask.shape[0]
    packed = base is None
    blk = source.shape[1] if packed else source.shape[0] // row_blocks
    base = 0 if packed else base
    info = jnp.concatenate([jnp.reshape(base, (1,)).astype(jnp.int32), mask.T.reshape(-1)])
    shapes = [jax.ShapeDtypeStruct((row_blocks * blk, columns * blk), source.dtype) for columns in parts]
    return pl.pallas_call(
        functools.partial(spread_kernel, blk, row_blocks, parts, source.shape[0] if packed else None),
        out_shape=shapes,
        in_specs=[pl.BlockSpec(memory_space=pltpu.SMEM), pl.BlockSpec(memory_space=pl.ANY)],
        out_specs=[pl.BlockSpec(memory_space=pl.ANY)] * len(parts),
        scratch_shapes=[pltpu.VMEM((blk, blk), source.dtype), pltpu.SemaphoreType.DMA],
        cost_estimate=pl.CostEstimate(
            flops=0, bytes_accessed=4 * sum(parts) * row_blocks * blk * blk, transcendentals=0
        ),
        name="spread_tiles",
    )(info, source)


def dots_kernel(blk, count, ids, blocks, out):
    rest = jnp.zeros((out.shape[1] - blk - 2, blk), jnp.float32)

    def one(k, carry):
        def side(which):
            start = pl.multiple_of(ids[which, 1, k] * blk, blk)
            return blocks[ids[which, 0, k], :, pl.ds(start, blk)]

        left, right = side(0), side(1)
        out[k, :blk, :] = lax.dot_general(
            left, right, (((0,), (0,)), ((), ())),
            precision=lax.Precision.HIGHEST, preferred_element_type=jnp.float32,
        )
        out[k, blk:, :] = jnp.concatenate(
            [jnp.sum(left * left, axis=0, keepdims=True), jnp.sum(right * right, axis=0, keepdims=True), rest]
        )
        return carry

    lax.fori_loop(0, count, one, 0)


def pair_dots(blocks, ids, blk):
    count = ids.shape[2]
    return pl.pallas_call(
        functools.partial(dots_kernel, blk, count),
        out_shape=jax.ShapeDtypeStruct((count, blk + 8, blk), jnp.float32),
        in_specs=[pl.BlockSpec(memory_space=pltpu.SMEM), pl.BlockSpec(memory_space=pltpu.VMEM)],
        out_specs=pl.BlockSpec(memory_space=pltpu.VMEM),
        compiler_params=params(vmem_limit_bytes=48 << 20),
        name="pair_dots",
    )(ids, blocks)


def turn(count, k):
    return [(d, (d + k) % count) for d in range(count)]


def scatter_sum(values, axis, dim):
    count = lax.axis_size(axis)
    here = lax.axis_index(axis)
    piece = values.shape[dim] // count

    def part(owner):
        return lax.dynamic_slice_in_dim(values, owner * piece, piece, dim)

    total = part(here)
    for k in range(1, count):
        total = total + lax.ppermute(part((here + k) % count), axis, turn(count, k))
    return total


class Lane:
    def __init__(self, depth):
        self.depth = depth
        self.arrived = []

    def send(self, values, axis, pairs):
        if len(self.arrived) >= self.depth:
            values, _ = lax.optimization_barrier((values, self.arrived[-self.depth]))
        got = lax.ppermute(values, axis, pairs)
        self.arrived.append(got)
        return got


def along_line(block, inner):
    near = lax.ppermute(block, "z", NEAR)
    middle = lax.ppermute(block, "z", MIDDLE)
    far = lax.ppermute(near, "z", MIDDLE)
    out1 = lax.ppermute(middle, "z", OUTWARD)
    out2 = lax.ppermute(far, "z", OUTWARD)
    return [block, near, jnp.where(inner, middle, out1), jnp.where(inner, far, out2)]


def dense(hist, tile_mask, planes, pairs):
    sess, act = ("z", "x"), ("y", "core")
    rows, acts = hist.shape
    row_blocks, act_blocks = tile_mask.shape
    blk = rows // row_blocks
    masked = (
        hist.reshape(row_blocks, blk, act_blocks, blk)
        * (tile_mask != 0).astype(jnp.bfloat16)[:, None, :, None]
    ).reshape(rows, acts)
    partial_proj = jnp.dot(
        masked, lax.all_gather(planes, sess, axis=1, tiled=True), preferred_element_type=jnp.float32
    )
    proj = lax.psum_scatter(partial_proj, act, scatter_dimension=1, tiled=True)
    own_count = pairs.shape[0] // lax.axis_size(act)
    place = lax.axis_index(act) * own_count
    sq = lax.psum(jnp.sum(proj * proj, axis=1), act)
    blocks = lax.all_gather(proj, sess, axis=0, tiled=True).reshape(-1, blk, proj.shape[1])
    norms = lax.all_gather(sq, sess, axis=0, tiled=True).reshape(-1, blk)
    dots = jnp.einsum(
        "kuc,kvc->kuv", blocks[pairs[:, 0]], blocks[pairs[:, 1]], precision=lax.Precision.HIGHEST
    )
    dots = lax.psum_scatter(dots, act, scatter_dimension=0, tiled=True)
    own = lax.dynamic_slice_in_dim(pairs, place, own_count, 0)
    scale = lax.rsqrt(norms[own] / P_SIZE + 1e-06)
    return dots / P_SIZE * scale[:, 0, :, None] * scale[:, 1, None, :]


def body(hist, tile_mask, planes, pairs):
    rows, acts = hist.shape
    row_blocks, act_blocks = tile_mask.shape
    blk = rows // row_blocks
    own_planes = planes.shape[1]
    wide = lax.axis_size("x")
    x, z = lax.axis_index("x"), lax.axis_index("z")
    inner = jnp.logical_or(z == 1, z == 2)
    columns = act_blocks // wide
    tile_mask = (tile_mask != 0).astype(jnp.int32)

    lent = columns * LENT[0] // LENT[1]
    kept = columns - lent
    cuts = bounds(kept, 4) + [kept + c for c in bounds(lent, 2)[1:]]
    widths = [b - a for a, b in zip(cuts[:-1], cuts[1:])]
    streams = {"lent": (4, 6), "early": (0, 2), "late": (2, 4)}

    def mask_of(owner):
        return lax.dynamic_slice_in_dim(tile_mask, owner * columns, columns, 1)

    def over_x(make):
        return [lax.ppermute(make((x + k) % wide), "x", turn(wide, k)) for k in range(1, wide)]

    masks = [mask_of(x)] + [lax.ppermute(mask_of((x + k) % wide), "x", turn(wide, k)) for k in range(1, wide)]
    guest_masks = lax.ppermute(jnp.stack([m[:, kept:] for m in masks]), "z", INWARD)

    over_x, ends, middle, ends_out = Lane(2), Lane(1), Lane(2), Lane(2)

    def planes_of(owner, c):
        return lax.dynamic_slice_in_dim(planes, (owner * columns + cuts[c]) * blk, widths[c] * blk, 0)

    def group(c):
        whole = jnp.zeros((widths[c] * blk, wide * own_planes), planes.dtype)
        whole = lax.dynamic_update_slice_in_dim(whole, planes_of(x, c), x * own_planes, 1)
        for k in range(1, wide):
            part = over_x.send(planes_of((x + k) % wide, c), "x", turn(wide, k))
            whole = lax.dynamic_update_slice_in_dim(whole, part, ((x - k) % wide) * own_planes, 1)
        return whole

    def tiles_of(name):
        low, high = (cuts[c] for c in streams[name])
        slots = room((high - low) * row_blocks)
        got = []
        for k in range(1, wide):
            owner = (x + k) % wide
            tiles = pack(hist, mask_of(owner)[:, low:high], owner * columns + low, slots)
            got.append(over_x.send(tiles, "x", turn(wide, k)))
        return got

    groups = [group(c) for c in range(4)]
    tiles = {"lent": tiles_of("lent")}
    groups += [group(c) for c in (4, 5)]
    tiles["early"] = tiles_of("early")
    tiles["late"] = tiles_of("late")

    over = jnp.int32(0)
    sessions = [[None] * 6 for _ in range(wide)]
    for name, (first, last) in streams.items():
        low, high = cuts[first], cuts[last]
        for owner in range(wide):
            count = jnp.sum(tile_mask[:, owner * columns + low : owner * columns + high])
            over = jnp.maximum(over, (count > room((high - low) * row_blocks)).astype(jnp.int32))
        parts = tuple(widths[first:last])
        for k in range(wide):
            mask = masks[k][:, low:high]
            if k == 0:
                sessions[k][first:last] = spread(hist, mask, x * columns + low, parts)
            else:
                sessions[k][first:last] = spread(tiles[name][k - 1], mask, None, parts)

    near, mid, far = {}, {}, {}
    for c in range(4):
        near[c] = ends.send(groups[c], "z", NEAR)
    own_tiles = pack(hist, masks[0][:, kept:], x * columns + kept, room(lent * row_blocks))
    lent_tiles = [ends.send(own_tiles, "z", INWARD)]
    for c in (4, 5):
        near[c] = ends.send(groups[c], "z", INWARD)
    for c in range(6):
        mid[c] = middle.send(groups[c], "z", MIDDLE)
    for c in range(6):
        far[c] = middle.send(near[c], "z", MIDDLE)
    held = [None] * 6
    out1 = [ends_out.send(mid[c], "z", OUTWARD) for c in range(4)]
    lent_tiles += [ends.send(t, "z", INWARD) for t in tiles["lent"]]
    out2 = [ends_out.send(far[c], "z", OUTWARD) for c in range(4)]
    for c in range(6):
        if c < 4:
            held[c] = [groups[c], near[c], jnp.where(inner, mid[c], out1[c]), jnp.where(inner, far[c], out2[c])]
        else:
            held[c] = [groups[c], near[c], mid[c], far[c]]
    guests = [
        spread(t, guest_masks[k], None, tuple(widths[4:])) for k, t in enumerate(lent_tiles)
    ]

    order = (x - jnp.arange(wide)) % wide

    def summed(terms):
        totals = []
        for source in terms:
            total = None
            for a, b in source:
                one = jnp.dot(a, b, preferred_element_type=jnp.float32)
                total = one if total is None else total + one
            totals.append(total)
        whole = jnp.stack(totals)[order].reshape(wide * rows, wide * own_planes).T
        for axis in ("core", "x", "y"):
            whole = scatter_sum(whole, axis, 0)
        return whole

    shares = []
    for s in range(DEPTH):
        share = summed([[(sessions[k][c], held[c][s]) for c in range(6)] for k in range(wide)])
        if s > 0:
            t = 0 if s == 1 else s
            guest = summed([[(guests[k][c - 4], held[c][t]) for c in (4, 5)] for k in range(wide)])
            share = share + lax.ppermute(guest, "z", OUTWARD)
        shares.append(share)
    proj = jnp.stack(shares)[jnp.asarray(PLACE)[z]].reshape(-1, wide * rows)

    blocks = jnp.stack(along_line(proj, inner))
    got = [pairs] + [lax.ppermute(pairs, "x", turn(wide, k)) for k in range(1, wide)]
    all_pairs = jnp.stack(got)[order].reshape(-1, 2).T
    plane_blocks = wide * row_blocks
    ids = jnp.stack([jnp.asarray(PLACE)[z][all_pairs // plane_blocks], all_pairs % plane_blocks], axis=1)
    sums = pair_dots(blocks, ids, blk)
    high, cores = lax.axis_size("y"), lax.axis_size("core")
    sums = sums.reshape((wide, high, cores, -1) + sums.shape[1:])
    for axis, dim in (("core", 2), ("x", 0), ("y", 1)):
        sums = scatter_sum(sums, axis, dim)
    own = sums.reshape((-1,) + sums.shape[4:])
    scale = lax.rsqrt(own[:, blk : blk + 2] / P_SIZE + 1e-06)
    scores = own[:, :blk] / P_SIZE * scale[:, 0, :, None] * scale[:, 1, None, :]

    over = lax.pmax(over, ("z", "x", "y", "core"))
    return lax.cond(over > 0, lambda: dense(hist, tile_mask, planes, pairs), lambda: scores)


def solution(mesh):
    sess, act = mesh.shape["sess"], mesh.shape["act"]
    fine = Mesh(
        mesh.devices.reshape(DEPTH, sess // DEPTH, act // CORES, CORES), ("z", "x", "y", "core")
    )
    sess_axes, act_axes = ("z", "x"), ("y", "core")
    placed = (
        P(sess_axes, act_axes), P(sess_axes, act_axes), P(act_axes, sess_axes), P(sess_axes, None)
    )
    return jax.shard_map(
        body, mesh=fine, in_specs=placed, out_specs=P(sess_axes + act_axes, None, None), check_vma=False
    )
```

```python
import functools

import jax
import jax.numpy as jnp
import numpy as np
from jax import lax
from jax.experimental import pallas as pl
from jax.experimental.pallas import tpu as pltpu
from jax.sharding import Mesh, PartitionSpec as P

P_SIZE = 1024
DEPTH = 4
CORES = 2

NEAR = ((0, 1), (1, 0), (2, 3), (3, 2))
INWARD = ((0, 1), (3, 2))
OUTWARD = ((1, 0), (2, 3))
MIDDLE = ((1, 2), (2, 1))
SOURCE = np.array([[0, 1, 2, 3], [1, 0, 2, 3], [2, 3, 1, 0], [3, 2, 1, 0]], np.int32)
PLACE = np.argsort(SOURCE, axis=1).astype(np.int32)

LENT = (5, 16)


def bounds(total, parts):
    return [total * k // parts for k in range(parts + 1)]


def room(tiles):
    return min(tiles, -(-(tiles // 2 + int(2.6 * tiles**0.5)) // 2) * 2)


def params(**kwargs):
    return pltpu.CompilerParams(**kwargs)


def pack_kernel(blk, row_blocks, columns, slots, info, hist, out, sem):
    base = info[0]

    def one_column(c, used):
        start = pl.multiple_of((base + c) * blk, blk)
        for b in range(row_blocks):
            take = jnp.logical_and(info[1 + c * row_blocks + b] != 0, used < slots)

            @pl.when(take)
            def _():
                pltpu.make_async_copy(
                    hist.at[pl.ds(b * blk, blk), pl.ds(start, blk)], out.at[used], sem
                ).start()

            used = used + take.astype(jnp.int32)
        return used

    used = lax.fori_loop(0, columns, one_column, jnp.int32(0))

    def one_wait(_, carry):
        pltpu.make_async_copy(hist.at[pl.ds(0, blk), pl.ds(0, blk)], out.at[0], sem).wait()
        return carry

    lax.fori_loop(0, used, one_wait, 0)


def pack(hist, mask, base, slots):
    row_blocks, columns = mask.shape
    blk = hist.shape[0] // row_blocks
    info = jnp.concatenate([jnp.reshape(base, (1,)).astype(jnp.int32), mask.T.reshape(-1)])
    return pl.pallas_call(
        functools.partial(pack_kernel, blk, row_blocks, columns, slots),
        out_shape=jax.ShapeDtypeStruct((slots, blk, blk), hist.dtype),
        in_specs=[pl.BlockSpec(memory_space=pltpu.SMEM), pl.BlockSpec(memory_space=pl.ANY)],
        out_specs=pl.BlockSpec(memory_space=pltpu.VMEM),
        scratch_shapes=[pltpu.SemaphoreType.DMA],
        compiler_params=params(vmem_limit_bytes=32 << 20),
        cost_estimate=pl.CostEstimate(flops=0, bytes_accessed=2 * slots * blk * blk * 2, transcendentals=0),
        name="pack_tiles",
    )(info, hist)


def spread_kernel(blk, row_blocks, parts, slots, info, source, *refs):
    outs, sem = refs[: len(parts)], refs[len(parts)]
    base = info[0]
    used = jnp.int32(0)
    first = 0
    for out, columns in zip(outs, parts):

        def one_column(c, used, out=out, first=first):
            start = pl.multiple_of((base + first + c) * blk, blk)
            place = pl.multiple_of(c * blk, blk)
            for b in range(row_blocks):
                there = info[1 + (first + c) * row_blocks + b] != 0
                if slots is not None:
                    there = jnp.logical_and(there, used < slots)
                rows = pl.ds(b * blk, blk)

                @pl.when(there)
                def _():
                    tile = source.at[rows, pl.ds(start, blk)] if slots is None else source.at[used]
                    pltpu.make_async_copy(tile, out.at[rows, pl.ds(place, blk)], sem).start()

                @pl.when(jnp.logical_not(there))
                def _():
                    out[rows, pl.ds(place, blk)] = jnp.zeros((blk, blk), out.dtype)

                used = used + there.astype(jnp.int32)
            return used

        used = lax.fori_loop(0, columns, one_column, used)
        first += columns

    def one_wait(_, carry):
        tile = source.at[pl.ds(0, blk), pl.ds(0, blk)] if slots is None else source.at[0]
        pltpu.make_async_copy(tile, outs[0].at[pl.ds(0, blk), pl.ds(0, blk)], sem).wait()
        return carry

    lax.fori_loop(0, used, one_wait, 0)


def spread(source, mask, base, parts):
    row_blocks = mask.shape[0]
    packed = base is None
    blk = source.shape[1] if packed else source.shape[0] // row_blocks
    base = 0 if packed else base
    info = jnp.concatenate([jnp.reshape(base, (1,)).astype(jnp.int32), mask.T.reshape(-1)])
    shapes = [jax.ShapeDtypeStruct((row_blocks * blk, columns * blk), source.dtype) for columns in parts]
    return pl.pallas_call(
        functools.partial(spread_kernel, blk, row_blocks, parts, source.shape[0] if packed else None),
        out_shape=shapes,
        in_specs=[pl.BlockSpec(memory_space=pltpu.SMEM), pl.BlockSpec(memory_space=pl.ANY)],
        out_specs=[pl.BlockSpec(memory_space=pltpu.VMEM)] * len(parts),
        scratch_shapes=[pltpu.SemaphoreType.DMA],
        compiler_params=params(vmem_limit_bytes=32 << 20),
        cost_estimate=pl.CostEstimate(
            flops=0, bytes_accessed=4 * sum(parts) * row_blocks * blk * blk, transcendentals=0
        ),
        name="spread_tiles",
    )(info, source)


def dots_kernel(blk, count, ids, blocks, out):
    rest = jnp.zeros((out.shape[1] - blk - 2, blk), jnp.float32)

    def one(k, carry):
        def side(which):
            start = pl.multiple_of(ids[which, 1, k] * blk, blk)
            return blocks[ids[which, 0, k], :, pl.ds(start, blk)]

        left, right = side(0), side(1)
        out[k, :blk, :] = lax.dot_general(
            left, right, (((0,), (0,)), ((), ())),
            precision=lax.Precision.HIGHEST, preferred_element_type=jnp.float32,
        )
        out[k, blk:, :] = jnp.concatenate(
            [jnp.sum(left * left, axis=0, keepdims=True), jnp.sum(right * right, axis=0, keepdims=True), rest]
        )
        return carry

    lax.fori_loop(0, count, one, 0)


def pair_dots(blocks, ids, blk):
    count = ids.shape[2]
    return pl.pallas_call(
        functools.partial(dots_kernel, blk, count),
        out_shape=jax.ShapeDtypeStruct((count, blk + 8, blk), jnp.float32),
        in_specs=[pl.BlockSpec(memory_space=pltpu.SMEM), pl.BlockSpec(memory_space=pltpu.VMEM)],
        out_specs=pl.BlockSpec(memory_space=pltpu.VMEM),
        compiler_params=params(vmem_limit_bytes=48 << 20),
        name="pair_dots",
    )(ids, blocks)


def turn(count, k):
    return [(d, (d + k) % count) for d in range(count)]


def scatter_sum(values, axis, dim):
    count = lax.axis_size(axis)
    here = lax.axis_index(axis)
    piece = values.shape[dim] // count

    def part(owner):
        return lax.dynamic_slice_in_dim(values, owner * piece, piece, dim)

    total = part(here)
    for k in range(1, count):
        total = total + lax.ppermute(part((here + k) % count), axis, turn(count, k))
    return total


class Lane:
    def __init__(self, depth):
        self.depth = depth
        self.arrived = []

    def send(self, values, axis, pairs):
        if len(self.arrived) >= self.depth:
            values, _ = lax.optimization_barrier((values, self.arrived[-self.depth]))
        got = lax.ppermute(values, axis, pairs)
        self.arrived.append(got)
        return got


def along_line(block, inner):
    near = lax.ppermute(block, "z", NEAR)
    middle = lax.ppermute(block, "z", MIDDLE)
    far = lax.ppermute(near, "z", MIDDLE)
    out1 = lax.ppermute(middle, "z", OUTWARD)
    out2 = lax.ppermute(far, "z", OUTWARD)
    return [block, near, jnp.where(inner, middle, out1), jnp.where(inner, far, out2)]


def dense(hist, tile_mask, planes, pairs):
    sess, act = ("z", "x"), ("y", "core")
    rows, acts = hist.shape
    row_blocks, act_blocks = tile_mask.shape
    blk = rows // row_blocks
    masked = (
        hist.reshape(row_blocks, blk, act_blocks, blk)
        * (tile_mask != 0).astype(jnp.bfloat16)[:, None, :, None]
    ).reshape(rows, acts)
    partial_proj = jnp.dot(
        masked, lax.all_gather(planes, sess, axis=1, tiled=True), preferred_element_type=jnp.float32
    )
    proj = lax.psum_scatter(partial_proj, act, scatter_dimension=1, tiled=True)
    own_count = pairs.shape[0] // lax.axis_size(act)
    place = lax.axis_index(act) * own_count
    sq = lax.psum(jnp.sum(proj * proj, axis=1), act)
    blocks = lax.all_gather(proj, sess, axis=0, tiled=True).reshape(-1, blk, proj.shape[1])
    norms = lax.all_gather(sq, sess, axis=0, tiled=True).reshape(-1, blk)
    dots = jnp.einsum(
        "kuc,kvc->kuv", blocks[pairs[:, 0]], blocks[pairs[:, 1]], precision=lax.Precision.HIGHEST
    )
    dots = lax.psum_scatter(dots, act, scatter_dimension=0, tiled=True)
    own = lax.dynamic_slice_in_dim(pairs, place, own_count, 0)
    scale = lax.rsqrt(norms[own] / P_SIZE + 1e-06)
    return dots / P_SIZE * scale[:, 0, :, None] * scale[:, 1, None, :]


def body(hist, tile_mask, planes, pairs):
    rows, acts = hist.shape
    row_blocks, act_blocks = tile_mask.shape
    blk = rows // row_blocks
    own_planes = planes.shape[1]
    wide = lax.axis_size("x")
    x, z = lax.axis_index("x"), lax.axis_index("z")
    inner = jnp.logical_or(z == 1, z == 2)
    columns = act_blocks // wide
    tile_mask = (tile_mask != 0).astype(jnp.int32)

    lent = columns * LENT[0] // LENT[1]
    kept = columns - lent
    cuts = bounds(kept, 4) + [kept + c for c in bounds(lent, 2)[1:]]
    widths = [b - a for a, b in zip(cuts[:-1], cuts[1:])]
    streams = {"lent": (4, 6), "early": (0, 2), "late": (2, 4)}

    def mask_of(owner):
        return lax.dynamic_slice_in_dim(tile_mask, owner * columns, columns, 1)

    def over_x(make):
        return [lax.ppermute(make((x + k) % wide), "x", turn(wide, k)) for k in range(1, wide)]

    masks = [mask_of(x)] + [lax.ppermute(mask_of((x + k) % wide), "x", turn(wide, k)) for k in range(1, wide)]
    guest_masks = lax.ppermute(jnp.stack([m[:, kept:] for m in masks]), "z", INWARD)

    over_x, ends, middle, ends_out = Lane(2), Lane(1), Lane(2), Lane(2)

    def planes_of(owner, c):
        return lax.dynamic_slice_in_dim(planes, (owner * columns + cuts[c]) * blk, widths[c] * blk, 0)

    def group(c):
        whole = jnp.zeros((widths[c] * blk, wide * own_planes), planes.dtype)
        whole = lax.dynamic_update_slice_in_dim(whole, planes_of(x, c), x * own_planes, 1)
        for k in range(1, wide):
            part = over_x.send(planes_of((x + k) % wide, c), "x", turn(wide, k))
            whole = lax.dynamic_update_slice_in_dim(whole, part, ((x - k) % wide) * own_planes, 1)
        return whole

    def tiles_of(name):
        low, high = (cuts[c] for c in streams[name])
        slots = room((high - low) * row_blocks)
        got = []
        for k in range(1, wide):
            owner = (x + k) % wide
            tiles = pack(hist, mask_of(owner)[:, low:high], owner * columns + low, slots)
            got.append(over_x.send(tiles, "x", turn(wide, k)))
        return got

    groups = [group(c) for c in range(6)]
    tiles = {name: tiles_of(name) for name in ("early", "lent", "late")}

    over = jnp.int32(0)
    sessions = [[None] * 6 for _ in range(wide)]
    for name, (first, last) in streams.items():
        low, high = cuts[first], cuts[last]
        for owner in range(wide):
            count = jnp.sum(tile_mask[:, owner * columns + low : owner * columns + high])
            over = jnp.maximum(over, (count > room((high - low) * row_blocks)).astype(jnp.int32))
        parts = tuple(widths[first:last])
        for k in range(wide):
            mask = masks[k][:, low:high]
            if k == 0:
                sessions[k][first:last] = spread(hist, mask, x * columns + low, parts)
            else:
                sessions[k][first:last] = spread(tiles[name][k - 1], mask, None, parts)

    near, mid, far = {}, {}, {}
    for c in range(4):
        near[c] = ends.send(groups[c], "z", NEAR)
    own_tiles = pack(hist, masks[0][:, kept:], x * columns + kept, room(lent * row_blocks))
    lent_tiles = [ends.send(own_tiles, "z", INWARD)]
    for c in (4, 5):
        near[c] = ends.send(groups[c], "z", INWARD)
    for c in range(6):
        mid[c] = middle.send(groups[c], "z", MIDDLE)
    for c in range(6):
        far[c] = middle.send(near[c], "z", MIDDLE)
    held = [None] * 6
    out1 = [ends_out.send(mid[c], "z", OUTWARD) for c in range(4)]
    lent_tiles += [ends.send(t, "z", INWARD) for t in tiles["lent"]]
    out2 = [ends_out.send(far[c], "z", OUTWARD) for c in range(4)]
    for c in range(6):
        if c < 4:
            held[c] = [groups[c], near[c], jnp.where(inner, mid[c], out1[c]), jnp.where(inner, far[c], out2[c])]
        else:
            held[c] = [groups[c], near[c], mid[c], far[c]]
    guests = [
        spread(t, guest_masks[k], None, tuple(widths[4:])) for k, t in enumerate(lent_tiles)
    ]

    order = (x - jnp.arange(wide)) % wide

    def summed(terms):
        totals = []
        for source in terms:
            total = None
            for a, b in source:
                one = jnp.dot(a, b, preferred_element_type=jnp.float32)
                total = one if total is None else total + one
            totals.append(total)
        whole = jnp.stack(totals)[order].reshape(wide * rows, wide * own_planes).T
        for axis in ("core", "x", "y"):
            whole = scatter_sum(whole, axis, 0)
        return whole

    shares = []
    for s in range(DEPTH):
        share = summed([[(sessions[k][c], held[c][s]) for c in range(6)] for k in range(wide)])
        if s > 0:
            t = 0 if s == 1 else s
            guest = summed([[(guests[k][c - 4], held[c][t]) for c in (4, 5)] for k in range(wide)])
            share = share + lax.ppermute(guest, "z", OUTWARD)
        shares.append(share)
    proj = jnp.stack(shares)[jnp.asarray(PLACE)[z]].reshape(-1, wide * rows)

    blocks = jnp.stack(along_line(proj, inner))
    got = [pairs] + [lax.ppermute(pairs, "x", turn(wide, k)) for k in range(1, wide)]
    all_pairs = jnp.stack(got)[order].reshape(-1, 2).T
    plane_blocks = wide * row_blocks
    ids = jnp.stack([jnp.asarray(PLACE)[z][all_pairs // plane_blocks], all_pairs % plane_blocks], axis=1)
    sums = pair_dots(blocks, ids, blk)
    high, cores = lax.axis_size("y"), lax.axis_size("core")
    sums = sums.reshape((wide, high, cores, -1) + sums.shape[1:])
    for axis, dim in (("core", 2), ("x", 0), ("y", 1)):
        sums = scatter_sum(sums, axis, dim)
    own = sums.reshape((-1,) + sums.shape[4:])
    scale = lax.rsqrt(own[:, blk : blk + 2] / P_SIZE + 1e-06)
    scores = own[:, :blk] / P_SIZE * scale[:, 0, :, None] * scale[:, 1, None, :]

    over = lax.pmax(over, ("z", "x", "y", "core"))
    return lax.cond(over > 0, lambda: dense(hist, tile_mask, planes, pairs), lambda: scores)


def solution(mesh):
    sess, act = mesh.shape["sess"], mesh.shape["act"]
    fine = Mesh(
        mesh.devices.reshape(DEPTH, sess // DEPTH, act // CORES, CORES), ("z", "x", "y", "core")
    )
    sess_axes, act_axes = ("z", "x"), ("y", "core")
    placed = (
        P(sess_axes, act_axes), P(sess_axes, act_axes), P(act_axes, sess_axes), P(sess_axes, None)
    )
    return jax.shard_map(
        body, mesh=fine, in_specs=placed, out_specs=P(sess_axes + act_axes, None, None), check_vma=False
    )
```

```python
import functools

import jax
import jax.numpy as jnp
import numpy as np
from jax import lax
from jax.experimental import pallas as pl
from jax.experimental.pallas import tpu as pltpu
from jax.sharding import Mesh, PartitionSpec as P

P_SIZE = 1024
DEPTH = 4
CORES = 2

NEAR = ((0, 1), (1, 0), (2, 3), (3, 2))
INWARD = ((0, 1), (3, 2))
OUTWARD = ((1, 0), (2, 3))
MIDDLE = ((1, 2), (2, 1))
SOURCE = np.array([[0, 1, 2, 3], [1, 0, 2, 3], [2, 3, 1, 0], [3, 2, 1, 0]], np.int32)
PLACE = np.argsort(SOURCE, axis=1).astype(np.int32)

LENT = (9, 32)


def bounds(total, parts):
    return [total * k // parts for k in range(parts + 1)]


def room(tiles):
    return min(tiles, -(-(tiles // 2 + int(2.6 * tiles**0.5)) // 2) * 2)


def params(**kwargs):
    return pltpu.CompilerParams(**kwargs)


def pack_kernel(blk, row_blocks, columns, slots, info, hist, out, sem):
    base = info[0]

    def one_column(c, used):
        start = pl.multiple_of((base + c) * blk, blk)
        for b in range(row_blocks):
            take = jnp.logical_and(info[1 + c * row_blocks + b] != 0, used < slots)

            @pl.when(take)
            def _():
                pltpu.make_async_copy(
                    hist.at[pl.ds(b * blk, blk), pl.ds(start, blk)], out.at[used], sem
                ).start()

            used = used + take.astype(jnp.int32)
        return used

    used = lax.fori_loop(0, columns, one_column, jnp.int32(0))

    def one_wait(_, carry):
        pltpu.make_async_copy(hist.at[pl.ds(0, blk), pl.ds(0, blk)], out.at[0], sem).wait()
        return carry

    lax.fori_loop(0, used, one_wait, 0)


def pack(hist, mask, base, slots):
    row_blocks, columns = mask.shape
    blk = hist.shape[0] // row_blocks
    info = jnp.concatenate([jnp.reshape(base, (1,)).astype(jnp.int32), mask.T.reshape(-1)])
    return pl.pallas_call(
        functools.partial(pack_kernel, blk, row_blocks, columns, slots),
        out_shape=jax.ShapeDtypeStruct((slots, blk, blk), hist.dtype),
        in_specs=[pl.BlockSpec(memory_space=pltpu.SMEM), pl.BlockSpec(memory_space=pl.ANY)],
        out_specs=pl.BlockSpec(memory_space=pltpu.VMEM),
        scratch_shapes=[pltpu.SemaphoreType.DMA],
        compiler_params=params(vmem_limit_bytes=32 << 20),
        cost_estimate=pl.CostEstimate(flops=0, bytes_accessed=2 * slots * blk * blk * 2, transcendentals=0),
        name="pack_tiles",
    )(info, hist)


def spread_kernel(blk, row_blocks, parts, slots, info, source, *refs):
    outs, sem = refs[: len(parts)], refs[len(parts)]
    base = info[0]
    used = jnp.int32(0)
    first = 0
    for out, columns in zip(outs, parts):

        def one_column(c, used, out=out, first=first):
            start = pl.multiple_of((base + first + c) * blk, blk)
            place = pl.multiple_of(c * blk, blk)
            for b in range(row_blocks):
                there = info[1 + (first + c) * row_blocks + b] != 0
                if slots is not None:
                    there = jnp.logical_and(there, used < slots)
                rows = pl.ds(b * blk, blk)

                @pl.when(there)
                def _():
                    tile = source.at[rows, pl.ds(start, blk)] if slots is None else source.at[used]
                    pltpu.make_async_copy(tile, out.at[rows, pl.ds(place, blk)], sem).start()

                @pl.when(jnp.logical_not(there))
                def _():
                    out[rows, pl.ds(place, blk)] = jnp.zeros((blk, blk), out.dtype)

                used = used + there.astype(jnp.int32)
            return used

        used = lax.fori_loop(0, columns, one_column, used)
        first += columns

    def one_wait(_, carry):
        tile = source.at[pl.ds(0, blk), pl.ds(0, blk)] if slots is None else source.at[0]
        pltpu.make_async_copy(tile, outs[0].at[pl.ds(0, blk), pl.ds(0, blk)], sem).wait()
        return carry

    lax.fori_loop(0, used, one_wait, 0)


def spread(source, mask, base, parts):
    row_blocks = mask.shape[0]
    packed = base is None
    blk = source.shape[1] if packed else source.shape[0] // row_blocks
    base = 0 if packed else base
    info = jnp.concatenate([jnp.reshape(base, (1,)).astype(jnp.int32), mask.T.reshape(-1)])
    shapes = [jax.ShapeDtypeStruct((row_blocks * blk, columns * blk), source.dtype) for columns in parts]
    return pl.pallas_call(
        functools.partial(spread_kernel, blk, row_blocks, parts, source.shape[0] if packed else None),
        out_shape=shapes,
        in_specs=[pl.BlockSpec(memory_space=pltpu.SMEM), pl.BlockSpec(memory_space=pl.ANY)],
        out_specs=[pl.BlockSpec(memory_space=pltpu.VMEM)] * len(parts),
        scratch_shapes=[pltpu.SemaphoreType.DMA],
        compiler_params=params(vmem_limit_bytes=32 << 20),
        cost_estimate=pl.CostEstimate(
            flops=0, bytes_accessed=4 * sum(parts) * row_blocks * blk * blk, transcendentals=0
        ),
        name="spread_tiles",
    )(info, source)


def dots_kernel(blk, count, depth, ids, blocks, out):
    flag = jnp.sum(blocks[:, depth : depth + 1, :blk], axis=0)
    rest = jnp.zeros((out.shape[1] - blk - 3, blk), jnp.float32)

    def one(k, carry):
        def side(which):
            start = pl.multiple_of(ids[which, 1, k] * blk, blk)
            return blocks[ids[which, 0, k], :depth, pl.ds(start, blk)]

        left, right = side(0), side(1)
        out[k, :blk, :] = lax.dot_general(
            left, right, (((0,), (0,)), ((), ())),
            precision=lax.Precision.HIGHEST, preferred_element_type=jnp.float32,
        )
        squares = [jnp.sum(v * v, axis=0, keepdims=True) for v in (left, right)]
        out[k, blk:, :] = jnp.concatenate(squares + [flag, rest])
        return carry

    lax.fori_loop(0, count, one, 0)


def pair_dots(blocks, ids, blk):
    count = ids.shape[2]
    return pl.pallas_call(
        functools.partial(dots_kernel, blk, count, blocks.shape[1] - 8),
        out_shape=jax.ShapeDtypeStruct((count, blk + 8, blk), jnp.float32),
        in_specs=[pl.BlockSpec(memory_space=pltpu.SMEM), pl.BlockSpec(memory_space=pltpu.VMEM)],
        out_specs=pl.BlockSpec(memory_space=pltpu.VMEM),
        compiler_params=params(vmem_limit_bytes=48 << 20),
        name="pair_dots",
    )(ids, blocks)


def turn(count, k):
    return [(d, (d + k) % count) for d in range(count)]


def scatter_sum(values, axis, dim):
    count = lax.axis_size(axis)
    here = lax.axis_index(axis)
    piece = values.shape[dim] // count

    def part(owner):
        return lax.dynamic_slice_in_dim(values, owner * piece, piece, dim)

    total = part(here)
    for k in range(1, count):
        total = total + lax.ppermute(part((here + k) % count), axis, turn(count, k))
    return total


def after(values, arrived):
    return lax.optimization_barrier((values, arrived))[0]


class Lane:
    def __init__(self, depth):
        self.depth = depth
        self.arrived = []

    def send(self, values, axis, pairs, later=None):
        if len(self.arrived) >= self.depth:
            values = after(values, self.arrived[-self.depth])
        if later is not None:
            values = after(values, later)
        got = lax.ppermute(values, axis, pairs)
        self.arrived.append(got)
        return got


def along_line(block, inner):
    near = lax.ppermute(block, "z", NEAR)
    middle = lax.ppermute(block, "z", MIDDLE)
    far = lax.ppermute(near, "z", MIDDLE)
    out1 = lax.ppermute(middle, "z", OUTWARD)
    out2 = lax.ppermute(far, "z", OUTWARD)
    return [block, near, jnp.where(inner, middle, out1), jnp.where(inner, far, out2)]


def dense(hist, tile_mask, planes, pairs):
    sess, act = ("z", "x"), ("y", "core")
    rows, acts = hist.shape
    row_blocks, act_blocks = tile_mask.shape
    blk = rows // row_blocks
    masked = (
        hist.reshape(row_blocks, blk, act_blocks, blk)
        * (tile_mask != 0).astype(jnp.bfloat16)[:, None, :, None]
    ).reshape(rows, acts)
    partial_proj = jnp.dot(
        masked, lax.all_gather(planes, sess, axis=1, tiled=True), preferred_element_type=jnp.float32
    )
    proj = lax.psum_scatter(partial_proj, act, scatter_dimension=1, tiled=True)
    own_count = pairs.shape[0] // lax.axis_size(act)
    place = lax.axis_index(act) * own_count
    sq = lax.psum(jnp.sum(proj * proj, axis=1), act)
    blocks = lax.all_gather(proj, sess, axis=0, tiled=True).reshape(-1, blk, proj.shape[1])
    norms = lax.all_gather(sq, sess, axis=0, tiled=True).reshape(-1, blk)
    dots = jnp.einsum(
        "kuc,kvc->kuv", blocks[pairs[:, 0]], blocks[pairs[:, 1]], precision=lax.Precision.HIGHEST
    )
    dots = lax.psum_scatter(dots, act, scatter_dimension=0, tiled=True)
    own = lax.dynamic_slice_in_dim(pairs, place, own_count, 0)
    scale = lax.rsqrt(norms[own] / P_SIZE + 1e-06)
    return dots / P_SIZE * scale[:, 0, :, None] * scale[:, 1, None, :]


def body(hist, tile_mask, planes, pairs):
    rows, acts = hist.shape
    row_blocks, act_blocks = tile_mask.shape
    blk = rows // row_blocks
    own_planes = planes.shape[1]
    wide = lax.axis_size("x")
    x, z = lax.axis_index("x"), lax.axis_index("z")
    inner = jnp.logical_or(z == 1, z == 2)
    columns = act_blocks // wide
    tile_mask = (tile_mask != 0).astype(jnp.int32)

    lent = columns * LENT[0] // LENT[1]
    kept = columns - lent
    cuts = bounds(kept, 4) + [kept + c for c in bounds(lent, 2)[1:]]
    widths = [b - a for a, b in zip(cuts[:-1], cuts[1:])]
    streams = {"lent": (4, 6), "early": (0, 2), "late": (2, 4)}

    def mask_of(owner):
        return lax.dynamic_slice_in_dim(tile_mask, owner * columns, columns, 1)

    def over_x(make):
        return [lax.ppermute(make((x + k) % wide), "x", turn(wide, k)) for k in range(1, wide)]

    masks = [mask_of(x)] + [lax.ppermute(mask_of((x + k) % wide), "x", turn(wide, k)) for k in range(1, wide)]
    guest_masks = lax.ppermute(jnp.stack([m[:, kept:] for m in masks]), "z", INWARD)

    over_x, inward, outward, middle = Lane(1), Lane(2), Lane(1), Lane(2)

    def planes_of(owner, c):
        return lax.dynamic_slice_in_dim(planes, (owner * columns + cuts[c]) * blk, widths[c] * blk, 0)

    def planes_over_x(first, last):
        def part(owner):
            start = (owner * columns + cuts[first]) * blk
            return lax.dynamic_slice_in_dim(planes, start, (cuts[last] - cuts[first]) * blk, 0)

        got = [over_x.send(part((x + k) % wide), "x", turn(wide, k)) for k in range(1, wide)]
        groups = []
        for c in range(first, last):
            whole = jnp.zeros((widths[c] * blk, wide * own_planes), planes.dtype)
            whole = lax.dynamic_update_slice_in_dim(whole, planes_of(x, c), x * own_planes, 1)
            for k in range(1, wide):
                rows_of = slice((cuts[c] - cuts[first]) * blk, (cuts[c + 1] - cuts[first]) * blk)
                whole = lax.dynamic_update_slice_in_dim(
                    whole, got[k - 1][rows_of], ((x - k) % wide) * own_planes, 1
                )
            groups.append(whole)
        return groups

    def tiles_of(name, later):
        low, high = (cuts[c] for c in streams[name])
        slots = room((high - low) * row_blocks)
        got = []
        for k in range(1, wide):
            owner = (x + k) % wide
            mask = after(mask_of(owner)[:, low:high], later)
            tiles = pack(hist, mask, owner * columns + low, slots)
            got.append(over_x.send(tiles, "x", turn(wide, k)))
        return got

    groups = planes_over_x(0, 1)
    groups += planes_over_x(1, 2)
    groups += planes_over_x(2, 4)
    tiles = {"early": tiles_of("early", groups[0])}
    groups += planes_over_x(4, 6)
    tiles["lent"] = tiles_of("lent", groups[1])
    tiles["late"] = tiles_of("late", groups[2])

    near, mid, far = {}, {}, {}
    for c in range(4):
        near[c] = inward.send(groups[c], "z", NEAR)
        mid[c] = middle.send(groups[c], "z", MIDDLE)
    inward.depth = 1
    outward.arrived = [near[3]]
    own_tiles = pack(hist, after(masks[0], groups[3])[:, kept:], x * columns + kept, room(lent * row_blocks))
    lent_tiles = [inward.send(own_tiles, "z", INWARD)]
    for c in range(4):
        far[c] = middle.send(near[c], "z", MIDDLE)
    for c in (4, 5):
        near[c] = inward.send(groups[c], "z", INWARD)
    for c in (4, 5):
        mid[c] = middle.send(groups[c], "z", MIDDLE)
    for c in (4, 5):
        far[c] = middle.send(near[c], "z", MIDDLE)
    out1 = [outward.send(mid[c], "z", OUTWARD) for c in range(4)]
    out2 = [outward.send(far[c], "z", OUTWARD) for c in range(4)]
    lent_tiles += [inward.send(t, "z", INWARD) for t in tiles["lent"]]
    held = []
    for c in range(6):
        if c < 4:
            held.append([groups[c], near[c], jnp.where(inner, mid[c], out1[c]), jnp.where(inner, far[c], out2[c])])
        else:
            held.append([groups[c], near[c], mid[c], far[c]])

    over = jnp.int32(0)
    sessions = [[None] * 6 for _ in range(wide)]
    for name, (first, last) in streams.items():
        low, high = cuts[first], cuts[last]
        for owner in range(wide):
            count = jnp.sum(tile_mask[:, owner * columns + low : owner * columns + high])
            over = jnp.maximum(over, (count > room((high - low) * row_blocks)).astype(jnp.int32))
        parts = tuple(widths[first:last])
        for k in range(wide):
            mask = masks[k][:, low:high]
            if k == 0:
                later = groups[3] if name == "early" else near[0] if name == "lent" else near[1]
                sessions[k][first:last] = spread(hist, after(mask, later), x * columns + low, parts)
            else:
                sessions[k][first:last] = spread(tiles[name][k - 1], mask, None, parts)
    guests = [
        spread(t, guest_masks[k], None, tuple(widths[4:])) for k, t in enumerate(lent_tiles)
    ]

    def total(sources, chunks, s):
        found = []
        for source in sources:
            one = None
            for c in chunks:
                term = jnp.dot(source[c], held[c][s], preferred_element_type=jnp.float32)
                one = term if one is None else one + term
            found.append(one)
        rows_in_order = []
        for owner in range(wide):
            part = found[0]
            for k in range(1, wide):
                part = jnp.where((x - owner) % wide == k, found[k], part)
            rows_in_order.append(part)
        return jnp.concatenate(rows_in_order)

    def summed(totals):
        whole = scatter_sum(jnp.stack(totals), "core", 2)
        whole = jnp.swapaxes(whole, 1, 2)
        return scatter_sum(scatter_sum(whole, "x", 1), "y", 1)

    every = range(6)
    first_three = summed([total(sessions, every, s) for s in range(3)])
    guest_chunks = [{4: g[0], 5: g[1]} for g in guests]
    visitors = summed([total(guest_chunks, (4, 5), s) for s in (0, 2, 3)])
    visitors = lax.ppermute(visitors, "z", OUTWARD)
    last_one = summed([total(sessions, every, 3)])
    shares = jnp.concatenate([first_three, last_one]) + jnp.concatenate([jnp.zeros_like(last_one), visitors])
    proj = shares[jnp.asarray(PLACE)[z]].reshape(-1, wide * rows)
    flags = jnp.full((8, proj.shape[1]), over.astype(jnp.float32))
    proj = jnp.concatenate([proj, flags])

    blocks = jnp.stack(along_line(proj, inner))
    got = [pairs] + [lax.ppermute(pairs, "x", turn(wide, k)) for k in range(1, wide)]
    order = (x - jnp.arange(wide)) % wide
    all_pairs = jnp.stack(got)[order].reshape(-1, 2).T
    plane_blocks = wide * row_blocks
    ids = jnp.stack([jnp.asarray(PLACE)[z][all_pairs // plane_blocks], all_pairs % plane_blocks], axis=1)
    sums = pair_dots(blocks, ids, blk)
    high, cores = lax.axis_size("y"), lax.axis_size("core")
    sums = sums.reshape((wide, high, cores, -1) + sums.shape[1:])
    for axis, dim in (("core", 2), ("x", 0), ("y", 1)):
        sums = scatter_sum(sums, axis, dim)
    own = sums.reshape((-1,) + sums.shape[4:])
    scale = lax.rsqrt(own[:, blk : blk + 2] / P_SIZE + 1e-06)
    scores = own[:, :blk] / P_SIZE * scale[:, 0, :, None] * scale[:, 1, None, :]
    crowded = own[0, blk + 2, 0] > 0
    return lax.cond(crowded, lambda: dense(hist, tile_mask, planes, pairs), lambda: scores)


def solution(mesh):
    sess, act = mesh.shape["sess"], mesh.shape["act"]
    fine = Mesh(
        mesh.devices.reshape(DEPTH, sess // DEPTH, act // CORES, CORES), ("z", "x", "y", "core")
    )
    sess_axes, act_axes = ("z", "x"), ("y", "core")
    placed = (
        P(sess_axes, act_axes), P(sess_axes, act_axes), P(act_axes, sess_axes), P(sess_axes, None)
    )
    return jax.shard_map(
        body, mesh=fine, in_specs=placed, out_specs=P(sess_axes + act_axes, None, None), check_vma=False
    )
```

```python
import functools

import jax
import jax.numpy as jnp
import numpy as np
from jax import lax
from jax.experimental import pallas as pl
from jax.experimental.pallas import tpu as pltpu
from jax.sharding import Mesh, PartitionSpec as P

P_SIZE = 1024
DEPTH = 4
CORES = 2

NEAR = ((0, 1), (1, 0), (2, 3), (3, 2))
INWARD = ((0, 1), (3, 2))
OUTWARD = ((1, 0), (2, 3))
MIDDLE = ((1, 2), (2, 1))
SOURCE = np.array([[0, 1, 2, 3], [1, 0, 2, 3], [2, 3, 1, 0], [3, 2, 1, 0]], np.int32)
PLACE = np.argsort(SOURCE, axis=1).astype(np.int32)

LENT = (9, 32)


def bounds(total, parts):
    return [total * k // parts for k in range(parts + 1)]


def room(tiles):
    return min(tiles, -(-(tiles // 2 + int(2.6 * tiles**0.5)) // 2) * 2)


def params(**kwargs):
    return pltpu.CompilerParams(**kwargs)


def pack_kernel(blk, row_blocks, columns, slots, info, hist, out, sem):
    base = info[0]

    def one_column(c, used):
        start = pl.multiple_of((base + c) * blk, blk)
        for b in range(row_blocks):
            take = jnp.logical_and(info[1 + c * row_blocks + b] != 0, used < slots)

            @pl.when(take)
            def _():
                pltpu.make_async_copy(
                    hist.at[pl.ds(b * blk, blk), pl.ds(start, blk)], out.at[used], sem
                ).start()

            used = used + take.astype(jnp.int32)
        return used

    used = lax.fori_loop(0, columns, one_column, jnp.int32(0))

    def one_wait(_, carry):
        pltpu.make_async_copy(hist.at[pl.ds(0, blk), pl.ds(0, blk)], out.at[0], sem).wait()
        return carry

    lax.fori_loop(0, used, one_wait, 0)


def pack(hist, mask, base, slots):
    row_blocks, columns = mask.shape
    blk = hist.shape[0] // row_blocks
    info = jnp.concatenate([jnp.reshape(base, (1,)).astype(jnp.int32), mask.T.reshape(-1)])
    return pl.pallas_call(
        functools.partial(pack_kernel, blk, row_blocks, columns, slots),
        out_shape=jax.ShapeDtypeStruct((slots, blk, blk), hist.dtype),
        in_specs=[pl.BlockSpec(memory_space=pltpu.SMEM), pl.BlockSpec(memory_space=pl.ANY)],
        out_specs=pl.BlockSpec(memory_space=pltpu.VMEM),
        scratch_shapes=[pltpu.SemaphoreType.DMA],
        compiler_params=params(vmem_limit_bytes=32 << 20),
        cost_estimate=pl.CostEstimate(flops=0, bytes_accessed=2 * slots * blk * blk * 2, transcendentals=0),
        name="pack_tiles",
    )(info, hist)


def spread_kernel(blk, row_blocks, parts, slots, info, source, *refs):
    outs, sem = refs[: len(parts)], refs[len(parts)]
    base = info[0]
    used = jnp.int32(0)
    first = 0
    for out, columns in zip(outs, parts):

        def one_column(c, used, out=out, first=first):
            start = pl.multiple_of((base + first + c) * blk, blk)
            place = pl.multiple_of(c * blk, blk)
            for b in range(row_blocks):
                there = info[1 + (first + c) * row_blocks + b] != 0
                if slots is not None:
                    there = jnp.logical_and(there, used < slots)
                rows = pl.ds(b * blk, blk)

                @pl.when(there)
                def _():
                    tile = source.at[rows, pl.ds(start, blk)] if slots is None else source.at[used]
                    pltpu.make_async_copy(tile, out.at[rows, pl.ds(place, blk)], sem).start()

                @pl.when(jnp.logical_not(there))
                def _():
                    out[rows, pl.ds(place, blk)] = jnp.zeros((blk, blk), out.dtype)

                used = used + there.astype(jnp.int32)
            return used

        used = lax.fori_loop(0, columns, one_column, used)
        first += columns

    def one_wait(_, carry):
        tile = source.at[pl.ds(0, blk), pl.ds(0, blk)] if slots is None else source.at[0]
        pltpu.make_async_copy(tile, outs[0].at[pl.ds(0, blk), pl.ds(0, blk)], sem).wait()
        return carry

    lax.fori_loop(0, used, one_wait, 0)


def spread(source, mask, base, parts):
    row_blocks = mask.shape[0]
    packed = base is None
    blk = source.shape[1] if packed else source.shape[0] // row_blocks
    base = 0 if packed else base
    info = jnp.concatenate([jnp.reshape(base, (1,)).astype(jnp.int32), mask.T.reshape(-1)])
    shapes = [jax.ShapeDtypeStruct((row_blocks * blk, columns * blk), source.dtype) for columns in parts]
    return pl.pallas_call(
        functools.partial(spread_kernel, blk, row_blocks, parts, source.shape[0] if packed else None),
        out_shape=shapes,
        in_specs=[pl.BlockSpec(memory_space=pltpu.SMEM), pl.BlockSpec(memory_space=pl.ANY)],
        out_specs=[pl.BlockSpec(memory_space=pltpu.VMEM)] * len(parts),
        scratch_shapes=[pltpu.SemaphoreType.DMA],
        compiler_params=params(vmem_limit_bytes=32 << 20),
        cost_estimate=pl.CostEstimate(
            flops=0, bytes_accessed=4 * sum(parts) * row_blocks * blk * blk, transcendentals=0
        ),
        name="spread_tiles",
    )(info, source)


def dots_kernel(blk, count, ids, early, late, out):
    groups, share = early.shape[1] - 1, late.shape[1] - 8
    flag = jnp.sum(late[:, share : share + 1, :blk], axis=0)
    rest = jnp.zeros((out.shape[1] - blk - 3, blk), jnp.float32)

    def one(k, carry):
        def side(which):
            place, start = ids[which, 0, k], pl.multiple_of(ids[which, 1, k] * blk, blk)
            held = [early[place, g, :, pl.ds(start, blk)] for g in range(groups + 1)]
            held.append(late[place, :share, pl.ds(start, blk)])
            order = [ids[which, 2 + g, k] for g in range(groups + 2)]
            picked = []
            for g in range(groups + 2):
                part = held[0]
                for s in range(1, groups + 2):
                    part = jnp.where(order[g] == s, held[s], part)
                picked.append(part)
            return jnp.concatenate(picked)

        left, right = side(0), side(1)
        out[k, :blk, :] = lax.dot_general(
            left, right, (((0,), (0,)), ((), ())),
            precision=lax.Precision.HIGHEST, preferred_element_type=jnp.float32,
        )
        squares = [jnp.sum(v * v, axis=0, keepdims=True) for v in (left, right)]
        out[k, blk:, :] = jnp.concatenate(squares + [flag, rest])
        return carry

    lax.fori_loop(0, count, one, 0)


def pair_dots(early, late, ids, blk):
    count = ids.shape[2]
    return pl.pallas_call(
        functools.partial(dots_kernel, blk, count),
        out_shape=jax.ShapeDtypeStruct((count, blk + 8, blk), jnp.float32),
        in_specs=[pl.BlockSpec(memory_space=pltpu.SMEM)] + [pl.BlockSpec(memory_space=pltpu.VMEM)] * 2,
        out_specs=pl.BlockSpec(memory_space=pltpu.VMEM),
        compiler_params=params(vmem_limit_bytes=48 << 20),
        name="pair_dots",
    )(ids, early, late)


def turn(count, k):
    return [(d, (d + k) % count) for d in range(count)]


def scatter_sum(values, axis, dim):
    count = lax.axis_size(axis)
    here = lax.axis_index(axis)
    piece = values.shape[dim] // count

    def part(owner):
        return lax.dynamic_slice_in_dim(values, owner * piece, piece, dim)

    total = part(here)
    for k in range(1, count):
        total = total + lax.ppermute(part((here + k) % count), axis, turn(count, k))
    return total


def after(values, arrived):
    return lax.optimization_barrier((values, arrived))[0]


class Transfers:
    RATE = 1e5
    SLOTS = 5
    LATENCY = 2.0
    STEP = 1.0

    def __init__(self, depths):
        self.depths = depths
        self.listed = []
        self.got = {}

    def add(self, name, links, size, needs, make, axis, routes):
        self.listed.append((name, links, CORES * size / self.RATE, needs, make, axis, routes))

    def run(self):
        now, free, ends, waiting = 0.0, {}, {}, list(self.listed)
        while waiting:
            flying = [t for t in self.listed if ends.get(t[0], -1.0) > now]
            chosen = None
            for t in waiting:
                ready = all(ends.get(n, 1e9) <= now for n in t[3])
                room_left = all(sum(link in f[1] for f in flying) < self.depths[link] for link in t[1])
                if ready and room_left and len(flying) < self.SLOTS:
                    chosen = t
                    break
            if chosen is None:
                now = min(e for e in ends.values() if e > now)
                continue
            waiting.remove(chosen)
            name, links, length, _, make, axis, routes = chosen
            arrived = sorted((n for n in ends if ends[n] <= now), key=ends.get)[-self.SLOTS :]
            values = make()
            if arrived:
                values = after(values, [self.got[n] for n in arrived])
            self.got[name] = [lax.ppermute(v, axis, route) for v, route in zip(values, routes)]
            now += self.STEP
            end = max([now + self.LATENCY] + [free.get(link, 0.0) for link in links]) + length
            for link in links:
                free[link] = end
            ends[name] = end + self.STEP


def along_line(block, inner):
    near = lax.ppermute(block, "z", NEAR)
    middle = lax.ppermute(block, "z", MIDDLE)
    far = lax.ppermute(near, "z", MIDDLE)
    out1 = lax.ppermute(middle, "z", OUTWARD)
    out2 = lax.ppermute(far, "z", OUTWARD)
    return [block, near, jnp.where(inner, middle, out1), jnp.where(inner, far, out2)]


def dense(hist, tile_mask, planes, pairs):
    sess, act = ("z", "x"), ("y", "core")
    rows, acts = hist.shape
    row_blocks, act_blocks = tile_mask.shape
    blk = rows // row_blocks
    masked = (
        hist.reshape(row_blocks, blk, act_blocks, blk)
        * (tile_mask != 0).astype(jnp.bfloat16)[:, None, :, None]
    ).reshape(rows, acts)
    partial_proj = jnp.dot(
        masked, lax.all_gather(planes, sess, axis=1, tiled=True), preferred_element_type=jnp.float32
    )
    proj = lax.psum_scatter(partial_proj, act, scatter_dimension=1, tiled=True)
    own_count = pairs.shape[0] // lax.axis_size(act)
    place = lax.axis_index(act) * own_count
    sq = lax.psum(jnp.sum(proj * proj, axis=1), act)
    blocks = lax.all_gather(proj, sess, axis=0, tiled=True).reshape(-1, blk, proj.shape[1])
    norms = lax.all_gather(sq, sess, axis=0, tiled=True).reshape(-1, blk)
    dots = jnp.einsum(
        "kuc,kvc->kuv", blocks[pairs[:, 0]], blocks[pairs[:, 1]], precision=lax.Precision.HIGHEST
    )
    dots = lax.psum_scatter(dots, act, scatter_dimension=0, tiled=True)
    own = lax.dynamic_slice_in_dim(pairs, place, own_count, 0)
    scale = lax.rsqrt(norms[own] / P_SIZE + 1e-06)
    return dots / P_SIZE * scale[:, 0, :, None] * scale[:, 1, None, :]


def body(hist, tile_mask, planes, pairs):
    rows, acts = hist.shape
    row_blocks, act_blocks = tile_mask.shape
    blk = rows // row_blocks
    own_planes = planes.shape[1]
    wide = lax.axis_size("x")
    x, z = lax.axis_index("x"), lax.axis_index("z")
    inner = jnp.logical_or(z == 1, z == 2)
    columns = act_blocks // wide
    tile_mask = (tile_mask != 0).astype(jnp.int32)

    lent = columns * LENT[0] // LENT[1]
    kept = columns - lent
    cuts = [0] + [kept * c // 9 for c in (1, 3, 6, 9)] + [kept + c for c in bounds(lent, 2)[1:]]
    widths = [b - a for a, b in zip(cuts[:-1], cuts[1:])]
    streams = {"lent": (4, 6), "early": (0, 2), "late": (2, 4)}

    def mask_of(owner):
        return lax.dynamic_slice_in_dim(tile_mask, owner * columns, columns, 1)

    def over_x(make):
        return [lax.ppermute(make((x + k) % wide), "x", turn(wide, k)) for k in range(1, wide)]

    moves = Transfers({"x": 1, "in": 2, "out": 2, "mid": 2})
    row_routes = [turn(wide, k) for k in range(1, wide)]
    others = [(x + k) % wide for k in range(1, wide)]
    slots_of = {n: room((cuts[b] - cuts[a]) * row_blocks) for n, (a, b) in streams.items()}
    tile_bytes = blk * blk * 2
    groups, packs = {}, {}

    def planes_of(owner, first, last):
        start = (owner * columns + cuts[first]) * blk
        return lax.dynamic_slice_in_dim(planes, start, (cuts[last] - cuts[first]) * blk, 0)

    def group(c):
        if c not in groups:
            name, first = next((n, a) for n, a, b in plane_moves if a <= c < b)
            whole = jnp.zeros((widths[c] * blk, wide * own_planes), planes.dtype)
            whole = lax.dynamic_update_slice_in_dim(whole, planes_of(x, c, c + 1), x * own_planes, 1)
            for k in range(1, wide):
                part = moves.got[name][k - 1][(cuts[c] - cuts[first]) * blk : (cuts[c + 1] - cuts[first]) * blk]
                whole = lax.dynamic_update_slice_in_dim(whole, part, ((x - k) % wide) * own_planes, 1)
            groups[c] = whole
        return groups[c]

    def packed(name, owner, later):
        low, high = (cuts[c] for c in streams[name])
        mask = after(mask_of(owner)[:, low:high], moves.got[later])
        return pack(hist, mask, owner * columns + low, slots_of[name])

    plane_moves = [("planes0", 0, 1), ("planes1", 1, 2), ("planes2", 2, 4), ("planes4", 4, 6)]
    source_of = ["planes0", "planes1", "planes2", "planes2", "planes4", "planes4"]

    def add_planes(name, first, last):
        size = (cuts[last] - cuts[first]) * blk * own_planes * 2 * len(others)
        moves.add(
            name, ["x"], size, [], lambda: [planes_of(o, first, last) for o in others], "x", row_routes
        )

    def add_tiles(name, later):
        size = slots_of[name] * tile_bytes * len(others)
        moves.add(
            name, ["x"], size, [later], lambda: [packed(name, o, later) for o in others], "x", row_routes
        )

    def add_group(name, links, c, needs, make, routes):
        size = widths[c] * blk * wide * own_planes * 2
        moves.add(name, links, size, needs, lambda: [make()], "z", [routes])

    moves.add("masks", ["x"], 0, [], lambda: [mask_of(o) for o in others], "x", row_routes)
    for c in range(4):
        add_group(f"out2{c}", ["out"], c, [f"far{c}"], lambda c=c: moves.got[f"far{c}"][0], OUTWARD)
    for c in range(4):
        add_group(f"out1{c}", ["out"], c, [f"mid{c}"], lambda c=c: moves.got[f"mid{c}"][0], OUTWARD)
    for c in range(4):
        add_group(f"near{c}", ["in", "out"], c, [source_of[c]], lambda c=c: group(c), NEAR)
    for c in range(4):
        add_group(f"mid{c}", ["mid"], c, [source_of[c]], lambda c=c: group(c), MIDDLE)
    for c in range(4):
        add_group(f"far{c}", ["mid"], c, [f"near{c}"], lambda c=c: moves.got[f"near{c}"][0], MIDDLE)
    for c in (4, 5):
        add_group(f"mid{c}", ["mid"], c, [source_of[c]], lambda c=c: group(c), MIDDLE)
    for c in (4, 5):
        add_group(f"far{c}", ["mid"], c, [f"near{c}"], lambda c=c: moves.got[f"near{c}"][0], MIDDLE)
    for name, first, last in plane_moves[:3]:
        add_planes(name, first, last)
    moves.add(
        "guests", ["in"], 0, ["masks", "planes0"],
        lambda: [jnp.stack([mask_of(x)[:, kept:]] + [m[:, kept:] for m in moves.got["masks"]])], "z", [INWARD],
    )
    add_tiles("early", "planes0")
    add_planes(*plane_moves[3])
    add_tiles("lent", "planes1")
    add_tiles("late", "planes2")
    lent_bytes = slots_of["lent"] * tile_bytes
    moves.add("loan0", ["in"], lent_bytes, ["near3"], lambda: [packed("lent", x, "planes2")], "z", [INWARD])
    for c in (4, 5):
        add_group(f"near{c}", ["in"], c, [source_of[c]], lambda c=c: group(c), INWARD)
    moves.add(
        "loan1", ["in"], lent_bytes * len(others), ["lent"],
        lambda: moves.got["lent"], "z", [INWARD] * len(others),
    )
    moves.run()
    got = moves.got
    held = []
    for c in range(6):
        near, mid, far = got[f"near{c}"][0], got[f"mid{c}"][0], got[f"far{c}"][0]
        if c < 4:
            mid = jnp.where(inner, mid, got[f"out1{c}"][0])
            far = jnp.where(inner, far, got[f"out2{c}"][0])
        held.append([groups[c], near, mid, far])
    masks = [mask_of(x)] + got["masks"]
    guest_masks = got["guests"][0]

    over = jnp.int32(0)
    sessions = [[None] * 6 for _ in range(wide)]
    for name, (first, last) in streams.items():
        low, high = cuts[first], cuts[last]
        for owner in range(wide):
            count = jnp.sum(tile_mask[:, owner * columns + low : owner * columns + high])
            over = jnp.maximum(over, (count > room((high - low) * row_blocks)).astype(jnp.int32))
        parts = tuple(widths[first:last])
        for k in range(wide):
            mask = masks[k][:, low:high]
            if k == 0:
                later = got[{"early": "near0", "lent": "near1", "late": "near2"}[name]]
                sessions[k][first:last] = spread(hist, after(mask, later), x * columns + low, parts)
            else:
                sessions[k][first:last] = spread(got[name][k - 1], mask, None, parts)
    guests = [
        spread(t, guest_masks[k], None, tuple(widths[4:])) for k, t in enumerate(got["loan0"] + got["loan1"])
    ]

    def total(sources, chunks, s):
        found = []
        for source in sources:
            one = None
            for c in chunks:
                term = jnp.dot(source[c], held[c][s], preferred_element_type=jnp.float32)
                one = term if one is None else one + term
            found.append(one)
        rows_in_order = []
        for owner in range(wide):
            part = found[0]
            for k in range(1, wide):
                part = jnp.where((x - owner) % wide == k, found[k], part)
            rows_in_order.append(part)
        return jnp.concatenate(rows_in_order)

    def summed(totals):
        whole = scatter_sum(jnp.stack(totals), "core", 2)
        whole = jnp.swapaxes(whole, 1, 2)
        return scatter_sum(scatter_sum(whole, "x", 1), "y", 1)

    every = range(6)
    first_three = summed([total(sessions, every, s) for s in range(3)])
    guest_chunks = [{4: g[0], 5: g[1]} for g in guests]
    visitors = summed([total(guest_chunks, (4, 5), s) for s in (0, 2, 3)])
    visitors = lax.ppermute(visitors, "z", OUTWARD)
    early = first_three.at[1:].add(visitors[:2])
    early = jnp.stack(along_line(early, inner))
    last_one = summed([total(sessions, every, 3)])[0] + visitors[2]
    flags = jnp.full((8, last_one.shape[1]), over.astype(jnp.float32))
    late = jnp.stack(along_line(jnp.concatenate([last_one, flags]), inner))

    listed = [pairs] + [lax.ppermute(pairs, "x", route) for route in row_routes]
    order = (x - jnp.arange(wide)) % wide
    all_pairs = jnp.stack(listed)[order].reshape(-1, 2).T
    plane_blocks = wide * row_blocks
    of_plane = all_pairs // plane_blocks
    places = jnp.moveaxis(jnp.asarray(PLACE)[of_plane], 2, 1)
    ids = jnp.concatenate(
        [jnp.asarray(PLACE)[z][of_plane][:, None], (all_pairs % plane_blocks)[:, None], places], axis=1
    )
    sums = pair_dots(early, late, ids, blk)
    high, cores = lax.axis_size("y"), lax.axis_size("core")
    sums = sums.reshape((wide, high, cores, -1) + sums.shape[1:])
    for axis, dim in (("core", 2), ("x", 0), ("y", 1)):
        sums = scatter_sum(sums, axis, dim)
    own = sums.reshape((-1,) + sums.shape[4:])
    scale = lax.rsqrt(own[:, blk : blk + 2] / P_SIZE + 1e-06)
    scores = own[:, :blk] / P_SIZE * scale[:, 0, :, None] * scale[:, 1, None, :]
    crowded = own[0, blk + 2, 0] > 0
    return lax.cond(crowded, lambda: dense(hist, tile_mask, planes, pairs), lambda: scores)


def solution(mesh):
    sess, act = mesh.shape["sess"], mesh.shape["act"]
    fine = Mesh(
        mesh.devices.reshape(DEPTH, sess // DEPTH, act // CORES, CORES), ("z", "x", "y", "core")
    )
    sess_axes, act_axes = ("z", "x"), ("y", "core")
    placed = (
        P(sess_axes, act_axes), P(sess_axes, act_axes), P(act_axes, sess_axes), P(sess_axes, None)
    )
    return jax.shard_map(
        body, mesh=fine, in_specs=placed, out_specs=P(sess_axes + act_axes, None, None), check_vma=False
    )
```

```python
import functools

import jax
import jax.numpy as jnp
import numpy as np
from jax import lax
from jax.experimental import pallas as pl
from jax.experimental.pallas import tpu as pltpu
from jax.sharding import Mesh, PartitionSpec as P

P_SIZE = 1024
DEPTH = 4
CORES = 2

NEAR = ((0, 1), (1, 0), (2, 3), (3, 2))
INWARD = ((0, 1), (3, 2))
OUTWARD = ((1, 0), (2, 3))
MIDDLE = ((1, 2), (2, 1))
SOURCE = np.array([[0, 1, 2, 3], [1, 0, 2, 3], [2, 3, 1, 0], [3, 2, 1, 0]], np.int32)
PLACE = np.argsort(SOURCE, axis=1).astype(np.int32)

LENT = (9, 32)


def bounds(total, parts):
    return [total * k // parts for k in range(parts + 1)]


def room(tiles):
    return min(tiles, -(-(tiles // 2 + int(2.6 * tiles**0.5)) // 2) * 2)


def params(**kwargs):
    return pltpu.CompilerParams(**kwargs)


def pack_kernel(blk, row_blocks, columns, slots, info, hist, out, sem):
    base = info[0]

    def one_column(c, used):
        start = pl.multiple_of((base + c) * blk, blk)
        for b in range(row_blocks):
            take = jnp.logical_and(info[1 + c * row_blocks + b] != 0, used < slots)

            @pl.when(take)
            def _():
                pltpu.make_async_copy(
                    hist.at[pl.ds(b * blk, blk), pl.ds(start, blk)], out.at[used], sem
                ).start()

            used = used + take.astype(jnp.int32)
        return used

    used = lax.fori_loop(0, columns, one_column, jnp.int32(0))

    def one_wait(_, carry):
        pltpu.make_async_copy(hist.at[pl.ds(0, blk), pl.ds(0, blk)], out.at[0], sem).wait()
        return carry

    lax.fori_loop(0, used, one_wait, 0)


def pack(hist, mask, base, slots):
    row_blocks, columns = mask.shape
    blk = hist.shape[0] // row_blocks
    info = jnp.concatenate([jnp.reshape(base, (1,)).astype(jnp.int32), mask.T.reshape(-1)])
    return pl.pallas_call(
        functools.partial(pack_kernel, blk, row_blocks, columns, slots),
        out_shape=jax.ShapeDtypeStruct((slots, blk, blk), hist.dtype),
        in_specs=[pl.BlockSpec(memory_space=pltpu.SMEM), pl.BlockSpec(memory_space=pl.ANY)],
        out_specs=pl.BlockSpec(memory_space=pltpu.VMEM),
        scratch_shapes=[pltpu.SemaphoreType.DMA],
        compiler_params=params(vmem_limit_bytes=32 << 20),
        cost_estimate=pl.CostEstimate(flops=0, bytes_accessed=2 * slots * blk * blk * 2, transcendentals=0),
        name="pack_tiles",
    )(info, hist)


def spread_kernel(blk, row_blocks, parts, slots, info, source, *refs):
    outs, sem = refs[: len(parts)], refs[len(parts)]
    base = info[0]
    used = jnp.int32(0)
    first = 0
    for out, columns in zip(outs, parts):

        def one_column(c, used, out=out, first=first):
            start = pl.multiple_of((base + first + c) * blk, blk)
            place = pl.multiple_of(c * blk, blk)
            for b in range(row_blocks):
                there = info[1 + (first + c) * row_blocks + b] != 0
                if slots is not None:
                    there = jnp.logical_and(there, used < slots)
                rows = pl.ds(b * blk, blk)

                @pl.when(there)
                def _():
                    tile = source.at[rows, pl.ds(start, blk)] if slots is None else source.at[used]
                    pltpu.make_async_copy(tile, out.at[rows, pl.ds(place, blk)], sem).start()

                @pl.when(jnp.logical_not(there))
                def _():
                    out[rows, pl.ds(place, blk)] = jnp.zeros((blk, blk), out.dtype)

                used = used + there.astype(jnp.int32)
            return used

        used = lax.fori_loop(0, columns, one_column, used)
        first += columns

    def one_wait(_, carry):
        tile = source.at[pl.ds(0, blk), pl.ds(0, blk)] if slots is None else source.at[0]
        pltpu.make_async_copy(tile, outs[0].at[pl.ds(0, blk), pl.ds(0, blk)], sem).wait()
        return carry

    lax.fori_loop(0, used, one_wait, 0)


def spread(source, mask, base, parts):
    row_blocks = mask.shape[0]
    packed = base is None
    blk = source.shape[1] if packed else source.shape[0] // row_blocks
    base = 0 if packed else base
    info = jnp.concatenate([jnp.reshape(base, (1,)).astype(jnp.int32), mask.T.reshape(-1)])
    shapes = [jax.ShapeDtypeStruct((row_blocks * blk, columns * blk), source.dtype) for columns in parts]
    return pl.pallas_call(
        functools.partial(spread_kernel, blk, row_blocks, parts, source.shape[0] if packed else None),
        out_shape=shapes,
        in_specs=[pl.BlockSpec(memory_space=pltpu.SMEM), pl.BlockSpec(memory_space=pl.ANY)],
        out_specs=[pl.BlockSpec(memory_space=pltpu.VMEM)] * len(parts),
        scratch_shapes=[pltpu.SemaphoreType.DMA],
        compiler_params=params(vmem_limit_bytes=32 << 20),
        cost_estimate=pl.CostEstimate(
            flops=0, bytes_accessed=4 * sum(parts) * row_blocks * blk * blk, transcendentals=0
        ),
        name="spread_tiles",
    )(info, source)


def dots_kernel(blk, count, ids, early, late, out):
    groups, share = early.shape[1] - 1, late.shape[1] - 8
    flag = jnp.sum(late[:, share : share + 1, :blk], axis=0)
    rest = jnp.zeros((out.shape[1] - blk - 3, blk), jnp.float32)

    def one(k, carry):
        def side(which):
            place, start = ids[which, 0, k], pl.multiple_of(ids[which, 1, k] * blk, blk)
            held = [early[place, g, :, pl.ds(start, blk)] for g in range(groups + 1)]
            held.append(late[place, :share, pl.ds(start, blk)])
            order = [ids[which, 2 + g, k] for g in range(groups + 2)]
            picked = []
            for g in range(groups + 2):
                part = held[0]
                for s in range(1, groups + 2):
                    part = jnp.where(order[g] == s, held[s], part)
                picked.append(part)
            return jnp.concatenate(picked)

        left, right = side(0), side(1)
        out[k, :blk, :] = lax.dot_general(
            left, right, (((0,), (0,)), ((), ())),
            precision=lax.Precision.HIGHEST, preferred_element_type=jnp.float32,
        )
        squares = [jnp.sum(v * v, axis=0, keepdims=True) for v in (left, right)]
        out[k, blk:, :] = jnp.concatenate(squares + [flag, rest])
        return carry

    lax.fori_loop(0, count, one, 0)


def pair_dots(early, late, ids, blk):
    count = ids.shape[2]
    return pl.pallas_call(
        functools.partial(dots_kernel, blk, count),
        out_shape=jax.ShapeDtypeStruct((count, blk + 8, blk), jnp.float32),
        in_specs=[pl.BlockSpec(memory_space=pltpu.SMEM)] + [pl.BlockSpec(memory_space=pltpu.VMEM)] * 2,
        out_specs=pl.BlockSpec(memory_space=pltpu.VMEM),
        compiler_params=params(vmem_limit_bytes=48 << 20),
        name="pair_dots",
    )(ids, early, late)


def turn(count, k):
    return [(d, (d + k) % count) for d in range(count)]


def scatter_sum(values, axis, dim):
    count = lax.axis_size(axis)
    here = lax.axis_index(axis)
    piece = values.shape[dim] // count

    def part(owner):
        return lax.dynamic_slice_in_dim(values, owner * piece, piece, dim)

    total = part(here)
    for k in range(1, count):
        total = total + lax.ppermute(part((here + k) % count), axis, turn(count, k))
    return total


def after(values, arrived):
    return lax.optimization_barrier((values, arrived))[0]


class Lane:
    def __init__(self, arrived=None):
        self.arrived = arrived

    def send(self, values, axis, routes):
        if self.arrived is not None:
            values = after(values, self.arrived)
        self.arrived = [lax.ppermute(v, axis, route) for v, route in zip(values, routes)]
        return self.arrived


def along_line(block, inner):
    near = lax.ppermute(block, "z", NEAR)
    middle = lax.ppermute(block, "z", MIDDLE)
    far = lax.ppermute(near, "z", MIDDLE)
    out1 = lax.ppermute(middle, "z", OUTWARD)
    out2 = lax.ppermute(far, "z", OUTWARD)
    return [block, near, jnp.where(inner, middle, out1), jnp.where(inner, far, out2)]


def dense(hist, tile_mask, planes, pairs):
    sess, act = ("z", "x"), ("y", "core")
    rows, acts = hist.shape
    row_blocks, act_blocks = tile_mask.shape
    blk = rows // row_blocks
    masked = (
        hist.reshape(row_blocks, blk, act_blocks, blk)
        * (tile_mask != 0).astype(jnp.bfloat16)[:, None, :, None]
    ).reshape(rows, acts)
    partial_proj = jnp.dot(
        masked, lax.all_gather(planes, sess, axis=1, tiled=True), preferred_element_type=jnp.float32
    )
    proj = lax.psum_scatter(partial_proj, act, scatter_dimension=1, tiled=True)
    own_count = pairs.shape[0] // lax.axis_size(act)
    place = lax.axis_index(act) * own_count
    sq = lax.psum(jnp.sum(proj * proj, axis=1), act)
    blocks = lax.all_gather(proj, sess, axis=0, tiled=True).reshape(-1, blk, proj.shape[1])
    norms = lax.all_gather(sq, sess, axis=0, tiled=True).reshape(-1, blk)
    dots = jnp.einsum(
        "kuc,kvc->kuv", blocks[pairs[:, 0]], blocks[pairs[:, 1]], precision=lax.Precision.HIGHEST
    )
    dots = lax.psum_scatter(dots, act, scatter_dimension=0, tiled=True)
    own = lax.dynamic_slice_in_dim(pairs, place, own_count, 0)
    scale = lax.rsqrt(norms[own] / P_SIZE + 1e-06)
    return dots / P_SIZE * scale[:, 0, :, None] * scale[:, 1, None, :]


def body(hist, tile_mask, planes, pairs):
    rows, acts = hist.shape
    row_blocks, act_blocks = tile_mask.shape
    blk = rows // row_blocks
    own_planes = planes.shape[1]
    wide = lax.axis_size("x")
    x, z = lax.axis_index("x"), lax.axis_index("z")
    inner = jnp.logical_or(z == 1, z == 2)
    columns = act_blocks // wide
    tile_mask = (tile_mask != 0).astype(jnp.int32)

    lent = columns * LENT[0] // LENT[1]
    kept = columns - lent
    cuts = [0, kept // 3, kept, columns]
    widths = [b - a for a, b in zip(cuts[:-1], cuts[1:])]
    slots = [room(w * row_blocks) for w in widths]

    def mask_of(owner):
        return lax.dynamic_slice_in_dim(tile_mask, owner * columns, columns, 1)

    def over_x(make):
        return [lax.ppermute(make((x + k) % wide), "x", turn(wide, k)) for k in range(1, wide)]

    others = [(x + k) % wide for k in range(1, wide)]
    row_routes = [turn(wide, k) for k in range(1, wide)]

    def in_row_order(parts, dim):
        ordered = []
        for owner in range(wide):
            chosen = parts[0]
            for k in range(1, wide):
                chosen = jnp.where((x - owner) % wide == k, parts[k], chosen)
            ordered.append(chosen)
        return jnp.concatenate(ordered, axis=dim)

    def planes_of(owner, c):
        return lax.dynamic_slice_in_dim(planes, (owner * columns + cuts[c]) * blk, widths[c] * blk, 0)

    def packed(owner, c, later):
        mask = after(mask_of(owner)[:, cuts[c] : cuts[c + 1]], later)
        return pack(hist, mask, owner * columns + cuts[c], slots[c])

    over_x = Lane()
    groups = []
    for c in range(3):
        got = over_x.send([planes_of(o, c) for o in others], "x", row_routes)
        groups.append(in_row_order([planes_of(x, c)] + got, 1))
        if c == 0:
            start = got
            others_masks = [
                lax.ppermute(after(mask_of(o), start), "x", r) for o, r in zip(others, row_routes)
            ]
    tiles = [None] * 3
    for c in (0, 2, 1):
        tiles[c] = over_x.send([packed(o, c, groups[0]) for o in others], "x", row_routes)

    ends, middle = Lane(), Lane()
    near, mid, far = [], [], []
    for c in range(2):
        near += ends.send([groups[c]], "z", [NEAR])
        mid += middle.send([groups[c]], "z", [MIDDLE])
    inward, outward = Lane(near[1:]), Lane(near[1:])
    for c in range(2):
        far += middle.send([near[c]], "z", [MIDDLE])
    loans = inward.send([packed(x, 2, near[0])], "z", [INWARD])
    near += inward.send([groups[2]], "z", [INWARD])
    mid += middle.send([groups[2]], "z", [MIDDLE])
    far += middle.send([near[2]], "z", [MIDDLE])
    outer = [outward.send([v], "z", [OUTWARD])[0] for v in mid[:2] + far[:2]]
    loans = loans + inward.send(tiles[2], "z", [INWARD] * len(others))
    masks = [mask_of(x)] + others_masks
    guest_masks = lax.ppermute(jnp.stack([m[:, kept:] for m in masks]), "z", INWARD)
    held = [
        [groups[c], near[c], jnp.where(inner, mid[c], outer[c]), jnp.where(inner, far[c], outer[2 + c])]
        for c in range(2)
    ]
    held.append([groups[2], near[2], mid[2], far[2]])

    over = jnp.int32(0)
    sessions = [[None] * 3 for _ in range(wide)]
    for c in range(3):
        for owner in range(wide):
            count = jnp.sum(tile_mask[:, owner * columns + cuts[c] : owner * columns + cuts[c + 1]])
            over = jnp.maximum(over, (count > slots[c]).astype(jnp.int32))
        for k in range(wide):
            mask = masks[k][:, cuts[c] : cuts[c + 1]]
            if k == 0:
                (sessions[k][c],) = spread(hist, after(mask, near[0]), x * columns + cuts[c], (widths[c],))
            else:
                (sessions[k][c],) = spread(tiles[c][k - 1], mask, None, (widths[c],))
    guests = [{2: spread(t, guest_masks[k], None, (widths[2],))[0]} for k, t in enumerate(loans)]

    def total(sources, chunks, s):
        found = []
        for source in sources:
            one = None
            for c in chunks:
                term = jnp.dot(source[c], held[c][s], preferred_element_type=jnp.float32)
                one = term if one is None else one + term
            found.append(one)
        return in_row_order(found, 0)

    def summed(totals):
        whole = scatter_sum(jnp.stack(totals), "core", 2)
        whole = jnp.swapaxes(whole, 1, 2)
        return scatter_sum(scatter_sum(whole, "x", 1), "y", 1)

    every = range(3)
    first_three = summed([total(sessions, every, s) for s in range(3)])
    visitors = summed([total(guests, (2,), s) for s in (0, 2, 3)])
    visitors = lax.ppermute(visitors, "z", OUTWARD)
    early = first_three.at[1:].add(visitors[:2])
    early = jnp.stack(along_line(early, inner))
    last_one = summed([total(sessions, every, 3)])[0] + visitors[2]
    flags = jnp.full((8, last_one.shape[1]), over.astype(jnp.float32))
    late = jnp.stack(along_line(jnp.concatenate([last_one, flags]), inner))

    listed = [pairs] + [lax.ppermute(pairs, "x", route) for route in row_routes]
    order = (x - jnp.arange(wide)) % wide
    all_pairs = jnp.stack(listed)[order].reshape(-1, 2).T
    plane_blocks = wide * row_blocks
    of_plane = all_pairs // plane_blocks
    places = jnp.moveaxis(jnp.asarray(PLACE)[of_plane], 2, 1)
    ids = jnp.concatenate(
        [jnp.asarray(PLACE)[z][of_plane][:, None], (all_pairs % plane_blocks)[:, None], places], axis=1
    )
    sums = pair_dots(early, late, ids, blk)
    high, cores = lax.axis_size("y"), lax.axis_size("core")
    sums = sums.reshape((wide, high, cores, -1) + sums.shape[1:])
    for axis, dim in (("core", 2), ("x", 0), ("y", 1)):
        sums = scatter_sum(sums, axis, dim)
    own = sums.reshape((-1,) + sums.shape[4:])
    scale = lax.rsqrt(own[:, blk : blk + 2] / P_SIZE + 1e-06)
    scores = own[:, :blk] / P_SIZE * scale[:, 0, :, None] * scale[:, 1, None, :]
    crowded = own[0, blk + 2, 0] > 0
    return lax.cond(crowded, lambda: dense(hist, tile_mask, planes, pairs), lambda: scores)


def solution(mesh):
    sess, act = mesh.shape["sess"], mesh.shape["act"]
    fine = Mesh(
        mesh.devices.reshape(DEPTH, sess // DEPTH, act // CORES, CORES), ("z", "x", "y", "core")
    )
    sess_axes, act_axes = ("z", "x"), ("y", "core")
    placed = (
        P(sess_axes, act_axes), P(sess_axes, act_axes), P(act_axes, sess_axes), P(sess_axes, None)
    )
    return jax.shard_map(
        body, mesh=fine, in_specs=placed, out_specs=P(sess_axes + act_axes, None, None), check_vma=False
    )
```

```python
import functools

import jax
import jax.numpy as jnp
import numpy as np
from jax import lax
from jax.experimental import pallas as pl
from jax.experimental.pallas import tpu as pltpu
from jax.sharding import Mesh, PartitionSpec as P

P_SIZE = 1024
DEPTH = 4
CORES = 2

NEAR = ((0, 1), (1, 0), (2, 3), (3, 2))
INWARD = ((0, 1), (3, 2))
OUTWARD = ((1, 0), (2, 3))
MIDDLE = ((1, 2), (2, 1))
SOURCE = np.array([[0, 1, 2, 3], [1, 0, 2, 3], [2, 3, 1, 0], [3, 2, 1, 0]], np.int32)
PLACE = np.argsort(SOURCE, axis=1).astype(np.int32)

LENT = (9, 32)


def bounds(total, parts):
    return [total * k // parts for k in range(parts + 1)]


def room(tiles):
    return min(tiles, -(-(tiles // 2 + int(2.6 * tiles**0.5)) // 2) * 2)


def params(**kwargs):
    return pltpu.CompilerParams(**kwargs)


def pack_kernel(blk, row_blocks, columns, slots, info, hist, out, sem):
    base = info[0]

    def one_column(c, used):
        start = pl.multiple_of((base + c) * blk, blk)
        for b in range(row_blocks):
            take = jnp.logical_and(info[1 + c * row_blocks + b] != 0, used < slots)

            @pl.when(take)
            def _():
                pltpu.make_async_copy(
                    hist.at[pl.ds(b * blk, blk), pl.ds(start, blk)], out.at[used], sem
                ).start()

            used = used + take.astype(jnp.int32)
        return used

    used = lax.fori_loop(0, columns, one_column, jnp.int32(0))

    def one_wait(_, carry):
        pltpu.make_async_copy(hist.at[pl.ds(0, blk), pl.ds(0, blk)], out.at[0], sem).wait()
        return carry

    lax.fori_loop(0, used, one_wait, 0)


def pack(hist, mask, base, slots):
    row_blocks, columns = mask.shape
    blk = hist.shape[0] // row_blocks
    info = jnp.concatenate([jnp.reshape(base, (1,)).astype(jnp.int32), mask.T.reshape(-1)])
    return pl.pallas_call(
        functools.partial(pack_kernel, blk, row_blocks, columns, slots),
        out_shape=jax.ShapeDtypeStruct((slots, blk, blk), hist.dtype),
        in_specs=[pl.BlockSpec(memory_space=pltpu.SMEM), pl.BlockSpec(memory_space=pl.ANY)],
        out_specs=pl.BlockSpec(memory_space=pltpu.VMEM),
        scratch_shapes=[pltpu.SemaphoreType.DMA],
        compiler_params=params(vmem_limit_bytes=32 << 20),
        cost_estimate=pl.CostEstimate(flops=0, bytes_accessed=2 * slots * blk * blk * 2, transcendentals=0),
        name="pack_tiles",
    )(info, hist)


def spread_kernel(blk, row_blocks, parts, slots, info, source, *refs):
    outs, sem = refs[: len(parts)], refs[len(parts)]
    base = info[0]
    used = jnp.int32(0)
    first = 0
    for out, columns in zip(outs, parts):

        def one_column(c, used, out=out, first=first):
            start = pl.multiple_of((base + first + c) * blk, blk)
            place = pl.multiple_of(c * blk, blk)
            for b in range(row_blocks):
                there = info[1 + (first + c) * row_blocks + b] != 0
                if slots is not None:
                    there = jnp.logical_and(there, used < slots)
                rows = pl.ds(b * blk, blk)

                @pl.when(there)
                def _():
                    tile = source.at[rows, pl.ds(start, blk)] if slots is None else source.at[used]
                    pltpu.make_async_copy(tile, out.at[rows, pl.ds(place, blk)], sem).start()

                @pl.when(jnp.logical_not(there))
                def _():
                    out[rows, pl.ds(place, blk)] = jnp.zeros((blk, blk), out.dtype)

                used = used + there.astype(jnp.int32)
            return used

        used = lax.fori_loop(0, columns, one_column, used)
        first += columns

    def one_wait(_, carry):
        tile = source.at[pl.ds(0, blk), pl.ds(0, blk)] if slots is None else source.at[0]
        pltpu.make_async_copy(tile, outs[0].at[pl.ds(0, blk), pl.ds(0, blk)], sem).wait()
        return carry

    lax.fori_loop(0, used, one_wait, 0)


def spread(source, mask, base, parts):
    row_blocks = mask.shape[0]
    packed = base is None
    blk = source.shape[1] if packed else source.shape[0] // row_blocks
    base = 0 if packed else base
    info = jnp.concatenate([jnp.reshape(base, (1,)).astype(jnp.int32), mask.T.reshape(-1)])
    shapes = [jax.ShapeDtypeStruct((row_blocks * blk, columns * blk), source.dtype) for columns in parts]
    return pl.pallas_call(
        functools.partial(spread_kernel, blk, row_blocks, parts, source.shape[0] if packed else None),
        out_shape=shapes,
        in_specs=[pl.BlockSpec(memory_space=pltpu.SMEM), pl.BlockSpec(memory_space=pl.ANY)],
        out_specs=[pl.BlockSpec(memory_space=pltpu.VMEM)] * len(parts),
        scratch_shapes=[pltpu.SemaphoreType.DMA],
        compiler_params=params(vmem_limit_bytes=32 << 20),
        cost_estimate=pl.CostEstimate(
            flops=0, bytes_accessed=4 * sum(parts) * row_blocks * blk * blk, transcendentals=0
        ),
        name="spread_tiles",
    )(info, source)


def dots_kernel(blk, count, ids, early, late, out):
    groups, share = early.shape[1] - 1, late.shape[1] - 8
    flag = jnp.sum(late[:, share : share + 1, :blk], axis=0)
    rest = jnp.zeros((out.shape[1] - blk - 3, blk), jnp.float32)

    def one(k, carry):
        def side(which):
            place, start = ids[which, 0, k], pl.multiple_of(ids[which, 1, k] * blk, blk)
            held = [early[place, g, :, pl.ds(start, blk)] for g in range(groups + 1)]
            held.append(late[place, :share, pl.ds(start, blk)])
            order = [ids[which, 2 + g, k] for g in range(groups + 2)]
            picked = []
            for g in range(groups + 2):
                part = held[0]
                for s in range(1, groups + 2):
                    part = jnp.where(order[g] == s, held[s], part)
                picked.append(part)
            return jnp.concatenate(picked)

        left, right = side(0), side(1)
        out[k, :blk, :] = lax.dot_general(
            left, right, (((0,), (0,)), ((), ())),
            precision=lax.Precision.HIGHEST, preferred_element_type=jnp.float32,
        )
        squares = [jnp.sum(v * v, axis=0, keepdims=True) for v in (left, right)]
        out[k, blk:, :] = jnp.concatenate(squares + [flag, rest])
        return carry

    lax.fori_loop(0, count, one, 0)


def pair_dots(early, late, ids, blk):
    count = ids.shape[2]
    return pl.pallas_call(
        functools.partial(dots_kernel, blk, count),
        out_shape=jax.ShapeDtypeStruct((count, blk + 8, blk), jnp.float32),
        in_specs=[pl.BlockSpec(memory_space=pltpu.SMEM)] + [pl.BlockSpec(memory_space=pltpu.VMEM)] * 2,
        out_specs=pl.BlockSpec(memory_space=pltpu.VMEM),
        compiler_params=params(vmem_limit_bytes=48 << 20),
        name="pair_dots",
    )(ids, early, late)


def turn(count, k):
    return [(d, (d + k) % count) for d in range(count)]


def scatter_sum(values, axis, dim):
    count = lax.axis_size(axis)
    here = lax.axis_index(axis)
    piece = values.shape[dim] // count

    def part(owner):
        return lax.dynamic_slice_in_dim(values, owner * piece, piece, dim)

    total = part(here)
    for k in range(1, count):
        total = total + lax.ppermute(part((here + k) % count), axis, turn(count, k))
    return total


def after(values, arrived):
    return lax.optimization_barrier((values, arrived))[0]


class Lane:
    def __init__(self, arrived=None):
        self.arrived = arrived

    def send(self, values, axis, routes):
        if self.arrived is not None:
            values = after(values, self.arrived)
        self.arrived = [lax.ppermute(v, axis, route) for v, route in zip(values, routes)]
        return self.arrived


def along_line(block, inner):
    near = lax.ppermute(block, "z", NEAR)
    middle = lax.ppermute(block, "z", MIDDLE)
    far = lax.ppermute(near, "z", MIDDLE)
    out1 = lax.ppermute(middle, "z", OUTWARD)
    out2 = lax.ppermute(far, "z", OUTWARD)
    return [block, near, jnp.where(inner, middle, out1), jnp.where(inner, far, out2)]


def dense(hist, tile_mask, planes, pairs):
    sess, act = ("z", "x"), ("y", "core")
    rows, acts = hist.shape
    row_blocks, act_blocks = tile_mask.shape
    blk = rows // row_blocks
    masked = (
        hist.reshape(row_blocks, blk, act_blocks, blk)
        * (tile_mask != 0).astype(jnp.bfloat16)[:, None, :, None]
    ).reshape(rows, acts)
    partial_proj = jnp.dot(
        masked, lax.all_gather(planes, sess, axis=1, tiled=True), preferred_element_type=jnp.float32
    )
    proj = lax.psum_scatter(partial_proj, act, scatter_dimension=1, tiled=True)
    own_count = pairs.shape[0] // lax.axis_size(act)
    place = lax.axis_index(act) * own_count
    sq = lax.psum(jnp.sum(proj * proj, axis=1), act)
    blocks = lax.all_gather(proj, sess, axis=0, tiled=True).reshape(-1, blk, proj.shape[1])
    norms = lax.all_gather(sq, sess, axis=0, tiled=True).reshape(-1, blk)
    dots = jnp.einsum(
        "kuc,kvc->kuv", blocks[pairs[:, 0]], blocks[pairs[:, 1]], precision=lax.Precision.HIGHEST
    )
    dots = lax.psum_scatter(dots, act, scatter_dimension=0, tiled=True)
    own = lax.dynamic_slice_in_dim(pairs, place, own_count, 0)
    scale = lax.rsqrt(norms[own] / P_SIZE + 1e-06)
    return dots / P_SIZE * scale[:, 0, :, None] * scale[:, 1, None, :]


def body(hist, tile_mask, planes, pairs):
    rows, acts = hist.shape
    row_blocks, act_blocks = tile_mask.shape
    blk = rows // row_blocks
    own_planes = planes.shape[1]
    wide = lax.axis_size("x")
    x, z = lax.axis_index("x"), lax.axis_index("z")
    inner = jnp.logical_or(z == 1, z == 2)
    columns = act_blocks // wide
    tile_mask = (tile_mask != 0).astype(jnp.int32)

    lent = columns * LENT[0] // LENT[1]
    kept = columns - lent
    cuts = [0, kept // 3, kept, columns]
    widths = [b - a for a, b in zip(cuts[:-1], cuts[1:])]
    slots = [room(w * row_blocks) for w in widths]

    def mask_of(owner):
        return lax.dynamic_slice_in_dim(tile_mask, owner * columns, columns, 1)

    def over_x(make):
        return [lax.ppermute(make((x + k) % wide), "x", turn(wide, k)) for k in range(1, wide)]

    others = [(x + k) % wide for k in range(1, wide)]
    row_routes = [turn(wide, k) for k in range(1, wide)]

    def in_row_order(parts, dim):
        ordered = []
        for owner in range(wide):
            chosen = parts[0]
            for k in range(1, wide):
                chosen = jnp.where((x - owner) % wide == k, parts[k], chosen)
            ordered.append(chosen)
        return jnp.concatenate(ordered, axis=dim)

    def planes_of(owner, c):
        return lax.dynamic_slice_in_dim(planes, (owner * columns + cuts[c]) * blk, widths[c] * blk, 0)

    def packed(owner, c, later):
        mask = after(mask_of(owner)[:, cuts[c] : cuts[c + 1]], later)
        return pack(hist, mask, owner * columns + cuts[c], slots[c])

    over_x = Lane()
    both_masks = jnp.stack([tile_mask, lax.ppermute(tile_mask, "z", INWARD)])

    def both_of(owner):
        return lax.dynamic_slice_in_dim(both_masks, owner * columns, columns, 2)

    known = [both_of(x)] + [lax.ppermute(both_of(o), "x", r) for o, r in zip(others, row_routes)]
    listed = [pairs] + [lax.ppermute(pairs, "x", route) for route in row_routes]
    masks, guest_masks = [m[0] for m in known], [m[1][:, kept:] for m in known]
    groups = []
    for c in range(3):
        got = over_x.send([planes_of(o, c) for o in others], "x", row_routes)
        groups.append(in_row_order([planes_of(x, c)] + got, 1))
        if c == 0:
            over_x.arrived = got + known[1:] + listed[1:]
    tiles = [None] * 3
    for c in (0, 2, 1):
        tiles[c] = over_x.send([packed(o, c, groups[0]) for o in others], "x", row_routes)

    ends, middle = Lane(), Lane()
    near, mid, far = [], [], []
    for c in range(2):
        near += ends.send([groups[c]], "z", [NEAR])
        mid += middle.send([groups[c]], "z", [MIDDLE])
    inward, outward = Lane(near[1:]), Lane(near[1:])
    for c in range(2):
        far += middle.send([near[c]], "z", [MIDDLE])
    loans = inward.send([packed(x, 2, near[0])], "z", [INWARD])
    near += inward.send([groups[2]], "z", [INWARD])
    mid += middle.send([groups[2]], "z", [MIDDLE])
    far += middle.send([near[2]], "z", [MIDDLE])
    outer = [outward.send([v], "z", [OUTWARD])[0] for v in (mid[0], mid[1], far[1], far[0])]
    loans = loans + inward.send(tiles[2], "z", [INWARD] * len(others))
    held = [
        [groups[c], near[c], jnp.where(inner, mid[c], outer[c]), jnp.where(inner, far[c], outer[3 - c])]
        for c in range(2)
    ]
    held.append([groups[2], near[2], mid[2], far[2]])

    over = jnp.int32(0)
    sessions = [[None] * 3 for _ in range(wide)]
    for c in range(3):
        for owner in range(wide):
            count = jnp.sum(tile_mask[:, owner * columns + cuts[c] : owner * columns + cuts[c + 1]])
            over = jnp.maximum(over, (count > slots[c]).astype(jnp.int32))
        for k in range(wide):
            mask = masks[k][:, cuts[c] : cuts[c + 1]]
            if k == 0:
                (sessions[k][c],) = spread(hist, after(mask, near[0]), x * columns + cuts[c], (widths[c],))
            else:
                (sessions[k][c],) = spread(tiles[c][k - 1], mask, None, (widths[c],))
    guests = [{2: spread(t, guest_masks[k], None, (widths[2],))[0]} for k, t in enumerate(loans)]

    def total(sources, chunks, s):
        found = []
        for source in sources:
            one = None
            for c in chunks:
                term = jnp.dot(source[c], held[c][s], preferred_element_type=jnp.float32)
                one = term if one is None else one + term
            found.append(one)
        return in_row_order(found, 0)

    def summed(totals):
        whole = scatter_sum(jnp.stack(totals), "core", 2)
        whole = jnp.swapaxes(whole, 1, 2)
        return scatter_sum(scatter_sum(whole, "x", 1), "y", 1)

    every = range(3)
    first_three = summed([total(sessions, every, s) for s in range(3)])
    visitors = summed([total(guests, (2,), s) for s in (0, 2, 3)])
    visitors = lax.ppermute(visitors, "z", OUTWARD)
    early = first_three.at[1:].add(visitors[:2])
    early = jnp.stack(along_line(early, inner))
    last_one = summed([total(sessions, every, 3)])[0] + visitors[2]
    flags = jnp.full((8, last_one.shape[1]), over.astype(jnp.float32))
    late = jnp.stack(along_line(jnp.concatenate([last_one, flags]), inner))

    order = (x - jnp.arange(wide)) % wide
    all_pairs = jnp.stack(listed)[order].reshape(-1, 2).T
    plane_blocks = wide * row_blocks
    of_plane = all_pairs // plane_blocks
    places = jnp.moveaxis(jnp.asarray(PLACE)[of_plane], 2, 1)
    ids = jnp.concatenate(
        [jnp.asarray(PLACE)[z][of_plane][:, None], (all_pairs % plane_blocks)[:, None], places], axis=1
    )
    sums = pair_dots(early, late, ids, blk)
    high, cores = lax.axis_size("y"), lax.axis_size("core")
    sums = sums.reshape((wide, high, cores, -1) + sums.shape[1:])
    for axis, dim in (("core", 2), ("x", 0), ("y", 1)):
        sums = scatter_sum(sums, axis, dim)
    own = sums.reshape((-1,) + sums.shape[4:])
    scale = lax.rsqrt(own[:, blk : blk + 2] / P_SIZE + 1e-06)
    scores = own[:, :blk] / P_SIZE * scale[:, 0, :, None] * scale[:, 1, None, :]
    crowded = own[0, blk + 2, 0] > 0
    return lax.cond(crowded, lambda: dense(hist, tile_mask, planes, pairs), lambda: scores)


def solution(mesh):
    sess, act = mesh.shape["sess"], mesh.shape["act"]
    fine = Mesh(
        mesh.devices.reshape(DEPTH, sess // DEPTH, act // CORES, CORES), ("z", "x", "y", "core")
    )
    sess_axes, act_axes = ("z", "x"), ("y", "core")
    placed = (
        P(sess_axes, act_axes), P(sess_axes, act_axes), P(act_axes, sess_axes), P(sess_axes, None)
    )
    return jax.shard_map(
        body, mesh=fine, in_specs=placed, out_specs=P(sess_axes + act_axes, None, None), check_vma=False
    )
```

```python
import functools

import jax
import jax.numpy as jnp
import numpy as np
from jax import lax
from jax.experimental import pallas as pl
from jax.experimental.pallas import tpu as pltpu
from jax.sharding import Mesh, PartitionSpec as P

P_SIZE = 1024
DEPTH = 4
CORES = 2

NEAR = ((0, 1), (1, 0), (2, 3), (3, 2))
INWARD = ((0, 1), (3, 2))
OUTWARD = ((1, 0), (2, 3))
MIDDLE = ((1, 2), (2, 1))
SOURCE = np.array([[0, 1, 2, 3], [1, 0, 2, 3], [2, 3, 1, 0], [3, 2, 1, 0]], np.int32)
PLACE = np.argsort(SOURCE, axis=1).astype(np.int32)

LENT = (9, 32)


def bounds(total, parts):
    return [total * k // parts for k in range(parts + 1)]


def room(tiles):
    return min(tiles, -(-(tiles // 2 + int(2.6 * tiles**0.5)) // 2) * 2)


def params(**kwargs):
    return pltpu.CompilerParams(**kwargs)


def pack_kernel(blk, row_blocks, columns, slots, info, hist, out, sem):
    base = info[0]

    def one_column(c, used):
        start = pl.multiple_of((base + c) * blk, blk)
        for b in range(row_blocks):
            take = jnp.logical_and(info[1 + c * row_blocks + b] != 0, used < slots)

            @pl.when(take)
            def _():
                pltpu.make_async_copy(
                    hist.at[pl.ds(b * blk, blk), pl.ds(start, blk)], out.at[used], sem
                ).start()

            used = used + take.astype(jnp.int32)
        return used

    used = lax.fori_loop(0, columns, one_column, jnp.int32(0))

    def one_wait(_, carry):
        pltpu.make_async_copy(hist.at[pl.ds(0, blk), pl.ds(0, blk)], out.at[0], sem).wait()
        return carry

    lax.fori_loop(0, used, one_wait, 0)


def pack(hist, mask, base, slots):
    row_blocks, columns = mask.shape
    blk = hist.shape[0] // row_blocks
    info = jnp.concatenate([jnp.reshape(base, (1,)).astype(jnp.int32), mask.T.reshape(-1)])
    return pl.pallas_call(
        functools.partial(pack_kernel, blk, row_blocks, columns, slots),
        out_shape=jax.ShapeDtypeStruct((slots, blk, blk), hist.dtype),
        in_specs=[pl.BlockSpec(memory_space=pltpu.SMEM), pl.BlockSpec(memory_space=pl.ANY)],
        out_specs=pl.BlockSpec(memory_space=pltpu.VMEM),
        scratch_shapes=[pltpu.SemaphoreType.DMA],
        compiler_params=params(vmem_limit_bytes=32 << 20),
        cost_estimate=pl.CostEstimate(flops=0, bytes_accessed=2 * slots * blk * blk * 2, transcendentals=0),
        name="pack_tiles",
    )(info, hist)


STRIDE = 4


def product_kernel(blk, row_blocks, steps, slots, paired, info, *refs):
    count, groups = len(slots), len(paired)
    sources, refs = refs[:count], refs[count:]
    planes, at = [], 0
    for two in paired:
        planes.append(refs[at : at + 1 + two])
        at += 1 + two
    out, total, tiles, held, tile_sem, held_sem = refs[at:]
    rows = row_blocks * blk
    depth = STRIDE * blk
    inner, base = info[0] != 0, info[1]
    per_source = steps * STRIDE * row_blocks

    def fetch(i, slot, used, active):
        first = pl.multiple_of(i * depth, depth)
        for g, choice in enumerate(planes):
            for which, ref in enumerate(choice):
                wanted = active
                if len(choice) == 2:
                    wanted = jnp.logical_and(active, inner if which == 0 else jnp.logical_not(inner))

                @pl.when(wanted)
                def _():
                    pltpu.make_async_copy(ref.at[pl.ds(first, depth)], held.at[slot, g], held_sem.at[slot]).start()

        started = jnp.int32(0)
        following = []
        for k in range(count):
            mine = used[k]
            for j in range(STRIDE):
                column = i * STRIDE + j
                start = pl.multiple_of((base + column) * blk, blk)
                for b in range(row_blocks):
                    there = info[2 + count + k * per_source + column * row_blocks + b] != 0
                    there = jnp.logical_and(there, active)
                    if slots[k] is not None:
                        there = jnp.logical_and(there, mine < slots[k])
                    place = (pl.ds(k * rows + b * blk, blk), pl.ds(j * blk, blk))

                    @pl.when(there)
                    def _():
                        if slots[k] is None:
                            tile = sources[k].at[pl.ds(b * blk, blk), pl.ds(start, blk)]
                        else:
                            tile = sources[k].at[mine]
                        pltpu.make_async_copy(tile, tiles.at[(slot,) + place], tile_sem.at[slot]).start()

                    @pl.when(jnp.logical_not(there))
                    def _():
                        tiles[(slot,) + place] = jnp.zeros((blk, blk), tiles.dtype)

                    mine = mine + there.astype(jnp.int32)
                    started = started + there.astype(jnp.int32)
            following.append(mine)
        return tuple(following), started

    total[...] = jnp.zeros_like(total)
    first_used, first_started = fetch(0, 0, (jnp.int32(0),) * count, True)

    def one_step(i, carry):
        used, started = carry
        slot = lax.rem(i, 2)
        after_used, after_started = fetch(
            jnp.minimum(i + 1, steps - 1), 1 - slot, used, i + 1 < steps
        )

        def one_wait(_, nothing):
            tile = tiles.at[slot, pl.ds(0, blk), pl.ds(0, blk)]
            pltpu.make_async_copy(tile, tile, tile_sem.at[slot]).wait()
            return nothing

        lax.fori_loop(0, started, one_wait, 0)
        for g in range(groups):
            pltpu.make_async_copy(held.at[slot, g], held.at[slot, g], held_sem.at[slot]).wait()
        for k in range(count):
            block = tiles[slot, k * rows : (k + 1) * rows, :]
            for g in range(groups):
                total[g, k * rows : (k + 1) * rows, :] += jnp.dot(
                    block, held[slot, g], preferred_element_type=jnp.float32
                )
        return after_used, after_started

    lax.fori_loop(0, steps, one_step, (first_used, first_started))
    for k in range(count):
        place = pl.ds(pl.multiple_of(info[2 + k], rows), rows)
        for g in range(groups):
            out[g, :, place] = total[g, k * rows : (k + 1) * rows, :].T


def product(sources, masks, planes, inner, base, places):
    row_blocks, columns = masks[0].shape
    packed = [v.ndim == 3 for v in sources]
    blk = next(v.shape[1] if p else v.shape[0] // row_blocks for v, p in zip(sources, packed))
    rows = row_blocks * blk
    wide = planes[0][0].shape[1]
    dtype = sources[0].dtype
    head = [jnp.asarray(v, jnp.int32).reshape(1) for v in [inner, base] + list(places)]
    info = jnp.concatenate(head + [m.T.reshape(-1) for m in masks])
    flat = [v for choice in planes for v in choice]
    shape = (len(planes), wide, len(sources) * rows)
    flops = 2 * shape[0] * shape[1] * shape[2] * columns * blk
    size = columns * blk * (wide * len(planes) + rows * len(sources) // 2) * 2
    return pl.pallas_call(
        functools.partial(
            product_kernel, blk, row_blocks, columns // STRIDE,
            [v.shape[0] if p else None for v, p in zip(sources, packed)],
            [len(choice) - 1 for choice in planes],
        ),
        out_shape=jax.ShapeDtypeStruct(shape, jnp.float32),
        in_specs=[pl.BlockSpec(memory_space=pltpu.SMEM)]
        + [pl.BlockSpec(memory_space=pl.ANY)] * (len(sources) + len(flat)),
        out_specs=pl.BlockSpec(memory_space=pltpu.VMEM),
        scratch_shapes=[
            pltpu.VMEM((len(planes), len(sources) * rows, wide), jnp.float32),
            pltpu.VMEM((2, len(sources) * rows, STRIDE * blk), dtype),
            pltpu.VMEM((2, len(planes), STRIDE * blk, wide), dtype),
            pltpu.SemaphoreType.DMA((2,)),
            pltpu.SemaphoreType.DMA((2,)),
        ],
        compiler_params=params(vmem_limit_bytes=32 << 20),
        cost_estimate=pl.CostEstimate(flops=flops, bytes_accessed=size, transcendentals=0),
        name="tiles_times_planes",
    )(info, *sources, *flat)


def dots_kernel(blk, count, ids, early, late, out):
    groups, share = early.shape[1] - 1, late.shape[1] - 8
    flag = jnp.sum(late[:, share : share + 1, :blk], axis=0)
    rest = jnp.zeros((out.shape[1] - blk - 3, blk), jnp.float32)

    def one(k, carry):
        def side(which):
            place, start = ids[which, 0, k], pl.multiple_of(ids[which, 1, k] * blk, blk)
            held = [early[place, g, :, pl.ds(start, blk)] for g in range(groups + 1)]
            held.append(late[place, :share, pl.ds(start, blk)])
            order = [ids[which, 2 + g, k] for g in range(groups + 2)]
            picked = []
            for g in range(groups + 2):
                part = held[0]
                for s in range(1, groups + 2):
                    part = jnp.where(order[g] == s, held[s], part)
                picked.append(part)
            return jnp.concatenate(picked)

        left, right = side(0), side(1)
        out[k, :blk, :] = lax.dot_general(
            left, right, (((0,), (0,)), ((), ())),
            precision=lax.Precision.HIGHEST, preferred_element_type=jnp.float32,
        )
        squares = [jnp.sum(v * v, axis=0, keepdims=True) for v in (left, right)]
        out[k, blk:, :] = jnp.concatenate(squares + [flag, rest])
        return carry

    lax.fori_loop(0, count, one, 0)


def pair_dots(early, late, ids, blk):
    count = ids.shape[2]
    return pl.pallas_call(
        functools.partial(dots_kernel, blk, count),
        out_shape=jax.ShapeDtypeStruct((count, blk + 8, blk), jnp.float32),
        in_specs=[pl.BlockSpec(memory_space=pltpu.SMEM)] + [pl.BlockSpec(memory_space=pltpu.VMEM)] * 2,
        out_specs=pl.BlockSpec(memory_space=pltpu.VMEM),
        compiler_params=params(vmem_limit_bytes=48 << 20),
        name="pair_dots",
    )(ids, early, late)


def turn(count, k):
    return [(d, (d + k) % count) for d in range(count)]


def scatter_sum(values, axis, dim):
    count = lax.axis_size(axis)
    here = lax.axis_index(axis)
    piece = values.shape[dim] // count

    def part(owner):
        return lax.dynamic_slice_in_dim(values, owner * piece, piece, dim)

    total = part(here)
    for k in range(1, count):
        total = total + lax.ppermute(part((here + k) % count), axis, turn(count, k))
    return total


def after(values, arrived):
    return lax.optimization_barrier((values, arrived))[0]


class Lane:
    def __init__(self, arrived=None):
        self.arrived = arrived

    def send(self, values, axis, routes):
        if self.arrived is not None:
            values = after(values, self.arrived)
        self.arrived = [lax.ppermute(v, axis, route) for v, route in zip(values, routes)]
        return self.arrived


def along_line(block, inner):
    near = lax.ppermute(block, "z", NEAR)
    middle = lax.ppermute(block, "z", MIDDLE)
    far = lax.ppermute(near, "z", MIDDLE)
    out1 = lax.ppermute(middle, "z", OUTWARD)
    out2 = lax.ppermute(far, "z", OUTWARD)
    return [block, near, jnp.where(inner, middle, out1), jnp.where(inner, far, out2)]


def dense(hist, tile_mask, planes, pairs):
    sess, act = ("z", "x"), ("y", "core")
    rows, acts = hist.shape
    row_blocks, act_blocks = tile_mask.shape
    blk = rows // row_blocks
    masked = (
        hist.reshape(row_blocks, blk, act_blocks, blk)
        * (tile_mask != 0).astype(jnp.bfloat16)[:, None, :, None]
    ).reshape(rows, acts)
    partial_proj = jnp.dot(
        masked, lax.all_gather(planes, sess, axis=1, tiled=True), preferred_element_type=jnp.float32
    )
    proj = lax.psum_scatter(partial_proj, act, scatter_dimension=1, tiled=True)
    own_count = pairs.shape[0] // lax.axis_size(act)
    place = lax.axis_index(act) * own_count
    sq = lax.psum(jnp.sum(proj * proj, axis=1), act)
    blocks = lax.all_gather(proj, sess, axis=0, tiled=True).reshape(-1, blk, proj.shape[1])
    norms = lax.all_gather(sq, sess, axis=0, tiled=True).reshape(-1, blk)
    dots = jnp.einsum(
        "kuc,kvc->kuv", blocks[pairs[:, 0]], blocks[pairs[:, 1]], precision=lax.Precision.HIGHEST
    )
    dots = lax.psum_scatter(dots, act, scatter_dimension=0, tiled=True)
    own = lax.dynamic_slice_in_dim(pairs, place, own_count, 0)
    scale = lax.rsqrt(norms[own] / P_SIZE + 1e-06)
    return dots / P_SIZE * scale[:, 0, :, None] * scale[:, 1, None, :]


def body(hist, tile_mask, planes, pairs):
    rows, acts = hist.shape
    row_blocks, act_blocks = tile_mask.shape
    blk = rows // row_blocks
    own_planes = planes.shape[1]
    wide = lax.axis_size("x")
    x, z = lax.axis_index("x"), lax.axis_index("z")
    inner = jnp.logical_or(z == 1, z == 2)
    columns = act_blocks // wide
    tile_mask = (tile_mask != 0).astype(jnp.int32)

    lent = columns * LENT[0] // LENT[1] // STRIDE * STRIDE
    kept = columns - lent
    cuts = [0, (kept // 3 + STRIDE // 2) // STRIDE * STRIDE, kept, columns]
    widths = [b - a for a, b in zip(cuts[:-1], cuts[1:])]
    slots = [room(w * row_blocks) for w in widths]

    def mask_of(owner):
        return lax.dynamic_slice_in_dim(tile_mask, owner * columns, columns, 1)

    def over_x(make):
        return [lax.ppermute(make((x + k) % wide), "x", turn(wide, k)) for k in range(1, wide)]

    others = [(x + k) % wide for k in range(1, wide)]
    row_routes = [turn(wide, k) for k in range(1, wide)]

    def in_row_order(parts, dim):
        ordered = []
        for owner in range(wide):
            chosen = parts[0]
            for k in range(1, wide):
                chosen = jnp.where((x - owner) % wide == k, parts[k], chosen)
            ordered.append(chosen)
        return jnp.concatenate(ordered, axis=dim)

    def planes_of(owner, c):
        return lax.dynamic_slice_in_dim(planes, (owner * columns + cuts[c]) * blk, widths[c] * blk, 0)

    def packed(owner, c, later):
        mask = after(mask_of(owner)[:, cuts[c] : cuts[c + 1]], later)
        return pack(hist, mask, owner * columns + cuts[c], slots[c])

    over_x = Lane()
    both_masks = jnp.stack([tile_mask, lax.ppermute(tile_mask, "z", INWARD)])

    def both_of(owner):
        return lax.dynamic_slice_in_dim(both_masks, owner * columns, columns, 2)

    known = [both_of(x)] + [lax.ppermute(both_of(o), "x", r) for o, r in zip(others, row_routes)]
    listed = [pairs] + [lax.ppermute(pairs, "x", route) for route in row_routes]
    masks, guest_masks = [m[0] for m in known], [m[1][:, kept:] for m in known]
    groups = []
    for c in range(3):
        got = over_x.send([planes_of(o, c) for o in others], "x", row_routes)
        groups.append(in_row_order([planes_of(x, c)] + got, 1))
        if c == 0:
            over_x.arrived = got + known[1:] + listed[1:]
    tiles = [None] * 3
    for c in (0, 2, 1):
        tiles[c] = over_x.send([packed(o, c, groups[0]) for o in others], "x", row_routes)

    ends, middle = Lane(), Lane()
    near, mid, far = [], [], []
    for c in range(2):
        near += ends.send([groups[c]], "z", [NEAR])
        mid += middle.send([groups[c]], "z", [MIDDLE])
    inward, outward = Lane(near[1:]), Lane(near[1:])
    for c in range(2):
        far += middle.send([near[c]], "z", [MIDDLE])
    loans = inward.send([packed(x, 2, near[0])], "z", [INWARD])
    near += inward.send([groups[2]], "z", [INWARD])
    mid += middle.send([groups[2]], "z", [MIDDLE])
    far += middle.send([near[2]], "z", [MIDDLE])
    outer = [outward.send([v], "z", [OUTWARD])[0] for v in (mid[0], mid[1], far[1], far[0])]
    loans = loans + inward.send(tiles[2], "z", [INWARD] * len(others))
    over = jnp.int32(0)
    for c in range(3):
        for owner in range(wide):
            count = jnp.sum(tile_mask[:, owner * columns + cuts[c] : owner * columns + cuts[c + 1]])
            over = jnp.maximum(over, (count > slots[c]).astype(jnp.int32))
    row_places = [(x - k) % wide * rows for k in range(wide)]
    early_groups = [[[groups[c]], [near[c]], [mid[c], outer[c]]] for c in range(2)]
    last_group = [[[far[c], outer[3 - c]]] for c in range(2)]

    def times(c, sources, which, held, places):
        own = [masks[k][:, cuts[c] : cuts[c + 1]] for k in which]
        return product(sources, own, held, inner, x * columns + cuts[c], places)

    every = range(wide)
    part0 = times(0, [hist] + tiles[0], every, early_groups[0], row_places)
    part2 = times(2, [hist] + tiles[2], every, [[groups[2]], [near[2]], [mid[2]], [far[2]]], row_places)
    part1 = [times(1, [([hist] + tiles[1])[k]], [k], early_groups[1], [0]) for k in every]
    first_three = part0 + part2[:3] + in_row_order(part1, 2)
    end1 = times(1, [hist] + tiles[1], every, last_group[1], row_places)
    end0 = times(0, [hist] + tiles[0], every, last_group[0], row_places)
    last_one = end0 + (end1 + part2[3:])
    visitors = in_row_order(
        [
            product([t], [m], [[groups[2]], [mid[2]], [far[2]]], inner, 0, [0])
            for t, m in zip(loans, guest_masks)
        ],
        2,
    )

    def summed(totals):
        return scatter_sum(scatter_sum(scatter_sum(totals, "core", 1), "x", 1), "y", 1)

    first_three = summed(first_three)
    visitors = lax.ppermute(summed(visitors), "z", OUTWARD)
    early = first_three.at[1:].add(visitors[:2])
    early = jnp.stack(along_line(early, inner))
    last_one = summed(last_one)[0] + visitors[2]
    flags = jnp.full((8, last_one.shape[1]), over.astype(jnp.float32))
    late = jnp.stack(along_line(jnp.concatenate([last_one, flags]), inner))

    order = (x - jnp.arange(wide)) % wide
    all_pairs = jnp.stack(listed)[order].reshape(-1, 2).T
    plane_blocks = wide * row_blocks
    of_plane = all_pairs // plane_blocks
    places = jnp.moveaxis(jnp.asarray(PLACE)[of_plane], 2, 1)
    ids = jnp.concatenate(
        [jnp.asarray(PLACE)[z][of_plane][:, None], (all_pairs % plane_blocks)[:, None], places], axis=1
    )
    sums = pair_dots(early, late, ids, blk)
    high, cores = lax.axis_size("y"), lax.axis_size("core")
    sums = sums.reshape((wide, high, cores, -1) + sums.shape[1:])
    for axis, dim in (("core", 2), ("x", 0), ("y", 1)):
        sums = scatter_sum(sums, axis, dim)
    own = sums.reshape((-1,) + sums.shape[4:])
    scale = lax.rsqrt(own[:, blk : blk + 2] / P_SIZE + 1e-06)
    scores = own[:, :blk] / P_SIZE * scale[:, 0, :, None] * scale[:, 1, None, :]
    crowded = own[0, blk + 2, 0] > 0
    return lax.cond(crowded, lambda: dense(hist, tile_mask, planes, pairs), lambda: scores)


def solution(mesh):
    sess, act = mesh.shape["sess"], mesh.shape["act"]
    fine = Mesh(
        mesh.devices.reshape(DEPTH, sess // DEPTH, act // CORES, CORES), ("z", "x", "y", "core")
    )
    sess_axes, act_axes = ("z", "x"), ("y", "core")
    placed = (
        P(sess_axes, act_axes), P(sess_axes, act_axes), P(act_axes, sess_axes), P(sess_axes, None)
    )
    return jax.shard_map(
        body, mesh=fine, in_specs=placed, out_specs=P(sess_axes + act_axes, None, None), check_vma=False
    )
```

```python
import functools

import jax
import jax.numpy as jnp
import numpy as np
from jax import lax
from jax.experimental import pallas as pl
from jax.experimental.pallas import tpu as pltpu
from jax.sharding import Mesh, PartitionSpec as P

P_SIZE = 1024
DEPTH = 4
CORES = 2

NEAR = ((0, 1), (1, 0), (2, 3), (3, 2))
INWARD = ((0, 1), (3, 2))
OUTWARD = ((1, 0), (2, 3))
MIDDLE = ((1, 2), (2, 1))
SOURCE = np.array([[0, 1, 2, 3], [1, 0, 2, 3], [2, 3, 1, 0], [3, 2, 1, 0]], np.int32)
PLACE = np.argsort(SOURCE, axis=1).astype(np.int32)

LENT = (9, 32)


def bounds(total, parts):
    return [total * k // parts for k in range(parts + 1)]


def room(tiles):
    return min(tiles, -(-(tiles // 2 + int(2.6 * tiles**0.5)) // 2) * 2)


def params(**kwargs):
    return pltpu.CompilerParams(**kwargs)


def pack_kernel(blk, row_blocks, columns, slots, info, hist, out, sem):
    base = info[0]

    def one_column(c, used):
        start = pl.multiple_of((base + c) * blk, blk)
        for b in range(row_blocks):
            take = jnp.logical_and(info[1 + c * row_blocks + b] != 0, used < slots)

            @pl.when(take)
            def _():
                pltpu.make_async_copy(
                    hist.at[pl.ds(b * blk, blk), pl.ds(start, blk)], out.at[used], sem
                ).start()

            used = used + take.astype(jnp.int32)
        return used

    used = lax.fori_loop(0, columns, one_column, jnp.int32(0))

    def one_wait(_, carry):
        pltpu.make_async_copy(hist.at[pl.ds(0, blk), pl.ds(0, blk)], out.at[0], sem).wait()
        return carry

    lax.fori_loop(0, used, one_wait, 0)


def pack(hist, mask, base, slots):
    row_blocks, columns = mask.shape
    blk = hist.shape[0] // row_blocks
    info = jnp.concatenate([jnp.reshape(base, (1,)).astype(jnp.int32), mask.T.reshape(-1)])
    return pl.pallas_call(
        functools.partial(pack_kernel, blk, row_blocks, columns, slots),
        out_shape=jax.ShapeDtypeStruct((slots, blk, blk), hist.dtype),
        in_specs=[pl.BlockSpec(memory_space=pltpu.SMEM), pl.BlockSpec(memory_space=pl.ANY)],
        out_specs=pl.BlockSpec(memory_space=pltpu.VMEM),
        scratch_shapes=[pltpu.SemaphoreType.DMA],
        compiler_params=params(vmem_limit_bytes=32 << 20),
        cost_estimate=pl.CostEstimate(flops=0, bytes_accessed=2 * slots * blk * blk * 2, transcendentals=0),
        name="pack_tiles",
    )(info, hist)


STRIDE = 4


def product_kernel(blk, row_blocks, steps, slots, paired, info, *refs):
    count, groups = len(slots), len(paired)
    sources, refs = refs[:count], refs[count:]
    planes, at = [], 0
    for two in paired:
        planes.append(refs[at : at + 1 + two])
        at += 1 + two
    out, total, tiles, held, tile_sem, held_sem, own_sem = refs[at:]
    rows = row_blocks * blk
    depth = STRIDE * blk
    inner, base = info[0] != 0, info[1]
    per_source = steps * STRIDE * row_blocks

    def present(k, column, b):
        return info[2 + count + k * per_source + column * row_blocks + b] != 0

    def own_block(k, slot):
        return tiles.at[slot, pl.ds(k * rows, rows)]

    def fetch(i, slot, used, active):
        first = pl.multiple_of(i * depth, depth)
        for g, choice in enumerate(planes):
            for which, ref in enumerate(choice):
                wanted = active
                if len(choice) == 2:
                    wanted = jnp.logical_and(active, inner if which == 0 else jnp.logical_not(inner))

                @pl.when(wanted)
                def _():
                    pltpu.make_async_copy(ref.at[pl.ds(first, depth)], held.at[slot, g], held_sem.at[slot]).start()

        started = jnp.int32(0)
        following = []
        for k in range(count):
            mine = used[k]
            if slots[k] is None:
                start = pl.multiple_of((base + i * STRIDE) * blk, blk)

                @pl.when(active)
                def _():
                    pltpu.make_async_copy(
                        sources[k].at[:, pl.ds(start, depth)], own_block(k, slot), own_sem.at[slot]
                    ).start()

                following.append(mine)
                continue
            for j in range(STRIDE):
                column = i * STRIDE + j
                for b in range(row_blocks):
                    there = present(k, column, b)
                    there = jnp.logical_and(there, jnp.logical_and(active, mine < slots[k]))
                    place = (pl.ds(k * rows + b * blk, blk), pl.ds(j * blk, blk))

                    @pl.when(there)
                    def _():
                        pltpu.make_async_copy(sources[k].at[mine], tiles.at[(slot,) + place], tile_sem.at[slot]).start()

                    @pl.when(jnp.logical_not(there))
                    def _():
                        tiles[(slot,) + place] = jnp.zeros((blk, blk), tiles.dtype)

                    mine = mine + there.astype(jnp.int32)
                    started = started + there.astype(jnp.int32)
            following.append(mine)
        return tuple(following), started

    total[...] = jnp.zeros_like(total)
    first_used, first_started = fetch(0, 0, (jnp.int32(0),) * count, True)

    def one_step(i, carry):
        used, started = carry
        slot = lax.rem(i, 2)
        after_used, after_started = fetch(
            jnp.minimum(i + 1, steps - 1), 1 - slot, used, i + 1 < steps
        )

        def one_wait(_, nothing):
            tile = tiles.at[slot, pl.ds(0, blk), pl.ds(0, blk)]
            pltpu.make_async_copy(tile, tile, tile_sem.at[slot]).wait()
            return nothing

        lax.fori_loop(0, started, one_wait, 0)
        for k in range(count):
            if slots[k] is None:
                pltpu.make_async_copy(own_block(k, slot), own_block(k, slot), own_sem.at[slot]).wait()
                for j in range(STRIDE):
                    for b in range(row_blocks):

                        @pl.when(jnp.logical_not(present(k, i * STRIDE + j, b)))
                        def _():
                            place = (slot, pl.ds(k * rows + b * blk, blk), pl.ds(j * blk, blk))
                            tiles[place] = jnp.zeros((blk, blk), tiles.dtype)

        for g in range(groups):
            pltpu.make_async_copy(held.at[slot, g], held.at[slot, g], held_sem.at[slot]).wait()
        for k in range(count):
            block = tiles[slot, k * rows : (k + 1) * rows, :]
            for g in range(groups):
                total[g, k * rows : (k + 1) * rows, :] += jnp.dot(
                    block, held[slot, g], preferred_element_type=jnp.float32
                )
        return after_used, after_started

    lax.fori_loop(0, steps, one_step, (first_used, first_started))
    for k in range(count):
        place = pl.ds(pl.multiple_of(info[2 + k], rows), rows)
        for g in range(groups):
            out[g, :, place] = total[g, k * rows : (k + 1) * rows, :].T


def product(sources, masks, planes, inner, base, places):
    row_blocks, columns = masks[0].shape
    packed = [v.ndim == 3 for v in sources]
    blk = next(v.shape[1] if p else v.shape[0] // row_blocks for v, p in zip(sources, packed))
    rows = row_blocks * blk
    wide = planes[0][0].shape[1]
    dtype = sources[0].dtype
    head = [jnp.asarray(v, jnp.int32).reshape(1) for v in [inner, base] + list(places)]
    info = jnp.concatenate(head + [m.T.reshape(-1) for m in masks])
    flat = [v for choice in planes for v in choice]
    shape = (len(planes), wide, len(sources) * rows)
    flops = 2 * shape[0] * shape[1] * shape[2] * columns * blk
    size = columns * blk * (wide * len(planes) + rows * len(sources) // 2) * 2
    return pl.pallas_call(
        functools.partial(
            product_kernel, blk, row_blocks, columns // STRIDE,
            [v.shape[0] if p else None for v, p in zip(sources, packed)],
            [len(choice) - 1 for choice in planes],
        ),
        out_shape=jax.ShapeDtypeStruct(shape, jnp.float32),
        in_specs=[pl.BlockSpec(memory_space=pltpu.SMEM)]
        + [pl.BlockSpec(memory_space=pl.ANY)] * (len(sources) + len(flat)),
        out_specs=pl.BlockSpec(memory_space=pltpu.VMEM),
        scratch_shapes=[
            pltpu.VMEM((len(planes), len(sources) * rows, wide), jnp.float32),
            pltpu.VMEM((2, len(sources) * rows, STRIDE * blk), dtype),
            pltpu.VMEM((2, len(planes), STRIDE * blk, wide), dtype),
            pltpu.SemaphoreType.DMA((2,)),
            pltpu.SemaphoreType.DMA((2,)),
            pltpu.SemaphoreType.DMA((2,)),
        ],
        compiler_params=params(vmem_limit_bytes=32 << 20),
        cost_estimate=pl.CostEstimate(flops=flops, bytes_accessed=size, transcendentals=0),
        name="tiles_times_planes",
    )(info, *sources, *flat)


def dots_kernel(blk, count, ids, early, late, out):
    groups, share = early.shape[1] - 1, late.shape[1] - 8
    flag = jnp.sum(late[:, share : share + 1, :blk], axis=0)
    rest = jnp.zeros((out.shape[1] - blk - 3, blk), jnp.float32)

    def one(k, carry):
        def side(which):
            place, start = ids[which, 0, k], pl.multiple_of(ids[which, 1, k] * blk, blk)
            held = [early[place, g, :, pl.ds(start, blk)] for g in range(groups + 1)]
            held.append(late[place, :share, pl.ds(start, blk)])
            order = [ids[which, 2 + g, k] for g in range(groups + 2)]
            picked = []
            for g in range(groups + 2):
                part = held[0]
                for s in range(1, groups + 2):
                    part = jnp.where(order[g] == s, held[s], part)
                picked.append(part)
            return jnp.concatenate(picked)

        left, right = side(0), side(1)
        out[k, :blk, :] = lax.dot_general(
            left, right, (((0,), (0,)), ((), ())),
            precision=lax.Precision.HIGHEST, preferred_element_type=jnp.float32,
        )
        squares = [jnp.sum(v * v, axis=0, keepdims=True) for v in (left, right)]
        out[k, blk:, :] = jnp.concatenate(squares + [flag, rest])
        return carry

    lax.fori_loop(0, count, one, 0)


def pair_dots(early, late, ids, blk):
    count = ids.shape[2]
    return pl.pallas_call(
        functools.partial(dots_kernel, blk, count),
        out_shape=jax.ShapeDtypeStruct((count, blk + 8, blk), jnp.float32),
        in_specs=[pl.BlockSpec(memory_space=pltpu.SMEM)] + [pl.BlockSpec(memory_space=pltpu.VMEM)] * 2,
        out_specs=pl.BlockSpec(memory_space=pltpu.VMEM),
        compiler_params=params(vmem_limit_bytes=48 << 20),
        name="pair_dots",
    )(ids, early, late)


def turn(count, k):
    return [(d, (d + k) % count) for d in range(count)]


def scatter_sum(values, axis, dim):
    count = lax.axis_size(axis)
    here = lax.axis_index(axis)
    piece = values.shape[dim] // count

    def part(owner):
        return lax.dynamic_slice_in_dim(values, owner * piece, piece, dim)

    total = part(here)
    for k in range(1, count):
        total = total + lax.ppermute(part((here + k) % count), axis, turn(count, k))
    return total


def after(values, arrived):
    return lax.optimization_barrier((values, arrived))[0]


class Lane:
    def __init__(self, arrived=None):
        self.arrived = arrived

    def send(self, values, axis, routes):
        if self.arrived is not None:
            values = after(values, self.arrived)
        self.arrived = [lax.ppermute(v, axis, route) for v, route in zip(values, routes)]
        return self.arrived


def along_line(block, inner):
    near = lax.ppermute(block, "z", NEAR)
    middle = lax.ppermute(block, "z", MIDDLE)
    far = lax.ppermute(near, "z", MIDDLE)
    out1 = lax.ppermute(middle, "z", OUTWARD)
    out2 = lax.ppermute(far, "z", OUTWARD)
    return [block, near, jnp.where(inner, middle, out1), jnp.where(inner, far, out2)]


def dense(hist, tile_mask, planes, pairs):
    sess, act = ("z", "x"), ("y", "core")
    rows, acts = hist.shape
    row_blocks, act_blocks = tile_mask.shape
    blk = rows // row_blocks
    masked = (
        hist.reshape(row_blocks, blk, act_blocks, blk)
        * (tile_mask != 0).astype(jnp.bfloat16)[:, None, :, None]
    ).reshape(rows, acts)
    partial_proj = jnp.dot(
        masked, lax.all_gather(planes, sess, axis=1, tiled=True), preferred_element_type=jnp.float32
    )
    proj = lax.psum_scatter(partial_proj, act, scatter_dimension=1, tiled=True)
    own_count = pairs.shape[0] // lax.axis_size(act)
    place = lax.axis_index(act) * own_count
    sq = lax.psum(jnp.sum(proj * proj, axis=1), act)
    blocks = lax.all_gather(proj, sess, axis=0, tiled=True).reshape(-1, blk, proj.shape[1])
    norms = lax.all_gather(sq, sess, axis=0, tiled=True).reshape(-1, blk)
    dots = jnp.einsum(
        "kuc,kvc->kuv", blocks[pairs[:, 0]], blocks[pairs[:, 1]], precision=lax.Precision.HIGHEST
    )
    dots = lax.psum_scatter(dots, act, scatter_dimension=0, tiled=True)
    own = lax.dynamic_slice_in_dim(pairs, place, own_count, 0)
    scale = lax.rsqrt(norms[own] / P_SIZE + 1e-06)
    return dots / P_SIZE * scale[:, 0, :, None] * scale[:, 1, None, :]


def body(hist, tile_mask, planes, pairs):
    rows, acts = hist.shape
    row_blocks, act_blocks = tile_mask.shape
    blk = rows // row_blocks
    own_planes = planes.shape[1]
    wide = lax.axis_size("x")
    x, z = lax.axis_index("x"), lax.axis_index("z")
    inner = jnp.logical_or(z == 1, z == 2)
    columns = act_blocks // wide
    tile_mask = (tile_mask != 0).astype(jnp.int32)

    lent = columns * LENT[0] // LENT[1] // STRIDE * STRIDE
    kept = columns - lent
    cuts = [0, (kept // 3 + STRIDE // 2) // STRIDE * STRIDE, kept, columns]
    widths = [b - a for a, b in zip(cuts[:-1], cuts[1:])]
    slots = [room(w * row_blocks) for w in widths]

    def mask_of(owner):
        return lax.dynamic_slice_in_dim(tile_mask, owner * columns, columns, 1)

    def over_x(make):
        return [lax.ppermute(make((x + k) % wide), "x", turn(wide, k)) for k in range(1, wide)]

    others = [(x + k) % wide for k in range(1, wide)]
    row_routes = [turn(wide, k) for k in range(1, wide)]

    def in_row_order(parts, dim):
        ordered = []
        for owner in range(wide):
            chosen = parts[0]
            for k in range(1, wide):
                chosen = jnp.where((x - owner) % wide == k, parts[k], chosen)
            ordered.append(chosen)
        return jnp.concatenate(ordered, axis=dim)

    def planes_of(owner, c):
        return lax.dynamic_slice_in_dim(planes, (owner * columns + cuts[c]) * blk, widths[c] * blk, 0)

    def packed(owner, c, later):
        mask = after(mask_of(owner)[:, cuts[c] : cuts[c + 1]], later)
        return pack(hist, mask, owner * columns + cuts[c], slots[c])

    over_x = Lane()
    both_masks = jnp.stack([tile_mask, lax.ppermute(tile_mask, "z", INWARD)])

    def both_of(owner):
        return lax.dynamic_slice_in_dim(both_masks, owner * columns, columns, 2)

    known = [both_of(x)] + [lax.ppermute(both_of(o), "x", r) for o, r in zip(others, row_routes)]
    listed = [pairs] + [lax.ppermute(pairs, "x", route) for route in row_routes]
    masks, guest_masks = [m[0] for m in known], [m[1][:, kept:] for m in known]
    groups = []
    for c in range(3):
        got = over_x.send([planes_of(o, c) for o in others], "x", row_routes)
        groups.append(in_row_order([planes_of(x, c)] + got, 1))
        if c == 0:
            over_x.arrived = got + known[1:] + listed[1:]
    tiles = [None] * 3
    for c in (0, 2, 1):
        tiles[c] = over_x.send([packed(o, c, groups[0]) for o in others], "x", row_routes)

    ends, middle = Lane(), Lane()
    near, mid, far = [], [], []
    for c in range(2):
        near += ends.send([groups[c]], "z", [NEAR])
        mid += middle.send([groups[c]], "z", [MIDDLE])
    inward, outward = Lane(near[1:]), Lane(near[1:])
    for c in range(2):
        far += middle.send([near[c]], "z", [MIDDLE])
    loans = inward.send([packed(x, 2, near[0])], "z", [INWARD])
    near += inward.send([groups[2]], "z", [INWARD])
    mid += middle.send([groups[2]], "z", [MIDDLE])
    far += middle.send([near[2]], "z", [MIDDLE])
    outer = [outward.send([v], "z", [OUTWARD])[0] for v in mid[:2]]
    loans = loans + inward.send(tiles[2], "z", [INWARD] * len(others))
    over = jnp.int32(0)
    for c in range(3):
        for owner in range(wide):
            count = jnp.sum(tile_mask[:, owner * columns + cuts[c] : owner * columns + cuts[c + 1]])
            over = jnp.maximum(over, (count > slots[c]).astype(jnp.int32))
    row_places = [(x - k) % wide * rows for k in range(wide)]
    early_groups = [[[groups[c]], [near[c]], [mid[c], outer[c]]] for c in range(2)]

    def times(c, sources, which, held, places):
        own = [masks[k][:, cuts[c] : cuts[c + 1]] for k in which]
        return product(sources, own, held, inner, x * columns + cuts[c], places)

    every = range(wide)
    part0 = times(0, [hist] + tiles[0], every, early_groups[0], row_places)
    outer += outward.send([after(far[1], part0)], "z", [OUTWARD])
    part1 = [times(1, [hist], [0], early_groups[1], [0])]
    part2 = times(2, [hist] + tiles[2], every, [[groups[2]], [near[2]], [mid[2]]], row_places)
    guest = product([loans[0]], [guest_masks[0]], [[groups[2]], [mid[2]]], inner, 0, [0])
    outer += outward.send([after(far[0], [part1[0], part2, guest])], "z", [OUTWARD])
    part1 += [times(1, [tiles[1][k - 1]], [k], early_groups[1], [0]) for k in range(1, wide)]
    first_three = part0 + part2 + in_row_order(part1, 2)

    end2 = times(2, [hist] + tiles[2], every, [[far[2]]], row_places)
    end1 = times(1, [hist] + tiles[1], every, [[far[1], outer[2]]], row_places)
    end0 = times(0, [hist] + tiles[0], every, [[far[0], outer[3]]], row_places)
    last_one = end0 + (end1 + end2)
    guest = jnp.concatenate([guest, product([loans[0]], [guest_masks[0]], [[far[2]]], inner, 0, [0])])
    visitors = in_row_order(
        [guest]
        + [
            product([t], [m], [[groups[2]], [mid[2]], [far[2]]], inner, 0, [0])
            for t, m in zip(loans[1:], guest_masks[1:])
        ],
        2,
    )

    def summed(totals):
        return scatter_sum(scatter_sum(scatter_sum(totals, "core", 1), "x", 1), "y", 1)

    first_three = summed(first_three)
    visitors = lax.ppermute(summed(visitors), "z", OUTWARD)
    early = first_three.at[1:].add(visitors[:2])
    early = jnp.stack(along_line(early, inner))
    last_one = summed(last_one)[0] + visitors[2]
    flags = jnp.full((8, last_one.shape[1]), over.astype(jnp.float32))
    late = jnp.stack(along_line(jnp.concatenate([last_one, flags]), inner))

    order = (x - jnp.arange(wide)) % wide
    all_pairs = jnp.stack(listed)[order].reshape(-1, 2).T
    plane_blocks = wide * row_blocks
    of_plane = all_pairs // plane_blocks
    places = jnp.moveaxis(jnp.asarray(PLACE)[of_plane], 2, 1)
    ids = jnp.concatenate(
        [jnp.asarray(PLACE)[z][of_plane][:, None], (all_pairs % plane_blocks)[:, None], places], axis=1
    )
    sums = pair_dots(early, late, ids, blk)
    high, cores = lax.axis_size("y"), lax.axis_size("core")
    sums = sums.reshape((wide, high, cores, -1) + sums.shape[1:])
    for axis, dim in (("core", 2), ("x", 0), ("y", 1)):
        sums = scatter_sum(sums, axis, dim)
    own = sums.reshape((-1,) + sums.shape[4:])
    scale = lax.rsqrt(own[:, blk : blk + 2] / P_SIZE + 1e-06)
    scores = own[:, :blk] / P_SIZE * scale[:, 0, :, None] * scale[:, 1, None, :]
    crowded = own[0, blk + 2, 0] > 0
    return lax.cond(crowded, lambda: dense(hist, tile_mask, planes, pairs), lambda: scores)


def solution(mesh):
    sess, act = mesh.shape["sess"], mesh.shape["act"]
    fine = Mesh(
        mesh.devices.reshape(DEPTH, sess // DEPTH, act // CORES, CORES), ("z", "x", "y", "core")
    )
    sess_axes, act_axes = ("z", "x"), ("y", "core")
    placed = (
        P(sess_axes, act_axes), P(sess_axes, act_axes), P(act_axes, sess_axes), P(sess_axes, None)
    )
    return jax.shard_map(
        body, mesh=fine, in_specs=placed, out_specs=P(sess_axes + act_axes, None, None), check_vma=False
    )
```

```python
import functools

import jax
import jax.numpy as jnp
import numpy as np
from jax import lax
from jax.experimental import pallas as pl
from jax.experimental.pallas import tpu as pltpu
from jax.sharding import Mesh, PartitionSpec as P

P_SIZE = 1024
DEPTH = 4
CORES = 2

NEAR = ((0, 1), (1, 0), (2, 3), (3, 2))
INWARD = ((0, 1), (3, 2))
OUTWARD = ((1, 0), (2, 3))
MIDDLE = ((1, 2), (2, 1))
SOURCE = np.array([[0, 1, 2, 3], [1, 0, 2, 3], [2, 3, 1, 0], [3, 2, 1, 0]], np.int32)
PLACE = np.argsort(SOURCE, axis=1).astype(np.int32)

LENT = (5, 16)


def bounds(total, parts):
    return [total * k // parts for k in range(parts + 1)]


def room(tiles):
    return min(tiles, -(-(tiles // 2 + int(2.6 * tiles**0.5)) // 2) * 2)


def params(**kwargs):
    return pltpu.CompilerParams(**kwargs)


def pack_kernel(blk, row_blocks, columns, slots, info, hist, out, sem):
    base = info[0]

    def one_column(c, used):
        start = pl.multiple_of((base + c) * blk, blk)
        for b in range(row_blocks):
            take = jnp.logical_and(info[1 + c * row_blocks + b] != 0, used < slots)

            @pl.when(take)
            def _():
                pltpu.make_async_copy(
                    hist.at[pl.ds(b * blk, blk), pl.ds(start, blk)], out.at[used], sem
                ).start()

            used = used + take.astype(jnp.int32)
        return used

    used = lax.fori_loop(0, columns, one_column, jnp.int32(0))

    def one_wait(_, carry):
        pltpu.make_async_copy(hist.at[pl.ds(0, blk), pl.ds(0, blk)], out.at[0], sem).wait()
        return carry

    lax.fori_loop(0, used, one_wait, 0)


def pack(hist, mask, base, slots):
    row_blocks, columns = mask.shape
    blk = hist.shape[0] // row_blocks
    info = jnp.concatenate([jnp.reshape(base, (1,)).astype(jnp.int32), mask.T.reshape(-1)])
    return pl.pallas_call(
        functools.partial(pack_kernel, blk, row_blocks, columns, slots),
        out_shape=jax.ShapeDtypeStruct((slots, blk, blk), hist.dtype),
        in_specs=[pl.BlockSpec(memory_space=pltpu.SMEM), pl.BlockSpec(memory_space=pl.ANY)],
        out_specs=pl.BlockSpec(memory_space=pltpu.VMEM),
        scratch_shapes=[pltpu.SemaphoreType.DMA],
        compiler_params=params(vmem_limit_bytes=32 << 20),
        cost_estimate=pl.CostEstimate(flops=0, bytes_accessed=2 * slots * blk * blk * 2, transcendentals=0),
        name="pack_tiles",
    )(info, hist)


STRIDE = 8


def product_kernel(blk, row_blocks, steps, slots, paired, info, *refs):
    count, groups = len(slots), len(paired)
    sources, refs = refs[:count], refs[count:]
    planes, at = [], 0
    for two in paired:
        planes.append(refs[at : at + 1 + two])
        at += 1 + two
    out, total, work, own, packed, held, source_sem, held_sem = refs[at:]
    rows = row_blocks * blk
    depth = STRIDE * blk
    step_tiles = STRIDE * row_blocks
    inner, base = info[0] != 0, info[1]
    lists = 2 + count
    starts = lists + count * steps * step_tiles

    def landing(k, slot):
        return own.at[slot] if slots[k] is None else packed.at[slot, sum(v is not None for v in slots[:k])]

    def fetch(i, slot):
        first = pl.multiple_of(i * depth, depth)
        for g, choice in enumerate(planes):
            for which, ref in enumerate(choice):
                wanted = True if len(choice) == 1 else inner if which == 0 else jnp.logical_not(inner)

                @pl.when(wanted)
                def _():
                    pltpu.make_async_copy(ref.at[pl.ds(first, depth)], held.at[slot, g], held_sem.at[slot]).start()

        for k in range(count):
            if slots[k] is None:
                start = pl.multiple_of((base + i * STRIDE) * blk, blk)
                part = sources[k].at[:, pl.ds(start, depth)]
            else:
                part = sources[k].at[pl.ds(info[starts + k * steps + i], step_tiles)]
            pltpu.make_async_copy(part, landing(k, slot), source_sem.at[slot, k]).start()

    total[...] = jnp.zeros_like(total)
    fetch(0, 0)

    def one_step(i, nothing):
        slot = lax.rem(i, 2)

        @pl.when(i + 1 < steps)
        def _():
            fetch(i + 1, 1 - slot)

        for k in range(count):
            pltpu.make_async_copy(landing(k, slot), landing(k, slot), source_sem.at[slot, k]).wait()
            for j in range(STRIDE):
                for b in range(row_blocks):
                    found = info[lists + (k * steps + i) * step_tiles + j * row_blocks + b]
                    area = (pl.ds(b * blk, blk), pl.ds(j * blk, blk))
                    if slots[k] is None:
                        tile = own[(slot,) + area]
                    else:
                        tile = landing(k, slot)[jnp.maximum(found, 0)]
                    work[pl.ds(k * rows + b * blk, blk), pl.ds(j * blk, blk)] = jnp.where(
                        found >= 0, tile, jnp.zeros_like(tile)
                    )
        for g in range(groups):
            pltpu.make_async_copy(held.at[slot, g], held.at[slot, g], held_sem.at[slot]).wait()
        for k in range(count):
            block = work[k * rows : (k + 1) * rows, :]
            for g in range(groups):
                total[g, k * rows : (k + 1) * rows, :] += jnp.dot(
                    block, held[slot, g], preferred_element_type=jnp.float32
                )
        return nothing

    lax.fori_loop(0, steps, one_step, 0)
    for k in range(count):
        place = pl.ds(pl.multiple_of(info[2 + k], rows), rows)
        for g in range(groups):
            out[g, :, place] = total[g, k * rows : (k + 1) * rows, :].T


def places_of(mask, slots):
    steps = mask.shape[1] // STRIDE
    there = mask.T.reshape(steps, -1)
    size = there.shape[1]
    if slots is None:
        return there - 1, jnp.zeros((steps,), jnp.int32)
    before = jnp.cumsum(there.reshape(-1)).reshape(steps, size) - there
    first = jnp.minimum(before[:, 0], slots - size)
    found = jnp.where((there != 0) & (before < slots), before - first[:, None], -1)
    return found, first


def product(sources, masks, planes, inner, base, places):
    row_blocks, columns = masks[0].shape
    slots = [v.shape[0] if v.ndim == 3 else None for v in sources]
    blk = next(v.shape[1] if n is not None else v.shape[0] // row_blocks for v, n in zip(sources, slots))
    rows = row_blocks * blk
    wide = planes[0][0].shape[1]
    dtype = sources[0].dtype
    head = [jnp.asarray(v, jnp.int32).reshape(1) for v in [inner, base] + list(places)]
    found, first = zip(*[places_of(m, n) for m, n in zip(masks, slots)])
    info = jnp.concatenate(head + [v.reshape(-1) for v in found] + list(first)).astype(jnp.int32)
    flat = [v for choice in planes for v in choice]
    shape = (len(planes), wide, len(sources) * rows)
    flops = 2 * shape[0] * shape[1] * shape[2] * columns * blk
    size = columns * blk * (wide * len(planes) + rows * len(sources)) * 2
    lists = max(1, sum(n is not None for n in slots))
    return pl.pallas_call(
        functools.partial(
            product_kernel, blk, row_blocks, columns // STRIDE, slots, [len(choice) - 1 for choice in planes]
        ),
        out_shape=jax.ShapeDtypeStruct(shape, jnp.float32),
        in_specs=[pl.BlockSpec(memory_space=pltpu.SMEM)]
        + [pl.BlockSpec(memory_space=pl.ANY)] * (len(sources) + len(flat)),
        out_specs=pl.BlockSpec(memory_space=pltpu.VMEM),
        scratch_shapes=[
            pltpu.VMEM((len(planes), len(sources) * rows, wide), jnp.float32),
            pltpu.VMEM((len(sources) * rows, STRIDE * blk), dtype),
            pltpu.VMEM((2, rows, STRIDE * blk), dtype),
            pltpu.VMEM((2, lists, STRIDE * row_blocks, blk, blk), dtype),
            pltpu.VMEM((2, len(planes), STRIDE * blk, wide), dtype),
            pltpu.SemaphoreType.DMA((2, len(sources))),
            pltpu.SemaphoreType.DMA((2,)),
        ],
        compiler_params=params(vmem_limit_bytes=48 << 20),
        cost_estimate=pl.CostEstimate(flops=flops, bytes_accessed=size, transcendentals=0),
        name="tiles_times_planes",
    )(info, *sources, *flat)


def dots_kernel(blk, count, ids, early, late, out):
    groups, share = early.shape[1] - 1, late.shape[1] - 8
    flag = jnp.sum(late[:, share : share + 1, :blk], axis=0)
    rest = jnp.zeros((out.shape[1] - blk - 3, blk), jnp.float32)

    def one(k, carry):
        def side(which):
            place, start = ids[which, 0, k], pl.multiple_of(ids[which, 1, k] * blk, blk)
            held = [early[place, g, :, pl.ds(start, blk)] for g in range(groups + 1)]
            held.append(late[place, :share, pl.ds(start, blk)])
            order = [ids[which, 2 + g, k] for g in range(groups + 2)]
            picked = []
            for g in range(groups + 2):
                part = held[0]
                for s in range(1, groups + 2):
                    part = jnp.where(order[g] == s, held[s], part)
                picked.append(part)
            return jnp.concatenate(picked)

        left, right = side(0), side(1)
        out[k, :blk, :] = lax.dot_general(
            left, right, (((0,), (0,)), ((), ())),
            precision=lax.Precision.HIGHEST, preferred_element_type=jnp.float32,
        )
        squares = [jnp.sum(v * v, axis=0, keepdims=True) for v in (left, right)]
        out[k, blk:, :] = jnp.concatenate(squares + [flag, rest])
        return carry

    lax.fori_loop(0, count, one, 0)


def pair_dots(early, late, ids, blk):
    count = ids.shape[2]
    return pl.pallas_call(
        functools.partial(dots_kernel, blk, count),
        out_shape=jax.ShapeDtypeStruct((count, blk + 8, blk), jnp.float32),
        in_specs=[pl.BlockSpec(memory_space=pltpu.SMEM)] + [pl.BlockSpec(memory_space=pltpu.VMEM)] * 2,
        out_specs=pl.BlockSpec(memory_space=pltpu.VMEM),
        compiler_params=params(vmem_limit_bytes=48 << 20),
        name="pair_dots",
    )(ids, early, late)


def turn(count, k):
    return [(d, (d + k) % count) for d in range(count)]


def scatter_sum(values, axis, dim):
    count = lax.axis_size(axis)
    here = lax.axis_index(axis)
    piece = values.shape[dim] // count

    def part(owner):
        return lax.dynamic_slice_in_dim(values, owner * piece, piece, dim)

    total = part(here)
    for k in range(1, count):
        total = total + lax.ppermute(part((here + k) % count), axis, turn(count, k))
    return total


def after(values, arrived):
    return lax.optimization_barrier((values, arrived))[0]


class Lane:
    def __init__(self, arrived=None):
        self.arrived = arrived

    def send(self, values, axis, routes):
        if self.arrived is not None:
            values = after(values, self.arrived)
        self.arrived = [lax.ppermute(v, axis, route) for v, route in zip(values, routes)]
        return self.arrived


def dense(hist, tile_mask, planes, pairs):
    sess, act = ("z", "x"), ("y", "core")
    rows, acts = hist.shape
    row_blocks, act_blocks = tile_mask.shape
    blk = rows // row_blocks
    masked = (
        hist.reshape(row_blocks, blk, act_blocks, blk)
        * (tile_mask != 0).astype(jnp.bfloat16)[:, None, :, None]
    ).reshape(rows, acts)
    partial_proj = jnp.dot(
        masked, lax.all_gather(planes, sess, axis=1, tiled=True), preferred_element_type=jnp.float32
    )
    proj = lax.psum_scatter(partial_proj, act, scatter_dimension=1, tiled=True)
    own_count = pairs.shape[0] // lax.axis_size(act)
    place = lax.axis_index(act) * own_count
    sq = lax.psum(jnp.sum(proj * proj, axis=1), act)
    blocks = lax.all_gather(proj, sess, axis=0, tiled=True).reshape(-1, blk, proj.shape[1])
    norms = lax.all_gather(sq, sess, axis=0, tiled=True).reshape(-1, blk)
    dots = jnp.einsum(
        "kuc,kvc->kuv", blocks[pairs[:, 0]], blocks[pairs[:, 1]], precision=lax.Precision.HIGHEST
    )
    dots = lax.psum_scatter(dots, act, scatter_dimension=0, tiled=True)
    own = lax.dynamic_slice_in_dim(pairs, place, own_count, 0)
    scale = lax.rsqrt(norms[own] / P_SIZE + 1e-06)
    return dots / P_SIZE * scale[:, 0, :, None] * scale[:, 1, None, :]


def body(hist, tile_mask, planes, pairs):
    rows, acts = hist.shape
    row_blocks, act_blocks = tile_mask.shape
    blk = rows // row_blocks
    own_planes = planes.shape[1]
    wide = lax.axis_size("x")
    x, z = lax.axis_index("x"), lax.axis_index("z")
    inner = jnp.logical_or(z == 1, z == 2)
    columns = act_blocks // wide
    tile_mask = (tile_mask != 0).astype(jnp.int32)

    lent = columns * LENT[0] // LENT[1] // STRIDE * STRIDE
    kept = columns - lent
    cuts = [0, (kept // 3 + STRIDE // 2) // STRIDE * STRIDE, kept, columns]
    widths = [b - a for a, b in zip(cuts[:-1], cuts[1:])]
    slots = [room(w * row_blocks) for w in widths]

    def mask_of(owner):
        return lax.dynamic_slice_in_dim(tile_mask, owner * columns, columns, 1)

    def over_x(make):
        return [lax.ppermute(make((x + k) % wide), "x", turn(wide, k)) for k in range(1, wide)]

    others = [(x + k) % wide for k in range(1, wide)]
    row_routes = [turn(wide, k) for k in range(1, wide)]

    def in_row_order(parts, dim):
        ordered = []
        for owner in range(wide):
            chosen = parts[0]
            for k in range(1, wide):
                chosen = jnp.where((x - owner) % wide == k, parts[k], chosen)
            ordered.append(chosen)
        return jnp.concatenate(ordered, axis=dim)

    def planes_of(owner, c):
        return lax.dynamic_slice_in_dim(planes, (owner * columns + cuts[c]) * blk, widths[c] * blk, 0)

    def packed(owner, c, later):
        mask = after(mask_of(owner)[:, cuts[c] : cuts[c + 1]], later)
        return pack(hist, mask, owner * columns + cuts[c], slots[c])

    over_x = Lane()
    both_masks = jnp.stack([tile_mask, lax.ppermute(tile_mask, "z", INWARD)])

    def both_of(owner):
        return lax.dynamic_slice_in_dim(both_masks, owner * columns, columns, 2)

    known = [both_of(x)] + [lax.ppermute(both_of(o), "x", r) for o, r in zip(others, row_routes)]
    listed = [pairs] + [lax.ppermute(pairs, "x", route) for route in row_routes]
    masks, guest_masks = [m[0] for m in known], [m[1][:, kept:] for m in known]
    ends, middle = Lane(), Lane()
    near, mid, far, groups = [], [], [], []
    for c in range(3):
        if c == 2:
            over_x.arrived = over_x.arrived + near[:1]
        got = over_x.send([planes_of(o, c) for o in others], "x", row_routes)
        groups.append(in_row_order([planes_of(x, c)] + got, 1))
        if c == 0:
            over_x.arrived = got + known[1:] + listed[1:]
        if c < 2:
            near += ends.send([groups[c]], "z", [NEAR])
            mid += middle.send([groups[c]], "z", [MIDDLE])
    tiles = [None] * 3
    for c in (0, 2, 1):
        tiles[c] = over_x.send([packed(o, c, groups[0]) for o in others], "x", row_routes)

    inward, outward = Lane(near[1:]), Lane(near[1:])
    middle.arrived = mid[1:] + near[1:]
    far += middle.send([near[0]], "z", [MIDDLE])
    outer = outward.send([mid[0]], "z", [OUTWARD])
    middle.arrived = far + outer
    far += middle.send([near[1]], "z", [MIDDLE])
    outer += outward.send([mid[1]], "z", [OUTWARD])
    middle.arrived = far[1:] + outer[1:]
    near += inward.send([groups[2]], "z", [INWARD])
    loans = inward.send([packed(x, 2, near[0])], "z", [INWARD])
    far += middle.send([near[2]], "z", [MIDDLE])
    mid += middle.send([groups[2]], "z", [MIDDLE])

    over = jnp.int32(0)
    for c in range(3):
        for owner in range(wide):
            count = jnp.sum(tile_mask[:, owner * columns + cuts[c] : owner * columns + cuts[c + 1]])
            over = jnp.maximum(over, (count > slots[c]).astype(jnp.int32))
    row_places = [(x - k) % wide * rows for k in range(wide)]
    every = range(wide)

    def times(c, sources, which, held, places):
        own = [masks[k][:, cuts[c] : cuts[c + 1]] for k in which]
        return product(sources, own, held, inner, x * columns + cuts[c], places)

    early_groups = [[[groups[c]], [near[c]], [mid[c], outer[c]]] for c in range(2)]
    part0 = times(0, [hist] + tiles[0], every, early_groups[0], row_places)
    loans += inward.send([after(t, part0) for t in tiles[2]], "z", [INWARD] * len(others))
    outer += outward.send([far[1]], "z", [OUTWARD])
    part1 = [times(1, [hist], [0], early_groups[1], [0])]
    part2 = times(2, [hist] + tiles[2], every, [[groups[2]], [near[2]]], row_places)
    end2 = times(2, [hist] + tiles[2], every, [[far[2]]], row_places)
    outer += outward.send([after(far[0], [part1, part2, end2])], "z", [OUTWARD])
    part1 += [times(1, [tiles[1][k - 1]], [k], early_groups[1], [0]) for k in range(1, wide)]
    end1 = times(1, [hist] + tiles[1], every, [[far[1], outer[2]]], row_places)
    guests = in_row_order(
        [product([t], [m], [[groups[2]], [far[2]]], inner, 0, [0]) for t, m in zip(loans, guest_masks)], 2
    )
    part2 = jnp.concatenate([part2, times(2, [hist] + tiles[2], every, [[mid[2]]], row_places)])
    first_three = part0 + part2 + in_row_order(part1, 2)
    guests_mid = product(loans, guest_masks, [[mid[2]]], inner, 0, row_places)
    end0 = times(0, [hist] + tiles[0], every, [[far[0], outer[3]]], row_places)
    last_one = end0 + (end1 + end2)
    visitors = jnp.concatenate([guests[:1], guests_mid, guests[1:]])

    def summed(share):
        return scatter_sum(scatter_sum(scatter_sum(share, "core", 1), "x", 1), "y", 1)

    first_three, visitors, last_one = summed(first_three), summed(visitors), summed(last_one)

    def all_along_line(share, extra):
        near = lax.ppermute(share, "z", NEAR) + extra
        mid = lax.ppermute(share, "z", MIDDLE)
        far = lax.ppermute(near, "z", MIDDLE)
        out1 = lax.ppermute(mid, "z", OUTWARD)
        out2 = lax.ppermute(far, "z", OUTWARD)
        own = share + lax.ppermute(extra, "z", OUTWARD)
        return jnp.stack([own, near, jnp.where(inner, mid, out1), jnp.where(inner, far, out2)])

    early = all_along_line(first_three, jnp.concatenate([jnp.zeros_like(visitors[:1]), visitors[:2]]))
    flags = jnp.full((8, last_one.shape[2]), over.astype(jnp.float32))
    late = all_along_line(
        jnp.concatenate([last_one[0], flags]), jnp.concatenate([visitors[2], jnp.zeros_like(flags)])
    )

    order = (x - jnp.arange(wide)) % wide
    all_pairs = jnp.stack(listed)[order].reshape(-1, 2).T
    plane_blocks = wide * row_blocks
    of_plane = all_pairs // plane_blocks
    places = jnp.moveaxis(jnp.asarray(PLACE)[of_plane], 2, 1)
    ids = jnp.concatenate(
        [jnp.asarray(PLACE)[z][of_plane][:, None], (all_pairs % plane_blocks)[:, None], places], axis=1
    )
    sums = pair_dots(early, late, ids, blk)
    high, cores = lax.axis_size("y"), lax.axis_size("core")
    sums = sums.reshape((wide, high, cores, -1) + sums.shape[1:])
    for axis, dim in (("core", 2), ("x", 0), ("y", 1)):
        sums = scatter_sum(sums, axis, dim)
    own = sums.reshape((-1,) + sums.shape[4:])
    scale = lax.rsqrt(own[:, blk : blk + 2] / P_SIZE + 1e-06)
    scores = own[:, :blk] / P_SIZE * scale[:, 0, :, None] * scale[:, 1, None, :]
    crowded = own[0, blk + 2, 0] > 0
    return lax.cond(crowded, lambda: dense(hist, tile_mask, planes, pairs), lambda: scores)


def solution(mesh):
    sess, act = mesh.shape["sess"], mesh.shape["act"]
    fine = Mesh(
        mesh.devices.reshape(DEPTH, sess // DEPTH, act // CORES, CORES), ("z", "x", "y", "core")
    )
    sess_axes, act_axes = ("z", "x"), ("y", "core")
    placed = (
        P(sess_axes, act_axes), P(sess_axes, act_axes), P(act_axes, sess_axes), P(sess_axes, None)
    )
    return jax.shard_map(
        body, mesh=fine, in_specs=placed, out_specs=P(sess_axes + act_axes, None, None), check_vma=False
    )
```

```python
import functools

import jax
import jax.numpy as jnp
import numpy as np
from jax import lax
from jax.experimental import pallas as pl
from jax.experimental.pallas import tpu as pltpu
from jax.sharding import Mesh, PartitionSpec as P

P_SIZE = 1024
DEPTH = 4
CORES = 2

NEAR = ((0, 1), (1, 0), (2, 3), (3, 2))
INWARD = ((0, 1), (3, 2))
OUTWARD = ((1, 0), (2, 3))
MIDDLE = ((1, 2), (2, 1))
SOURCE = np.array([[0, 1, 2, 3], [1, 0, 2, 3], [2, 3, 1, 0], [3, 2, 1, 0]], np.int32)
PLACE = np.argsort(SOURCE, axis=1).astype(np.int32)

LENT = (5, 16)


def bounds(total, parts):
    return [total * k // parts for k in range(parts + 1)]


def room(tiles):
    return min(tiles, -(-(tiles // 2 + int(2.6 * tiles**0.5)) // 2) * 2)


def params(**kwargs):
    return pltpu.CompilerParams(**kwargs)


def pack_kernel(blk, row_blocks, columns, slots, info, hist, out, sem):
    base = info[0]

    def one_column(c, used):
        start = pl.multiple_of((base + c) * blk, blk)
        for b in range(row_blocks):
            take = jnp.logical_and(info[1 + c * row_blocks + b] != 0, used < slots)

            @pl.when(take)
            def _():
                pltpu.make_async_copy(
                    hist.at[pl.ds(b * blk, blk), pl.ds(start, blk)], out.at[used], sem
                ).start()

            used = used + take.astype(jnp.int32)
        return used

    used = lax.fori_loop(0, columns, one_column, jnp.int32(0))

    def one_wait(_, carry):
        pltpu.make_async_copy(hist.at[pl.ds(0, blk), pl.ds(0, blk)], out.at[0], sem).wait()
        return carry

    lax.fori_loop(0, used, one_wait, 0)


def pack(hist, mask, base, slots):
    row_blocks, columns = mask.shape
    blk = hist.shape[0] // row_blocks
    info = jnp.concatenate([jnp.reshape(base, (1,)).astype(jnp.int32), mask.T.reshape(-1)])
    return pl.pallas_call(
        functools.partial(pack_kernel, blk, row_blocks, columns, slots),
        out_shape=jax.ShapeDtypeStruct((slots, blk, blk), hist.dtype),
        in_specs=[pl.BlockSpec(memory_space=pltpu.SMEM), pl.BlockSpec(memory_space=pl.ANY)],
        out_specs=pl.BlockSpec(memory_space=pltpu.VMEM),
        scratch_shapes=[pltpu.SemaphoreType.DMA],
        compiler_params=params(vmem_limit_bytes=32 << 20),
        cost_estimate=pl.CostEstimate(flops=0, bytes_accessed=2 * slots * blk * blk * 2, transcendentals=0),
        name="pack_tiles",
    )(info, hist)


STRIDE = 8


def product_kernel(blk, row_blocks, steps, slots, paired, info, *refs):
    count, groups = len(slots), len(paired)
    sources, refs = refs[:count], refs[count:]
    planes, at = [], 0
    for two in paired:
        planes.append(refs[at : at + 1 + two])
        at += 1 + two
    out, total, work, own, packed, held, source_sem, held_sem = refs[at:]
    rows = row_blocks * blk
    depth = STRIDE * blk
    step_tiles = STRIDE * row_blocks
    inner, base = info[0] != 0, info[1]
    lists = 2 + count
    starts = lists + count * steps * step_tiles

    def landing(k, slot):
        return own.at[slot] if slots[k] is None else packed.at[slot, sum(v is not None for v in slots[:k])]

    def fetch(i, slot):
        first = pl.multiple_of(i * depth, depth)
        for g, choice in enumerate(planes):
            for which, ref in enumerate(choice):
                wanted = True if len(choice) == 1 else inner if which == 0 else jnp.logical_not(inner)

                @pl.when(wanted)
                def _():
                    pltpu.make_async_copy(ref.at[pl.ds(first, depth)], held.at[slot, g], held_sem.at[slot]).start()

        for k in range(count):
            if slots[k] is None:
                start = pl.multiple_of((base + i * STRIDE) * blk, blk)
                part = sources[k].at[:, pl.ds(start, depth)]
            else:
                part = sources[k].at[pl.ds(info[starts + k * steps + i], step_tiles)]
            pltpu.make_async_copy(part, landing(k, slot), source_sem.at[slot, k]).start()

    total[...] = jnp.zeros_like(total)
    fetch(0, 0)

    def one_step(i, nothing):
        slot = lax.rem(i, 2)

        @pl.when(i + 1 < steps)
        def _():
            fetch(i + 1, 1 - slot)

        for k in range(count):
            pltpu.make_async_copy(landing(k, slot), landing(k, slot), source_sem.at[slot, k]).wait()
            for j in range(STRIDE):
                for b in range(row_blocks):
                    found = info[lists + (k * steps + i) * step_tiles + j * row_blocks + b]
                    area = (pl.ds(b * blk, blk), pl.ds(j * blk, blk))
                    if slots[k] is None:
                        tile = own[(slot,) + area]
                    else:
                        tile = landing(k, slot)[jnp.maximum(found, 0)]
                    work[pl.ds(k * rows + b * blk, blk), pl.ds(j * blk, blk)] = jnp.where(
                        found >= 0, tile, jnp.zeros_like(tile)
                    )
        for g in range(groups):
            pltpu.make_async_copy(held.at[slot, g], held.at[slot, g], held_sem.at[slot]).wait()
        for k in range(count):
            block = work[k * rows : (k + 1) * rows, :]
            for g in range(groups):
                total[g, k * rows : (k + 1) * rows, :] += jnp.dot(
                    block, held[slot, g], preferred_element_type=jnp.float32
                )
        return nothing

    lax.fori_loop(0, steps, one_step, 0)
    for k in range(count):
        place = pl.ds(pl.multiple_of(info[2 + k], rows), rows)
        for g in range(groups):
            out[g, :, place] = total[g, k * rows : (k + 1) * rows, :].T


def places_of(mask, slots):
    steps = mask.shape[1] // STRIDE
    there = mask.T.reshape(steps, -1)
    size = there.shape[1]
    if slots is None:
        return there - 1, jnp.zeros((steps,), jnp.int32)
    before = jnp.cumsum(there.reshape(-1)).reshape(steps, size) - there
    first = jnp.minimum(before[:, 0], slots - size)
    found = jnp.where((there != 0) & (before < slots), before - first[:, None], -1)
    return found, first


def product(sources, masks, planes, inner, base, places):
    row_blocks, columns = masks[0].shape
    slots = [v.shape[0] if v.ndim == 3 else None for v in sources]
    blk = next(v.shape[1] if n is not None else v.shape[0] // row_blocks for v, n in zip(sources, slots))
    rows = row_blocks * blk
    wide = planes[0][0].shape[1]
    dtype = sources[0].dtype
    head = [jnp.asarray(v, jnp.int32).reshape(1) for v in [inner, base] + list(places)]
    found, first = zip(*[places_of(m, n) for m, n in zip(masks, slots)])
    info = jnp.concatenate(head + [v.reshape(-1) for v in found] + list(first)).astype(jnp.int32)
    flat = [v for choice in planes for v in choice]
    shape = (len(planes), wide, len(sources) * rows)
    flops = 2 * shape[0] * shape[1] * shape[2] * columns * blk
    size = columns * blk * (wide * len(planes) + rows * len(sources)) * 2
    lists = max(1, sum(n is not None for n in slots))
    return pl.pallas_call(
        functools.partial(
            product_kernel, blk, row_blocks, columns // STRIDE, slots, [len(choice) - 1 for choice in planes]
        ),
        out_shape=jax.ShapeDtypeStruct(shape, jnp.float32),
        in_specs=[pl.BlockSpec(memory_space=pltpu.SMEM)]
        + [pl.BlockSpec(memory_space=pl.ANY)] * (len(sources) + len(flat)),
        out_specs=pl.BlockSpec(memory_space=pltpu.VMEM),
        scratch_shapes=[
            pltpu.VMEM((len(planes), len(sources) * rows, wide), jnp.float32),
            pltpu.VMEM((len(sources) * rows, STRIDE * blk), dtype),
            pltpu.VMEM((2, rows, STRIDE * blk), dtype),
            pltpu.VMEM((2, lists, STRIDE * row_blocks, blk, blk), dtype),
            pltpu.VMEM((2, len(planes), STRIDE * blk, wide), dtype),
            pltpu.SemaphoreType.DMA((2, len(sources))),
            pltpu.SemaphoreType.DMA((2,)),
        ],
        compiler_params=params(vmem_limit_bytes=48 << 20),
        cost_estimate=pl.CostEstimate(flops=flops, bytes_accessed=size, transcendentals=0),
        name="tiles_times_planes",
    )(info, *sources, *flat)


def dots_kernel(blk, count, ids, early, late, out):
    groups, share = early.shape[1] - 1, late.shape[1] - 8
    flag = jnp.sum(late[:, share : share + 1, :blk], axis=0)
    rest = jnp.zeros((out.shape[1] - blk - 3, blk), jnp.float32)

    def one(k, carry):
        def side(which):
            place, start = ids[which, 0, k], pl.multiple_of(ids[which, 1, k] * blk, blk)
            held = [early[place, g, :, pl.ds(start, blk)] for g in range(groups + 1)]
            held.append(late[place, :share, pl.ds(start, blk)])
            order = [ids[which, 2 + g, k] for g in range(groups + 2)]
            picked = []
            for g in range(groups + 2):
                part = held[0]
                for s in range(1, groups + 2):
                    part = jnp.where(order[g] == s, held[s], part)
                picked.append(part)
            return jnp.concatenate(picked)

        left, right = side(0), side(1)
        out[k, :blk, :] = lax.dot_general(
            left, right, (((0,), (0,)), ((), ())),
            precision=lax.Precision.HIGHEST, preferred_element_type=jnp.float32,
        )
        squares = [jnp.sum(v * v, axis=0, keepdims=True) for v in (left, right)]
        out[k, blk:, :] = jnp.concatenate(squares + [flag, rest])
        return carry

    lax.fori_loop(0, count, one, 0)


def pair_dots(early, late, ids, blk):
    count = ids.shape[2]
    return pl.pallas_call(
        functools.partial(dots_kernel, blk, count),
        out_shape=jax.ShapeDtypeStruct((count, blk + 8, blk), jnp.float32),
        in_specs=[pl.BlockSpec(memory_space=pltpu.SMEM)] + [pl.BlockSpec(memory_space=pltpu.VMEM)] * 2,
        out_specs=pl.BlockSpec(memory_space=pltpu.VMEM),
        compiler_params=params(vmem_limit_bytes=48 << 20),
        name="pair_dots",
    )(ids, early, late)


def turn(count, k):
    return [(d, (d + k) % count) for d in range(count)]


def scatter_sum(values, axis, dim):
    count = lax.axis_size(axis)
    here = lax.axis_index(axis)
    piece = values.shape[dim] // count

    def part(owner):
        return lax.dynamic_slice_in_dim(values, owner * piece, piece, dim)

    total = part(here)
    for k in range(1, count):
        total = total + lax.ppermute(part((here + k) % count), axis, turn(count, k))
    return total


def after(values, arrived):
    return lax.optimization_barrier((values, arrived))[0]


class Lane:
    def __init__(self, arrived=None):
        self.arrived = arrived

    def send(self, values, axis, routes):
        if self.arrived is not None:
            values = after(values, self.arrived)
        self.arrived = [lax.ppermute(v, axis, route) for v, route in zip(values, routes)]
        return self.arrived


def dense(hist, tile_mask, planes, pairs):
    sess, act = ("z", "x"), ("y", "core")
    rows, acts = hist.shape
    row_blocks, act_blocks = tile_mask.shape
    blk = rows // row_blocks
    masked = (
        hist.reshape(row_blocks, blk, act_blocks, blk)
        * (tile_mask != 0).astype(jnp.bfloat16)[:, None, :, None]
    ).reshape(rows, acts)
    partial_proj = jnp.dot(
        masked, lax.all_gather(planes, sess, axis=1, tiled=True), preferred_element_type=jnp.float32
    )
    proj = lax.psum_scatter(partial_proj, act, scatter_dimension=1, tiled=True)
    own_count = pairs.shape[0] // lax.axis_size(act)
    place = lax.axis_index(act) * own_count
    sq = lax.psum(jnp.sum(proj * proj, axis=1), act)
    blocks = lax.all_gather(proj, sess, axis=0, tiled=True).reshape(-1, blk, proj.shape[1])
    norms = lax.all_gather(sq, sess, axis=0, tiled=True).reshape(-1, blk)
    dots = jnp.einsum(
        "kuc,kvc->kuv", blocks[pairs[:, 0]], blocks[pairs[:, 1]], precision=lax.Precision.HIGHEST
    )
    dots = lax.psum_scatter(dots, act, scatter_dimension=0, tiled=True)
    own = lax.dynamic_slice_in_dim(pairs, place, own_count, 0)
    scale = lax.rsqrt(norms[own] / P_SIZE + 1e-06)
    return dots / P_SIZE * scale[:, 0, :, None] * scale[:, 1, None, :]


def body(hist, tile_mask, planes, pairs):
    rows, acts = hist.shape
    row_blocks, act_blocks = tile_mask.shape
    blk = rows // row_blocks
    own_planes = planes.shape[1]
    wide = lax.axis_size("x")
    x, z = lax.axis_index("x"), lax.axis_index("z")
    inner = jnp.logical_or(z == 1, z == 2)
    columns = act_blocks // wide
    tile_mask = (tile_mask != 0).astype(jnp.int32)

    lent = columns * LENT[0] // LENT[1] // STRIDE * STRIDE
    kept = columns - lent
    cuts = [0, (kept // 3 + STRIDE // 2) // STRIDE * STRIDE, kept, columns]
    widths = [b - a for a, b in zip(cuts[:-1], cuts[1:])]
    slots = [room(w * row_blocks) for w in widths]

    def mask_of(owner):
        return lax.dynamic_slice_in_dim(tile_mask, owner * columns, columns, 1)

    def over_x(make):
        return [lax.ppermute(make((x + k) % wide), "x", turn(wide, k)) for k in range(1, wide)]

    others = [(x + k) % wide for k in range(1, wide)]
    row_routes = [turn(wide, k) for k in range(1, wide)]

    def in_row_order(parts, dim):
        ordered = []
        for owner in range(wide):
            chosen = parts[0]
            for k in range(1, wide):
                chosen = jnp.where((x - owner) % wide == k, parts[k], chosen)
            ordered.append(chosen)
        return jnp.concatenate(ordered, axis=dim)

    def planes_of(owner, c):
        return lax.dynamic_slice_in_dim(planes, (owner * columns + cuts[c]) * blk, widths[c] * blk, 0)

    def packed(owner, c, later):
        mask = after(mask_of(owner)[:, cuts[c] : cuts[c + 1]], later)
        return pack(hist, mask, owner * columns + cuts[c], slots[c])

    over_x = Lane()
    both_masks = jnp.stack([tile_mask, lax.ppermute(tile_mask, "z", INWARD)])

    def both_of(owner):
        return lax.dynamic_slice_in_dim(both_masks, owner * columns, columns, 2)

    known = [both_of(x)] + [lax.ppermute(both_of(o), "x", r) for o, r in zip(others, row_routes)]
    listed = [pairs] + [lax.ppermute(pairs, "x", route) for route in row_routes]
    masks, guest_masks = [m[0] for m in known], [m[1][:, kept:] for m in known]
    ends, middle = Lane(), Lane()
    near, mid, far, groups = [], [], [], []
    for c in range(3):
        if c == 2:
            over_x.arrived = over_x.arrived + near[:1]
        got = over_x.send([planes_of(o, c) for o in others], "x", row_routes)
        groups.append(in_row_order([planes_of(x, c)] + got, 1))
        if c == 0:
            over_x.arrived = got + known[1:] + listed[1:]
        if c < 2:
            near += ends.send([groups[c]], "z", [NEAR])
            mid += middle.send([groups[c]], "z", [MIDDLE])
    tiles = [None] * 3
    for c in (0, 2):
        tiles[c] = over_x.send([packed(o, c, groups[0]) for o in others], "x", row_routes)

    inward, outward = Lane(near[1:]), Lane(near[1:])
    middle.arrived = mid[1:] + near[1:]
    far += middle.send([near[0]], "z", [MIDDLE])
    outer = outward.send([mid[0]], "z", [OUTWARD])
    middle.arrived = far + outer
    far += middle.send([near[1]], "z", [MIDDLE])
    outer += outward.send([mid[1]], "z", [OUTWARD])
    middle.arrived = far[1:] + outer[1:]
    near += inward.send([groups[2]], "z", [INWARD])
    loans = inward.send([packed(x, 2, near[0])], "z", [INWARD])
    far += middle.send([near[2]], "z", [MIDDLE])
    mid += middle.send([groups[2]], "z", [MIDDLE])

    over = jnp.int32(0)
    for c in range(3):
        for owner in range(wide):
            count = jnp.sum(tile_mask[:, owner * columns + cuts[c] : owner * columns + cuts[c + 1]])
            over = jnp.maximum(over, (count > slots[c]).astype(jnp.int32))
    row_places = [(x - k) % wide * rows for k in range(wide)]
    every = range(wide)

    def times(c, sources, which, held, places):
        own = [masks[k][:, cuts[c] : cuts[c + 1]] for k in which]
        return product(sources, own, held, inner, x * columns + cuts[c], places)

    early_groups = [[[groups[c]], [near[c]], [mid[c], outer[c]]] for c in range(2)]
    part0 = times(0, [hist] + tiles[0], every, early_groups[0], row_places)
    tiles[1] = over_x.send([packed(o, 1, part0) for o in others], "x", row_routes)
    loans += inward.send(tiles[2], "z", [INWARD] * len(others))
    part2 = times(2, [hist] + tiles[2], every, [[groups[2]], [near[2]]], row_places)
    outer += outward.send([far[1]], "z", [OUTWARD])
    part1 = [times(1, [hist], [0], early_groups[1], [0])]
    outer += outward.send([after(far[0], part1)], "z", [OUTWARD])
    end2 = times(2, [hist] + tiles[2], every, [[far[2]]], row_places)
    inner_late = after(inner, [outer[2], part2, end2])
    part1 += [
        product(
            [tiles[1][k - 1]], [masks[k][:, cuts[1] : cuts[2]]], early_groups[1], inner_late, x * columns + cuts[1], [0]
        )
        for k in range(1, wide)
    ]
    end1 = times(1, [hist] + tiles[1], every, [[far[1], outer[2]]], row_places)
    guests = in_row_order(
        [product([t], [m], [[groups[2]], [far[2]]], inner, 0, [0]) for t, m in zip(loans, guest_masks)], 2
    )
    part2_mid = product(
        [hist] + tiles[2], [m[:, cuts[2] :] for m in masks], [[mid[2]]], after(inner, end1), x * columns + cuts[2],
        row_places,
    )
    part2 = jnp.concatenate([part2, part2_mid])
    first_three = part0 + part2 + in_row_order(part1, 2)
    guests_mid = product(loans, guest_masks, [[mid[2]]], after(inner, first_three), 0, row_places)
    visitors = jnp.concatenate([guests[:1], guests_mid, guests[1:]])

    first_three = scatter_sum(first_three, "core", 1)
    inner_last = after(inner, first_three)
    end0 = product(
        [hist] + tiles[0], [m[:, : cuts[1]] for m in masks], [[far[0], outer[3]]], inner_last, x * columns, row_places
    )
    last_one = end0 + (end1 + end2)
    first_three = scatter_sum(scatter_sum(first_three, "x", 1), "y", 1)
    visitors = scatter_sum(scatter_sum(scatter_sum(visitors, "core", 1), "x", 1), "y", 1)
    last_one = scatter_sum(scatter_sum(scatter_sum(last_one, "core", 1), "x", 1), "y", 1)

    def all_along_line(share, extra):
        near = lax.ppermute(share, "z", NEAR) + extra
        mid = lax.ppermute(share, "z", MIDDLE)
        far = lax.ppermute(near, "z", MIDDLE)
        out1 = lax.ppermute(mid, "z", OUTWARD)
        out2 = lax.ppermute(far, "z", OUTWARD)
        own = share + lax.ppermute(extra, "z", OUTWARD)
        return jnp.stack([own, near, jnp.where(inner, mid, out1), jnp.where(inner, far, out2)])

    early = all_along_line(first_three, jnp.concatenate([jnp.zeros_like(visitors[:1]), visitors[:2]]))
    flags = jnp.full((8, last_one.shape[2]), over.astype(jnp.float32))
    late = all_along_line(
        jnp.concatenate([last_one[0], flags]), jnp.concatenate([visitors[2], jnp.zeros_like(flags)])
    )

    order = (x - jnp.arange(wide)) % wide
    all_pairs = jnp.stack(listed)[order].reshape(-1, 2).T
    plane_blocks = wide * row_blocks
    of_plane = all_pairs // plane_blocks
    places = jnp.moveaxis(jnp.asarray(PLACE)[of_plane], 2, 1)
    ids = jnp.concatenate(
        [jnp.asarray(PLACE)[z][of_plane][:, None], (all_pairs % plane_blocks)[:, None], places], axis=1
    )
    sums = pair_dots(early, late, ids, blk)
    high, cores = lax.axis_size("y"), lax.axis_size("core")
    sums = sums.reshape((wide, high, cores, -1) + sums.shape[1:])
    for axis, dim in (("core", 2), ("x", 0), ("y", 1)):
        sums = scatter_sum(sums, axis, dim)
    own = sums.reshape((-1,) + sums.shape[4:])
    scale = lax.rsqrt(own[:, blk : blk + 2] / P_SIZE + 1e-06)
    scores = own[:, :blk] / P_SIZE * scale[:, 0, :, None] * scale[:, 1, None, :]
    crowded = own[0, blk + 2, 0] > 0
    return lax.cond(crowded, lambda: dense(hist, tile_mask, planes, pairs), lambda: scores)


def solution(mesh):
    sess, act = mesh.shape["sess"], mesh.shape["act"]
    fine = Mesh(
        mesh.devices.reshape(DEPTH, sess // DEPTH, act // CORES, CORES), ("z", "x", "y", "core")
    )
    sess_axes, act_axes = ("z", "x"), ("y", "core")
    placed = (
        P(sess_axes, act_axes), P(sess_axes, act_axes), P(act_axes, sess_axes), P(sess_axes, None)
    )
    return jax.shard_map(
        body, mesh=fine, in_specs=placed, out_specs=P(sess_axes + act_axes, None, None), check_vma=False
    )
```

```python
import functools

import jax
import jax.numpy as jnp
import numpy as np
from jax import lax
from jax.experimental import pallas as pl
from jax.experimental.pallas import tpu as pltpu
from jax.sharding import Mesh, PartitionSpec as P

P_SIZE = 1024
DEPTH = 4
CORES = 2

NEAR = ((0, 1), (1, 0), (2, 3), (3, 2))
INWARD = ((0, 1), (3, 2))
OUTWARD = ((1, 0), (2, 3))
MIDDLE = ((1, 2), (2, 1))
SOURCE = np.array([[0, 1, 2, 3], [1, 0, 2, 3], [2, 3, 1, 0], [3, 2, 1, 0]], np.int32)
PLACE = np.argsort(SOURCE, axis=1).astype(np.int32)

LENT = (9, 32)


def bounds(total, parts):
    return [total * k // parts for k in range(parts + 1)]


def room(tiles):
    return min(tiles, -(-(tiles // 2 + int(2.6 * tiles**0.5)) // 2) * 2)


def params(**kwargs):
    return pltpu.CompilerParams(**kwargs)


def pack_kernel(blk, row_blocks, columns, slots, info, hist, out, sem):
    base = info[0]

    def one_column(c, used):
        start = pl.multiple_of((base + c) * blk, blk)
        for b in range(row_blocks):
            take = jnp.logical_and(info[1 + c * row_blocks + b] != 0, used < slots)

            @pl.when(take)
            def _():
                pltpu.make_async_copy(
                    hist.at[pl.ds(b * blk, blk), pl.ds(start, blk)], out.at[used], sem
                ).start()

            used = used + take.astype(jnp.int32)
        return used

    used = lax.fori_loop(0, columns, one_column, jnp.int32(0))

    def one_wait(_, carry):
        pltpu.make_async_copy(hist.at[pl.ds(0, blk), pl.ds(0, blk)], out.at[0], sem).wait()
        return carry

    lax.fori_loop(0, used, one_wait, 0)


def pack(hist, mask, base, slots):
    row_blocks, columns = mask.shape
    blk = hist.shape[0] // row_blocks
    info = jnp.concatenate([jnp.reshape(base, (1,)).astype(jnp.int32), mask.T.reshape(-1)])
    return pl.pallas_call(
        functools.partial(pack_kernel, blk, row_blocks, columns, slots),
        out_shape=jax.ShapeDtypeStruct((slots, blk, blk), hist.dtype),
        in_specs=[pl.BlockSpec(memory_space=pltpu.SMEM), pl.BlockSpec(memory_space=pl.ANY)],
        out_specs=pl.BlockSpec(memory_space=pltpu.VMEM),
        scratch_shapes=[pltpu.SemaphoreType.DMA],
        compiler_params=params(vmem_limit_bytes=32 << 20),
        cost_estimate=pl.CostEstimate(flops=0, bytes_accessed=2 * slots * blk * blk * 2, transcendentals=0),
        name="pack_tiles",
    )(info, hist)


STRIDE = 4


def product_kernel(blk, row_blocks, steps, slots, paired, info, *refs):
    count, groups = len(slots), len(paired)
    sources, refs = refs[:count], refs[count:]
    planes, at = [], 0
    for two in paired:
        planes.append(refs[at : at + 1 + two])
        at += 1 + two
    out, total, tiles, held, tile_sem, held_sem, own_sem = refs[at:]
    rows = row_blocks * blk
    depth = STRIDE * blk
    inner, base = info[0] != 0, info[1]
    per_source = steps * STRIDE * row_blocks

    def present(k, column, b):
        return info[2 + count + k * per_source + column * row_blocks + b] != 0

    def own_block(k, slot):
        return tiles.at[slot, pl.ds(k * rows, rows)]

    def fetch(i, slot, used, active):
        first = pl.multiple_of(i * depth, depth)
        for g, choice in enumerate(planes):
            for which, ref in enumerate(choice):
                wanted = active
                if len(choice) == 2:
                    wanted = jnp.logical_and(active, inner if which == 0 else jnp.logical_not(inner))

                @pl.when(wanted)
                def _():
                    pltpu.make_async_copy(ref.at[pl.ds(first, depth)], held.at[slot, g], held_sem.at[slot]).start()

        started = jnp.int32(0)
        following = []
        for k in range(count):
            mine = used[k]
            if slots[k] is None:
                start = pl.multiple_of((base + i * STRIDE) * blk, blk)

                @pl.when(active)
                def _():
                    pltpu.make_async_copy(
                        sources[k].at[:, pl.ds(start, depth)], own_block(k, slot), own_sem.at[slot]
                    ).start()

                following.append(mine)
                continue
            for j in range(STRIDE):
                column = i * STRIDE + j
                for b in range(row_blocks):
                    there = present(k, column, b)
                    there = jnp.logical_and(there, jnp.logical_and(active, mine < slots[k]))
                    place = (pl.ds(k * rows + b * blk, blk), pl.ds(j * blk, blk))

                    @pl.when(there)
                    def _():
                        pltpu.make_async_copy(sources[k].at[mine], tiles.at[(slot,) + place], tile_sem.at[slot]).start()

                    @pl.when(jnp.logical_not(there))
                    def _():
                        tiles[(slot,) + place] = jnp.zeros((blk, blk), tiles.dtype)

                    mine = mine + there.astype(jnp.int32)
                    started = started + there.astype(jnp.int32)
            following.append(mine)
        return tuple(following), started

    total[...] = jnp.zeros_like(total)
    first_used, first_started = fetch(0, 0, (jnp.int32(0),) * count, True)

    def one_step(i, carry):
        used, started = carry
        slot = lax.rem(i, 2)
        after_used, after_started = fetch(
            jnp.minimum(i + 1, steps - 1), 1 - slot, used, i + 1 < steps
        )

        def one_wait(_, nothing):
            tile = tiles.at[slot, pl.ds(0, blk), pl.ds(0, blk)]
            pltpu.make_async_copy(tile, tile, tile_sem.at[slot]).wait()
            return nothing

        lax.fori_loop(0, started, one_wait, 0)
        for k in range(count):
            if slots[k] is None:
                pltpu.make_async_copy(own_block(k, slot), own_block(k, slot), own_sem.at[slot]).wait()
                for j in range(STRIDE):
                    for b in range(row_blocks):

                        @pl.when(jnp.logical_not(present(k, i * STRIDE + j, b)))
                        def _():
                            place = (slot, pl.ds(k * rows + b * blk, blk), pl.ds(j * blk, blk))
                            tiles[place] = jnp.zeros((blk, blk), tiles.dtype)

        for g in range(groups):
            pltpu.make_async_copy(held.at[slot, g], held.at[slot, g], held_sem.at[slot]).wait()
        for k in range(count):
            block = tiles[slot, k * rows : (k + 1) * rows, :]
            for g in range(groups):
                total[g, k * rows : (k + 1) * rows, :] += jnp.dot(
                    block, held[slot, g], preferred_element_type=jnp.float32
                )
        return after_used, after_started

    lax.fori_loop(0, steps, one_step, (first_used, first_started))
    for k in range(count):
        place = pl.ds(pl.multiple_of(info[2 + k], rows), rows)
        for g in range(groups):
            out[g, :, place] = total[g, k * rows : (k + 1) * rows, :].T


def product(sources, masks, planes, inner, base, places):
    row_blocks, columns = masks[0].shape
    packed = [v.ndim == 3 for v in sources]
    blk = next(v.shape[1] if p else v.shape[0] // row_blocks for v, p in zip(sources, packed))
    rows = row_blocks * blk
    wide = planes[0][0].shape[1]
    dtype = sources[0].dtype
    head = [jnp.asarray(v, jnp.int32).reshape(1) for v in [inner, base] + list(places)]
    info = jnp.concatenate(head + [m.T.reshape(-1) for m in masks])
    flat = [v for choice in planes for v in choice]
    shape = (len(planes), wide, len(sources) * rows)
    flops = 2 * shape[0] * shape[1] * shape[2] * columns * blk
    size = columns * blk * (wide * len(planes) + rows * len(sources) // 2) * 2
    return pl.pallas_call(
        functools.partial(
            product_kernel, blk, row_blocks, columns // STRIDE,
            [v.shape[0] if p else None for v, p in zip(sources, packed)],
            [len(choice) - 1 for choice in planes],
        ),
        out_shape=jax.ShapeDtypeStruct(shape, jnp.float32),
        in_specs=[pl.BlockSpec(memory_space=pltpu.SMEM)]
        + [pl.BlockSpec(memory_space=pl.ANY)] * (len(sources) + len(flat)),
        out_specs=pl.BlockSpec(memory_space=pltpu.VMEM),
        scratch_shapes=[
            pltpu.VMEM((len(planes), len(sources) * rows, wide), jnp.float32),
            pltpu.VMEM((2, len(sources) * rows, STRIDE * blk), dtype),
            pltpu.VMEM((2, len(planes), STRIDE * blk, wide), dtype),
            pltpu.SemaphoreType.DMA((2,)),
            pltpu.SemaphoreType.DMA((2,)),
            pltpu.SemaphoreType.DMA((2,)),
        ],
        compiler_params=params(vmem_limit_bytes=32 << 20),
        cost_estimate=pl.CostEstimate(flops=flops, bytes_accessed=size, transcendentals=0),
        name="tiles_times_planes",
    )(info, *sources, *flat)


def dots_kernel(blk, count, ids, early, late, out):
    groups, share = early.shape[1] - 1, late.shape[1] - 8
    flag = jnp.sum(late[:, share : share + 1, :blk], axis=0)
    rest = jnp.zeros((out.shape[1] - blk - 3, blk), jnp.float32)

    def one(k, carry):
        def side(which):
            place, start = ids[which, 0, k], pl.multiple_of(ids[which, 1, k] * blk, blk)
            held = [early[place, g, :, pl.ds(start, blk)] for g in range(groups + 1)]
            held.append(late[place, :share, pl.ds(start, blk)])
            order = [ids[which, 2 + g, k] for g in range(groups + 2)]
            picked = []
            for g in range(groups + 2):
                part = held[0]
                for s in range(1, groups + 2):
                    part = jnp.where(order[g] == s, held[s], part)
                picked.append(part)
            return jnp.concatenate(picked)

        left, right = side(0), side(1)
        out[k, :blk, :] = lax.dot_general(
            left, right, (((0,), (0,)), ((), ())),
            precision=lax.Precision.HIGHEST, preferred_element_type=jnp.float32,
        )
        squares = [jnp.sum(v * v, axis=0, keepdims=True) for v in (left, right)]
        out[k, blk:, :] = jnp.concatenate(squares + [flag, rest])
        return carry

    lax.fori_loop(0, count, one, 0)


def pair_dots(early, late, ids, blk):
    count = ids.shape[2]
    return pl.pallas_call(
        functools.partial(dots_kernel, blk, count),
        out_shape=jax.ShapeDtypeStruct((count, blk + 8, blk), jnp.float32),
        in_specs=[pl.BlockSpec(memory_space=pltpu.SMEM)] + [pl.BlockSpec(memory_space=pltpu.VMEM)] * 2,
        out_specs=pl.BlockSpec(memory_space=pltpu.VMEM),
        compiler_params=params(vmem_limit_bytes=48 << 20),
        name="pair_dots",
    )(ids, early, late)


def turn(count, k):
    return [(d, (d + k) % count) for d in range(count)]


def scatter_sum(values, axis, dim):
    count = lax.axis_size(axis)
    here = lax.axis_index(axis)
    piece = values.shape[dim] // count

    def part(owner):
        return lax.dynamic_slice_in_dim(values, owner * piece, piece, dim)

    total = part(here)
    for k in range(1, count):
        total = total + lax.ppermute(part((here + k) % count), axis, turn(count, k))
    return total


def after(values, arrived):
    return lax.optimization_barrier((values, arrived))[0]


class Lane:
    def __init__(self, arrived=None):
        self.arrived = arrived

    def send(self, values, axis, routes):
        if self.arrived is not None:
            values = after(values, self.arrived)
        self.arrived = [lax.ppermute(v, axis, route) for v, route in zip(values, routes)]
        return self.arrived


def along_line(block, inner):
    near = lax.ppermute(block, "z", NEAR)
    middle = lax.ppermute(block, "z", MIDDLE)
    far = lax.ppermute(near, "z", MIDDLE)
    out1 = lax.ppermute(middle, "z", OUTWARD)
    out2 = lax.ppermute(far, "z", OUTWARD)
    return [block, near, jnp.where(inner, middle, out1), jnp.where(inner, far, out2)]


def dense(hist, tile_mask, planes, pairs):
    sess, act = ("z", "x"), ("y", "core")
    rows, acts = hist.shape
    row_blocks, act_blocks = tile_mask.shape
    blk = rows // row_blocks
    masked = (
        hist.reshape(row_blocks, blk, act_blocks, blk)
        * (tile_mask != 0).astype(jnp.bfloat16)[:, None, :, None]
    ).reshape(rows, acts)
    partial_proj = jnp.dot(
        masked, lax.all_gather(planes, sess, axis=1, tiled=True), preferred_element_type=jnp.float32
    )
    proj = lax.psum_scatter(partial_proj, act, scatter_dimension=1, tiled=True)
    own_count = pairs.shape[0] // lax.axis_size(act)
    place = lax.axis_index(act) * own_count
    sq = lax.psum(jnp.sum(proj * proj, axis=1), act)
    blocks = lax.all_gather(proj, sess, axis=0, tiled=True).reshape(-1, blk, proj.shape[1])
    norms = lax.all_gather(sq, sess, axis=0, tiled=True).reshape(-1, blk)
    dots = jnp.einsum(
        "kuc,kvc->kuv", blocks[pairs[:, 0]], blocks[pairs[:, 1]], precision=lax.Precision.HIGHEST
    )
    dots = lax.psum_scatter(dots, act, scatter_dimension=0, tiled=True)
    own = lax.dynamic_slice_in_dim(pairs, place, own_count, 0)
    scale = lax.rsqrt(norms[own] / P_SIZE + 1e-06)
    return dots / P_SIZE * scale[:, 0, :, None] * scale[:, 1, None, :]


def body(hist, tile_mask, planes, pairs):
    rows, acts = hist.shape
    row_blocks, act_blocks = tile_mask.shape
    blk = rows // row_blocks
    own_planes = planes.shape[1]
    wide = lax.axis_size("x")
    x, z = lax.axis_index("x"), lax.axis_index("z")
    inner = jnp.logical_or(z == 1, z == 2)
    columns = act_blocks // wide
    tile_mask = (tile_mask != 0).astype(jnp.int32)

    lent = columns * LENT[0] // LENT[1] // STRIDE * STRIDE
    kept = columns - lent
    cuts = [0, (kept // 3 + STRIDE // 2) // STRIDE * STRIDE, kept, columns]
    widths = [b - a for a, b in zip(cuts[:-1], cuts[1:])]
    slots = [room(w * row_blocks) for w in widths]

    def mask_of(owner):
        return lax.dynamic_slice_in_dim(tile_mask, owner * columns, columns, 1)

    def over_x(make):
        return [lax.ppermute(make((x + k) % wide), "x", turn(wide, k)) for k in range(1, wide)]

    others = [(x + k) % wide for k in range(1, wide)]
    row_routes = [turn(wide, k) for k in range(1, wide)]

    def in_row_order(parts, dim):
        ordered = []
        for owner in range(wide):
            chosen = parts[0]
            for k in range(1, wide):
                chosen = jnp.where((x - owner) % wide == k, parts[k], chosen)
            ordered.append(chosen)
        return jnp.concatenate(ordered, axis=dim)

    def planes_of(owner, c):
        return lax.dynamic_slice_in_dim(planes, (owner * columns + cuts[c]) * blk, widths[c] * blk, 0)

    def packed(owner, c, later):
        mask = after(mask_of(owner)[:, cuts[c] : cuts[c + 1]], later)
        return pack(hist, mask, owner * columns + cuts[c], slots[c])

    over_x = Lane()
    both_masks = jnp.stack([tile_mask, lax.ppermute(tile_mask, "z", INWARD)])

    def both_of(owner):
        return lax.dynamic_slice_in_dim(both_masks, owner * columns, columns, 2)

    known = [both_of(x)] + [lax.ppermute(both_of(o), "x", r) for o, r in zip(others, row_routes)]
    listed = [pairs] + [lax.ppermute(pairs, "x", route) for route in row_routes]
    masks, guest_masks = [m[0] for m in known], [m[1][:, kept:] for m in known]
    ends, middle = Lane(), Lane()
    near, mid, far, groups = [], [], [], []
    for c in range(3):
        if c == 2:
            over_x.arrived = over_x.arrived + near[:1]
        got = over_x.send([planes_of(o, c) for o in others], "x", row_routes)
        groups.append(in_row_order([planes_of(x, c)] + got, 1))
        if c == 0:
            over_x.arrived = got + known[1:] + listed[1:]
        if c < 2:
            near += ends.send([groups[c]], "z", [NEAR])
            mid += middle.send([groups[c]], "z", [MIDDLE])
    tiles = [None] * 3
    for c in (0, 2, 1):
        tiles[c] = over_x.send([packed(o, c, groups[0]) for o in others], "x", row_routes)

    middle.arrived = mid[1:] + near[1:]
    inward, outward = Lane(near[1:]), Lane(near[1:])
    for c in range(2):
        far += middle.send([near[c]], "z", [MIDDLE])
    loans = inward.send([packed(x, 2, near[0])], "z", [INWARD])
    near += inward.send([groups[2]], "z", [INWARD])
    mid += middle.send([groups[2]], "z", [MIDDLE])
    far += middle.send([near[2]], "z", [MIDDLE])
    outer = [outward.send([v], "z", [OUTWARD])[0] for v in mid[:2]]
    loans = loans + inward.send(tiles[2], "z", [INWARD] * len(others))
    over = jnp.int32(0)
    for c in range(3):
        for owner in range(wide):
            count = jnp.sum(tile_mask[:, owner * columns + cuts[c] : owner * columns + cuts[c + 1]])
            over = jnp.maximum(over, (count > slots[c]).astype(jnp.int32))
    row_places = [(x - k) % wide * rows for k in range(wide)]
    early_groups = [[[groups[c]], [near[c]], [mid[c], outer[c]]] for c in range(2)]

    def times(c, sources, which, held, places):
        own = [masks[k][:, cuts[c] : cuts[c + 1]] for k in which]
        return product(sources, own, held, inner, x * columns + cuts[c], places)

    every = range(wide)
    part0 = times(0, [hist] + tiles[0], every, early_groups[0], row_places)
    outer += outward.send([after(far[1], part0)], "z", [OUTWARD])
    part1 = [times(1, [hist], [0], early_groups[1], [0])]
    part2 = times(2, [hist] + tiles[2], every, [[groups[2]], [near[2]], [mid[2]]], row_places)
    guest = product([loans[0]], [guest_masks[0]], [[groups[2]], [mid[2]]], inner, 0, [0])
    outer += outward.send([after(far[0], [part1[0], part2, guest])], "z", [OUTWARD])
    part1 += [times(1, [tiles[1][k - 1]], [k], early_groups[1], [0]) for k in range(1, wide)]
    first_three = part0 + part2 + in_row_order(part1, 2)

    def end(c, held, later):
        own = [m[:, cuts[c] : cuts[c + 1]] for m in masks]
        return product([hist] + tiles[c], own, [held], after(inner, later), x * columns + cuts[c], row_places)

    first_three = scatter_sum(first_three, "core", 1)
    guest = jnp.concatenate([guest, product([loans[0]], [guest_masks[0]], [[far[2]]], inner, 0, [0])])
    visitors = in_row_order(
        [guest]
        + [
            product([t], [m], [[groups[2]], [mid[2]], [far[2]]], inner, 0, [0])
            for t, m in zip(loans[1:], guest_masks[1:])
        ],
        2,
    )
    visitors = scatter_sum(visitors, "core", 1)
    end1 = end(1, [far[1], outer[2]], first_three)
    end2 = end(2, [far[2]], visitors)
    first_three = scatter_sum(first_three, "x", 1)
    end0 = end(0, [far[0], outer[3]], first_three)
    last_one = end0 + (end1 + end2)
    visitors = scatter_sum(visitors, "x", 1)
    first_three, visitors = scatter_sum(first_three, "y", 1), scatter_sum(visitors, "y", 1)
    last_one = scatter_sum(scatter_sum(scatter_sum(last_one, "core", 1), "x", 1), "y", 1)
    visitors = lax.ppermute(visitors, "z", OUTWARD)
    early = first_three.at[1:].add(visitors[:2])
    early = jnp.stack(along_line(early, inner))
    last_one = last_one[0] + visitors[2]
    flags = jnp.full((8, last_one.shape[1]), over.astype(jnp.float32))
    late = jnp.stack(along_line(jnp.concatenate([last_one, flags]), inner))

    order = (x - jnp.arange(wide)) % wide
    all_pairs = jnp.stack(listed)[order].reshape(-1, 2).T
    plane_blocks = wide * row_blocks
    of_plane = all_pairs // plane_blocks
    places = jnp.moveaxis(jnp.asarray(PLACE)[of_plane], 2, 1)
    ids = jnp.concatenate(
        [jnp.asarray(PLACE)[z][of_plane][:, None], (all_pairs % plane_blocks)[:, None], places], axis=1
    )
    sums = pair_dots(early, late, ids, blk)
    high, cores = lax.axis_size("y"), lax.axis_size("core")
    sums = sums.reshape((wide, high, cores, -1) + sums.shape[1:])
    for axis, dim in (("core", 2), ("x", 0), ("y", 1)):
        sums = scatter_sum(sums, axis, dim)
    own = sums.reshape((-1,) + sums.shape[4:])
    scale = lax.rsqrt(own[:, blk : blk + 2] / P_SIZE + 1e-06)
    scores = own[:, :blk] / P_SIZE * scale[:, 0, :, None] * scale[:, 1, None, :]
    crowded = own[0, blk + 2, 0] > 0
    return lax.cond(crowded, lambda: dense(hist, tile_mask, planes, pairs), lambda: scores)


def solution(mesh):
    sess, act = mesh.shape["sess"], mesh.shape["act"]
    fine = Mesh(
        mesh.devices.reshape(DEPTH, sess // DEPTH, act // CORES, CORES), ("z", "x", "y", "core")
    )
    sess_axes, act_axes = ("z", "x"), ("y", "core")
    placed = (
        P(sess_axes, act_axes), P(sess_axes, act_axes), P(act_axes, sess_axes), P(sess_axes, None)
    )
    return jax.shard_map(
        body, mesh=fine, in_specs=placed, out_specs=P(sess_axes + act_axes, None, None), check_vma=False
    )
```

```python
import functools

import jax
import jax.numpy as jnp
import numpy as np
from jax import lax
from jax.experimental import pallas as pl
from jax.experimental.pallas import tpu as pltpu
from jax.sharding import Mesh, PartitionSpec as P

P_SIZE = 1024
DEPTH = 4
CORES = 2

NEAR = ((0, 1), (1, 0), (2, 3), (3, 2))
INWARD = ((0, 1), (3, 2))
OUTWARD = ((1, 0), (2, 3))
MIDDLE = ((1, 2), (2, 1))
SOURCE = np.array([[0, 1, 2, 3], [1, 0, 2, 3], [2, 3, 1, 0], [3, 2, 1, 0]], np.int32)
PLACE = np.argsort(SOURCE, axis=1).astype(np.int32)

LENT = (9, 32)


def bounds(total, parts):
    return [total * k // parts for k in range(parts + 1)]


def room(tiles):
    return min(tiles, max(48, -(-(tiles // 2 + int(2.6 * tiles**0.5)) // 2) * 2))


def params(**kwargs):
    return pltpu.CompilerParams(**kwargs)


def pack_kernel(blk, row_blocks, columns, slots, info, hist, out, sem):
    base = info[0]

    def one_column(c, used):
        start = pl.multiple_of((base + c) * blk, blk)
        for b in range(row_blocks):
            take = jnp.logical_and(info[1 + c * row_blocks + b] != 0, used < slots)

            @pl.when(take)
            def _():
                pltpu.make_async_copy(
                    hist.at[pl.ds(b * blk, blk), pl.ds(start, blk)], out.at[used], sem
                ).start()

            used = used + take.astype(jnp.int32)
        return used

    used = lax.fori_loop(0, columns, one_column, jnp.int32(0))

    def one_wait(_, carry):
        pltpu.make_async_copy(hist.at[pl.ds(0, blk), pl.ds(0, blk)], out.at[0], sem).wait()
        return carry

    lax.fori_loop(0, used, one_wait, 0)


def pack(hist, mask, base, slots):
    row_blocks, columns = mask.shape
    blk = hist.shape[0] // row_blocks
    info = jnp.concatenate([jnp.reshape(base, (1,)).astype(jnp.int32), mask.T.reshape(-1)])
    return pl.pallas_call(
        functools.partial(pack_kernel, blk, row_blocks, columns, slots),
        out_shape=jax.ShapeDtypeStruct((slots, blk, blk), hist.dtype),
        in_specs=[pl.BlockSpec(memory_space=pltpu.SMEM), pl.BlockSpec(memory_space=pl.ANY)],
        out_specs=pl.BlockSpec(memory_space=pltpu.VMEM),
        scratch_shapes=[pltpu.SemaphoreType.DMA],
        compiler_params=params(vmem_limit_bytes=32 << 20),
        cost_estimate=pl.CostEstimate(flops=0, bytes_accessed=2 * slots * blk * blk * 2, transcendentals=0),
        name="pack_tiles",
    )(info, hist)


STRIDE = 4


def product_kernel(blk, row_blocks, stride, steps, slots, paired, info, *refs):
    count, groups = len(slots), len(paired)
    sources, refs = refs[:count], refs[count:]
    planes, at = [], 0
    for two in paired:
        planes.append(refs[at : at + 1 + two])
        at += 1 + two
    out, total, work, own, packed, held, source_sem, held_sem = refs[at:]
    rows = row_blocks * blk
    depth = stride * blk
    step_tiles = stride * row_blocks
    inner, base = info[0] != 0, info[1]
    lists = 2 + count
    starts = lists + count * steps * step_tiles

    def landing(k, slot):
        return own.at[slot] if slots[k] is None else packed.at[slot, sum(v is not None for v in slots[:k])]

    def fetch(i, slot):
        first = pl.multiple_of(i * depth, depth)
        for g, choice in enumerate(planes):
            for which, ref in enumerate(choice):
                wanted = True if len(choice) == 1 else inner if which == 0 else jnp.logical_not(inner)

                @pl.when(wanted)
                def _():
                    pltpu.make_async_copy(ref.at[pl.ds(first, depth)], held.at[slot, g], held_sem.at[slot]).start()

        for k in range(count):
            if slots[k] is None:
                start = pl.multiple_of((base + i * stride) * blk, blk)
                part = sources[k].at[:, pl.ds(start, depth)]
            else:
                part = sources[k].at[pl.ds(info[starts + k * steps + i], step_tiles)]
            pltpu.make_async_copy(part, landing(k, slot), source_sem.at[slot, k]).start()

    total[...] = jnp.zeros_like(total)
    fetch(0, 0)

    def one_step(i, nothing):
        slot = lax.rem(i, 2)

        @pl.when(i + 1 < steps)
        def _():
            fetch(i + 1, 1 - slot)

        for k in range(count):
            pltpu.make_async_copy(landing(k, slot), landing(k, slot), source_sem.at[slot, k]).wait()
            for j in range(stride):
                for b in range(row_blocks):
                    found = info[lists + (k * steps + i) * step_tiles + j * row_blocks + b]
                    area = (pl.ds(b * blk, blk), pl.ds(j * blk, blk))
                    if slots[k] is None:
                        tile = own[(slot,) + area]
                    else:
                        tile = landing(k, slot)[jnp.maximum(found, 0)]
                    work[pl.ds(k * rows + b * blk, blk), pl.ds(j * blk, blk)] = jnp.where(
                        found >= 0, tile, jnp.zeros_like(tile)
                    )
        for g in range(groups):
            pltpu.make_async_copy(held.at[slot, g], held.at[slot, g], held_sem.at[slot]).wait()
        for k in range(count):
            block = work[k * rows : (k + 1) * rows, :]
            for g in range(groups):
                total[g, k * rows : (k + 1) * rows, :] += jnp.dot(
                    block, held[slot, g], preferred_element_type=jnp.float32
                )
        return nothing

    lax.fori_loop(0, steps, one_step, 0)
    for k in range(count):
        place = pl.ds(pl.multiple_of(info[2 + k], rows), rows)
        for g in range(groups):
            out[g, :, place] = total[g, k * rows : (k + 1) * rows, :].T


def places_of(mask, slots, stride):
    steps = mask.shape[1] // stride
    there = mask.T.reshape(steps, -1)
    size = there.shape[1]
    if slots is None:
        return there - 1, jnp.zeros((steps,), jnp.int32)
    before = jnp.cumsum(there.reshape(-1)).reshape(steps, size) - there
    first = jnp.minimum(before[:, 0], slots - size)
    found = jnp.where((there != 0) & (before < slots), before - first[:, None], -1)
    return found, first


def product(sources, masks, planes, inner, base, places):
    row_blocks, columns = masks[0].shape
    slots = [v.shape[0] if v.ndim == 3 else None for v in sources]
    blk = next(v.shape[1] if n is not None else v.shape[0] // row_blocks for v, n in zip(sources, slots))
    stride = next(n for n in (3 * STRIDE, 2 * STRIDE, STRIDE) if columns % n == 0)
    rows = row_blocks * blk
    wide = planes[0][0].shape[1]
    dtype = sources[0].dtype
    head = [jnp.asarray(v, jnp.int32).reshape(1) for v in [inner, base] + list(places)]
    found, first = zip(*[places_of(m, n, stride) for m, n in zip(masks, slots)])
    info = jnp.concatenate(head + [v.reshape(-1) for v in found] + list(first)).astype(jnp.int32)
    flat = [v for choice in planes for v in choice]
    shape = (len(planes), wide, len(sources) * rows)
    flops = 2 * shape[0] * shape[1] * shape[2] * columns * blk
    size = columns * blk * (wide * len(planes) + rows * len(sources) // 2) * 2
    lists = max(1, sum(n is not None for n in slots))
    return pl.pallas_call(
        functools.partial(
            product_kernel, blk, row_blocks, stride, columns // stride, slots, [len(choice) - 1 for choice in planes]
        ),
        out_shape=jax.ShapeDtypeStruct(shape, jnp.float32),
        in_specs=[pl.BlockSpec(memory_space=pltpu.SMEM)]
        + [pl.BlockSpec(memory_space=pl.ANY)] * (len(sources) + len(flat)),
        out_specs=pl.BlockSpec(memory_space=pltpu.VMEM),
        scratch_shapes=[
            pltpu.VMEM((len(planes), len(sources) * rows, wide), jnp.float32),
            pltpu.VMEM((len(sources) * rows, stride * blk), dtype),
            pltpu.VMEM((2, rows, stride * blk), dtype),
            pltpu.VMEM((2, lists, stride * row_blocks, blk, blk), dtype),
            pltpu.VMEM((2, len(planes), stride * blk, wide), dtype),
            pltpu.SemaphoreType.DMA((2, len(sources))),
            pltpu.SemaphoreType.DMA((2,)),
        ],
        compiler_params=params(vmem_limit_bytes=48 << 20),
        cost_estimate=pl.CostEstimate(flops=flops, bytes_accessed=size, transcendentals=0),
        name="tiles_times_planes",
    )(info, *sources, *flat)


def dots_kernel(blk, count, ids, early, late, out):
    groups, share = early.shape[1] - 1, late.shape[1] - 8
    flag = jnp.sum(late[:, share : share + 1, :blk], axis=0)
    rest = jnp.zeros((out.shape[1] - blk - 3, blk), jnp.float32)

    def one(k, carry):
        def side(which):
            place, start = ids[which, 0, k], pl.multiple_of(ids[which, 1, k] * blk, blk)
            held = [early[place, g, :, pl.ds(start, blk)] for g in range(groups + 1)]
            held.append(late[place, :share, pl.ds(start, blk)])
            order = [ids[which, 2 + g, k] for g in range(groups + 2)]
            picked = []
            for g in range(groups + 2):
                part = held[0]
                for s in range(1, groups + 2):
                    part = jnp.where(order[g] == s, held[s], part)
                picked.append(part)
            return jnp.concatenate(picked)

        left, right = side(0), side(1)
        out[k, :blk, :] = lax.dot_general(
            left, right, (((0,), (0,)), ((), ())),
            precision=lax.Precision.HIGHEST, preferred_element_type=jnp.float32,
        )
        squares = [jnp.sum(v * v, axis=0, keepdims=True) for v in (left, right)]
        out[k, blk:, :] = jnp.concatenate(squares + [flag, rest])
        return carry

    lax.fori_loop(0, count, one, 0)


def pair_dots(early, late, ids, blk):
    count = ids.shape[2]
    return pl.pallas_call(
        functools.partial(dots_kernel, blk, count),
        out_shape=jax.ShapeDtypeStruct((count, blk + 8, blk), jnp.float32),
        in_specs=[pl.BlockSpec(memory_space=pltpu.SMEM)] + [pl.BlockSpec(memory_space=pltpu.VMEM)] * 2,
        out_specs=pl.BlockSpec(memory_space=pltpu.VMEM),
        compiler_params=params(vmem_limit_bytes=48 << 20),
        name="pair_dots",
    )(ids, early, late)


def turn(count, k):
    return [(d, (d + k) % count) for d in range(count)]


def scatter_sum(values, axis, dim):
    count = lax.axis_size(axis)
    here = lax.axis_index(axis)
    piece = values.shape[dim] // count

    def part(owner):
        return lax.dynamic_slice_in_dim(values, owner * piece, piece, dim)

    total = part(here)
    for k in range(1, count):
        total = total + lax.ppermute(part((here + k) % count), axis, turn(count, k))
    return total


def after(values, arrived):
    return lax.optimization_barrier((values, arrived))[0]


class Lane:
    def __init__(self, arrived=None):
        self.arrived = arrived

    def send(self, values, axis, routes):
        if self.arrived is not None:
            values = after(values, self.arrived)
        self.arrived = [lax.ppermute(v, axis, route) for v, route in zip(values, routes)]
        return self.arrived


def along_line(block, inner):
    near = lax.ppermute(block, "z", NEAR)
    middle = lax.ppermute(block, "z", MIDDLE)
    far = lax.ppermute(near, "z", MIDDLE)
    out1 = lax.ppermute(middle, "z", OUTWARD)
    out2 = lax.ppermute(far, "z", OUTWARD)
    return [block, near, jnp.where(inner, middle, out1), jnp.where(inner, far, out2)]


def dense(hist, tile_mask, planes, pairs):
    sess, act = ("z", "x"), ("y", "core")
    rows, acts = hist.shape
    row_blocks, act_blocks = tile_mask.shape
    blk = rows // row_blocks
    masked = (
        hist.reshape(row_blocks, blk, act_blocks, blk)
        * (tile_mask != 0).astype(jnp.bfloat16)[:, None, :, None]
    ).reshape(rows, acts)
    partial_proj = jnp.dot(
        masked, lax.all_gather(planes, sess, axis=1, tiled=True), preferred_element_type=jnp.float32
    )
    proj = lax.psum_scatter(partial_proj, act, scatter_dimension=1, tiled=True)
    own_count = pairs.shape[0] // lax.axis_size(act)
    place = lax.axis_index(act) * own_count
    sq = lax.psum(jnp.sum(proj * proj, axis=1), act)
    blocks = lax.all_gather(proj, sess, axis=0, tiled=True).reshape(-1, blk, proj.shape[1])
    norms = lax.all_gather(sq, sess, axis=0, tiled=True).reshape(-1, blk)
    dots = jnp.einsum(
        "kuc,kvc->kuv", blocks[pairs[:, 0]], blocks[pairs[:, 1]], precision=lax.Precision.HIGHEST
    )
    dots = lax.psum_scatter(dots, act, scatter_dimension=0, tiled=True)
    own = lax.dynamic_slice_in_dim(pairs, place, own_count, 0)
    scale = lax.rsqrt(norms[own] / P_SIZE + 1e-06)
    return dots / P_SIZE * scale[:, 0, :, None] * scale[:, 1, None, :]


def body(hist, tile_mask, planes, pairs):
    rows, acts = hist.shape
    row_blocks, act_blocks = tile_mask.shape
    blk = rows // row_blocks
    own_planes = planes.shape[1]
    wide = lax.axis_size("x")
    x, z = lax.axis_index("x"), lax.axis_index("z")
    inner = jnp.logical_or(z == 1, z == 2)
    columns = act_blocks // wide
    tile_mask = (tile_mask != 0).astype(jnp.int32)

    lent = columns * LENT[0] // LENT[1] // STRIDE * STRIDE
    kept = columns - lent
    cuts = [0, (kept // 3 + STRIDE // 2) // STRIDE * STRIDE, kept, columns]
    widths = [b - a for a, b in zip(cuts[:-1], cuts[1:])]
    slots = [room(w * row_blocks) for w in widths]

    def mask_of(owner):
        return lax.dynamic_slice_in_dim(tile_mask, owner * columns, columns, 1)

    def over_x(make):
        return [lax.ppermute(make((x + k) % wide), "x", turn(wide, k)) for k in range(1, wide)]

    others = [(x + k) % wide for k in range(1, wide)]
    row_routes = [turn(wide, k) for k in range(1, wide)]

    def in_row_order(parts, dim):
        ordered = []
        for owner in range(wide):
            chosen = parts[0]
            for k in range(1, wide):
                chosen = jnp.where((x - owner) % wide == k, parts[k], chosen)
            ordered.append(chosen)
        return jnp.concatenate(ordered, axis=dim)

    def planes_of(owner, c):
        return lax.dynamic_slice_in_dim(planes, (owner * columns + cuts[c]) * blk, widths[c] * blk, 0)

    def packed(owner, c, later):
        mask = after(mask_of(owner)[:, cuts[c] : cuts[c + 1]], later)
        return pack(hist, mask, owner * columns + cuts[c], slots[c])

    over_x = Lane()
    both_masks = jnp.stack([tile_mask, lax.ppermute(tile_mask, "z", INWARD)])

    def both_of(owner):
        return lax.dynamic_slice_in_dim(both_masks, owner * columns, columns, 2)

    known = [both_of(x)] + [lax.ppermute(both_of(o), "x", r) for o, r in zip(others, row_routes)]
    listed = [pairs] + [lax.ppermute(pairs, "x", route) for route in row_routes]
    masks, guest_masks = [m[0] for m in known], [m[1][:, kept:] for m in known]
    groups = []
    for c in range(3):
        got = over_x.send([planes_of(o, c) for o in others], "x", row_routes)
        groups.append(in_row_order([planes_of(x, c)] + got, 1))
        if c == 0:
            over_x.arrived = got + known[1:] + listed[1:]
    tiles = [None] * 3
    for c in (0, 2, 1):
        tiles[c] = over_x.send([packed(o, c, groups[0]) for o in others], "x", row_routes)

    ends, middle = Lane(), Lane()
    near, mid, far = [], [], []
    for c in range(2):
        near += ends.send([groups[c]], "z", [NEAR])
        mid += middle.send([groups[c]], "z", [MIDDLE])
    inward, outward = Lane(near[1:]), Lane(near[1:])
    for c in range(2):
        far += middle.send([near[c]], "z", [MIDDLE])
    loans = inward.send([packed(x, 2, near[0])], "z", [INWARD])
    near += inward.send([groups[2]], "z", [INWARD])
    mid += middle.send([groups[2]], "z", [MIDDLE])
    far += middle.send([near[2]], "z", [MIDDLE])
    outer = [outward.send([v], "z", [OUTWARD])[0] for v in mid[:2]]
    loans = loans + inward.send(tiles[2], "z", [INWARD] * len(others))
    over = jnp.int32(0)
    for c in range(3):
        for owner in range(wide):
            count = jnp.sum(tile_mask[:, owner * columns + cuts[c] : owner * columns + cuts[c + 1]])
            over = jnp.maximum(over, (count > slots[c]).astype(jnp.int32))
    row_places = [(x - k) % wide * rows for k in range(wide)]
    early_groups = [[[groups[c]], [near[c]], [mid[c], outer[c]]] for c in range(2)]

    def times(c, sources, which, held, places):
        own = [masks[k][:, cuts[c] : cuts[c + 1]] for k in which]
        return product(sources, own, held, inner, x * columns + cuts[c], places)

    every = range(wide)
    part0 = times(0, [hist] + tiles[0], every, early_groups[0], row_places)
    outer += outward.send([after(far[1], part0)], "z", [OUTWARD])
    part1 = [times(1, [hist], [0], early_groups[1], [0])]
    part2 = times(2, [hist] + tiles[2], every, [[groups[2]], [near[2]], [mid[2]]], row_places)
    guest = product([loans[0]], [guest_masks[0]], [[groups[2]], [mid[2]]], inner, 0, [0])
    outer += outward.send([after(far[0], [part1[0], part2, guest])], "z", [OUTWARD])
    part1 += [times(1, [tiles[1][k - 1]], [k], early_groups[1], [0]) for k in range(1, wide)]
    first_three = part0 + part2 + in_row_order(part1, 2)

    end2 = times(2, [hist] + tiles[2], every, [[far[2]]], row_places)
    end1 = times(1, [hist] + tiles[1], every, [[far[1], outer[2]]], row_places)
    end0 = times(0, [hist] + tiles[0], every, [[far[0], outer[3]]], row_places)
    last_one = end0 + (end1 + end2)
    guest = jnp.concatenate([guest, product([loans[0]], [guest_masks[0]], [[far[2]]], inner, 0, [0])])
    visitors = in_row_order(
        [guest]
        + [
            product([t], [m], [[groups[2]], [mid[2]], [far[2]]], inner, 0, [0])
            for t, m in zip(loans[1:], guest_masks[1:])
        ],
        2,
    )

    def summed(totals):
        return scatter_sum(scatter_sum(scatter_sum(totals, "core", 1), "x", 1), "y", 1)

    first_three = summed(first_three)
    visitors = lax.ppermute(summed(visitors), "z", OUTWARD)
    early = first_three.at[1:].add(visitors[:2])
    early = jnp.stack(along_line(early, inner))
    last_one = summed(last_one)[0] + visitors[2]
    flags = jnp.full((8, last_one.shape[1]), over.astype(jnp.float32))
    late = jnp.stack(along_line(jnp.concatenate([last_one, flags]), inner))

    order = (x - jnp.arange(wide)) % wide
    all_pairs = jnp.stack(listed)[order].reshape(-1, 2).T
    plane_blocks = wide * row_blocks
    of_plane = all_pairs // plane_blocks
    places = jnp.moveaxis(jnp.asarray(PLACE)[of_plane], 2, 1)
    ids = jnp.concatenate(
        [jnp.asarray(PLACE)[z][of_plane][:, None], (all_pairs % plane_blocks)[:, None], places], axis=1
    )
    sums = pair_dots(early, late, ids, blk)
    high, cores = lax.axis_size("y"), lax.axis_size("core")
    sums = sums.reshape((wide, high, cores, -1) + sums.shape[1:])
    sums = scatter_sum(sums, "core", 2)
    half = sums.shape[3] // 2
    by_x = scatter_sum(scatter_sum(sums[:, :, :, :half], "x", 0), "y", 1)
    by_y = scatter_sum(scatter_sum(sums[:, :, :, half:], "y", 1), "x", 0)
    sums = jnp.concatenate([by_x, by_y], axis=3)
    own = sums.reshape((-1,) + sums.shape[4:])
    scale = lax.rsqrt(own[:, blk : blk + 2] / P_SIZE + 1e-06)
    scores = own[:, :blk] / P_SIZE * scale[:, 0, :, None] * scale[:, 1, None, :]
    crowded = own[0, blk + 2, 0] > 0
    return lax.cond(crowded, lambda: dense(hist, tile_mask, planes, pairs), lambda: scores)


def solution(mesh):
    sess, act = mesh.shape["sess"], mesh.shape["act"]
    fine = Mesh(
        mesh.devices.reshape(DEPTH, sess // DEPTH, act // CORES, CORES), ("z", "x", "y", "core")
    )
    sess_axes, act_axes = ("z", "x"), ("y", "core")
    placed = (
        P(sess_axes, act_axes), P(sess_axes, act_axes), P(act_axes, sess_axes), P(sess_axes, None)
    )
    return jax.shard_map(
        body, mesh=fine, in_specs=placed, out_specs=P(sess_axes + act_axes, None, None), check_vma=False
    )
```

```python
import functools

import jax
import jax.numpy as jnp
import numpy as np
from jax import lax
from jax.experimental import pallas as pl
from jax.experimental.pallas import tpu as pltpu
from jax.sharding import Mesh, PartitionSpec as P

P_SIZE = 1024
DEPTH = 4
CORES = 2

NEAR = ((0, 1), (1, 0), (2, 3), (3, 2))
INWARD = ((0, 1), (3, 2))
OUTWARD = ((1, 0), (2, 3))
MIDDLE = ((1, 2), (2, 1))
SOURCE = np.array([[0, 1, 2, 3], [1, 0, 2, 3], [2, 3, 1, 0], [3, 2, 1, 0]], np.int32)
PLACE = np.argsort(SOURCE, axis=1).astype(np.int32)

LENT = (9, 32)


def bounds(total, parts):
    return [total * k // parts for k in range(parts + 1)]


def room(tiles):
    return min(tiles, max(48, -(-(tiles // 2 + int(2.6 * tiles**0.5)) // 2) * 2))


def params(**kwargs):
    return pltpu.CompilerParams(**kwargs)


def pack_kernel(blk, row_blocks, columns, slots, info, hist, out, sem):
    base = info[0]

    def one_column(c, used):
        start = pl.multiple_of((base + c) * blk, blk)
        for b in range(row_blocks):
            take = jnp.logical_and(info[1 + c * row_blocks + b] != 0, used < slots)

            @pl.when(take)
            def _():
                pltpu.make_async_copy(
                    hist.at[pl.ds(b * blk, blk), pl.ds(start, blk)], out.at[used], sem
                ).start()

            used = used + take.astype(jnp.int32)
        return used

    used = lax.fori_loop(0, columns, one_column, jnp.int32(0))

    def one_wait(_, carry):
        pltpu.make_async_copy(hist.at[pl.ds(0, blk), pl.ds(0, blk)], out.at[0], sem).wait()
        return carry

    lax.fori_loop(0, used, one_wait, 0)


def pack(hist, mask, base, slots):
    row_blocks, columns = mask.shape
    blk = hist.shape[0] // row_blocks
    info = jnp.concatenate([jnp.reshape(base, (1,)).astype(jnp.int32), mask.T.reshape(-1)])
    return pl.pallas_call(
        functools.partial(pack_kernel, blk, row_blocks, columns, slots),
        out_shape=jax.ShapeDtypeStruct((slots, blk, blk), hist.dtype),
        in_specs=[pl.BlockSpec(memory_space=pltpu.SMEM), pl.BlockSpec(memory_space=pl.ANY)],
        out_specs=pl.BlockSpec(memory_space=pltpu.VMEM),
        scratch_shapes=[pltpu.SemaphoreType.DMA],
        compiler_params=params(vmem_limit_bytes=32 << 20),
        cost_estimate=pl.CostEstimate(flops=0, bytes_accessed=2 * slots * blk * blk * 2, transcendentals=0),
        name="pack_tiles",
    )(info, hist)


STRIDE = 4


def product_kernel(blk, row_blocks, stride, steps, slots, paired, info, *refs):
    count, groups = len(slots), len(paired)
    sources, refs = refs[:count], refs[count:]
    planes, at = [], 0
    for two in paired:
        planes.append(refs[at : at + 1 + two])
        at += 1 + two
    out, total, work, own, packed, held, source_sem, held_sem = refs[at:]
    rows = row_blocks * blk
    depth = stride * blk
    step_tiles = stride * row_blocks
    inner, base = info[0] != 0, info[1]
    lists = 2 + count
    starts = lists + count * steps * step_tiles

    def landing(k, slot):
        return own.at[slot] if slots[k] is None else packed.at[slot, sum(v is not None for v in slots[:k])]

    def fetch(i, slot):
        first = pl.multiple_of(i * depth, depth)
        for g, choice in enumerate(planes):
            for which, ref in enumerate(choice):
                wanted = True if len(choice) == 1 else inner if which == 0 else jnp.logical_not(inner)

                @pl.when(wanted)
                def _():
                    pltpu.make_async_copy(ref.at[pl.ds(first, depth)], held.at[slot, g], held_sem.at[slot]).start()

        for k in range(count):
            if slots[k] is None:
                start = pl.multiple_of((base + i * stride) * blk, blk)
                part = sources[k].at[:, pl.ds(start, depth)]
            else:
                part = sources[k].at[pl.ds(info[starts + k * steps + i], step_tiles)]
            pltpu.make_async_copy(part, landing(k, slot), source_sem.at[slot, k]).start()

    total[...] = jnp.zeros_like(total)
    fetch(0, 0)

    def one_step(i, nothing):
        slot = lax.rem(i, 2)

        @pl.when(i + 1 < steps)
        def _():
            fetch(i + 1, 1 - slot)

        for k in range(count):
            pltpu.make_async_copy(landing(k, slot), landing(k, slot), source_sem.at[slot, k]).wait()
            for j in range(stride):
                for b in range(row_blocks):
                    found = info[lists + (k * steps + i) * step_tiles + j * row_blocks + b]
                    area = (pl.ds(b * blk, blk), pl.ds(j * blk, blk))
                    if slots[k] is None:
                        tile = own[(slot,) + area]
                    else:
                        tile = landing(k, slot)[jnp.maximum(found, 0)]
                    work[pl.ds(k * rows + b * blk, blk), pl.ds(j * blk, blk)] = jnp.where(
                        found >= 0, tile, jnp.zeros_like(tile)
                    )
        for g in range(groups):
            pltpu.make_async_copy(held.at[slot, g], held.at[slot, g], held_sem.at[slot]).wait()
        for k in range(count):
            block = work[k * rows : (k + 1) * rows, :]
            for g in range(groups):
                total[g, k * rows : (k + 1) * rows, :] += jnp.dot(
                    block, held[slot, g], preferred_element_type=jnp.float32
                )
        return nothing

    lax.fori_loop(0, steps, one_step, 0)
    for k in range(count):
        place = pl.ds(pl.multiple_of(info[2 + k], rows), rows)
        for g in range(groups):
            out[g, :, place] = total[g, k * rows : (k + 1) * rows, :].T


def places_of(mask, slots, stride):
    steps = mask.shape[1] // stride
    there = mask.T.reshape(steps, -1)
    size = there.shape[1]
    if slots is None:
        return there - 1, jnp.zeros((steps,), jnp.int32)
    before = jnp.cumsum(there.reshape(-1)).reshape(steps, size) - there
    first = jnp.minimum(before[:, 0], slots - size)
    found = jnp.where((there != 0) & (before < slots), before - first[:, None], -1)
    return found, first


def product(sources, masks, planes, inner, base, places):
    row_blocks, columns = masks[0].shape
    slots = [v.shape[0] if v.ndim == 3 else None for v in sources]
    blk = next(v.shape[1] if n is not None else v.shape[0] // row_blocks for v, n in zip(sources, slots))
    stride = next(n for n in (3 * STRIDE, 2 * STRIDE, STRIDE) if columns % n == 0)
    rows = row_blocks * blk
    wide = planes[0][0].shape[1]
    dtype = sources[0].dtype
    head = [jnp.asarray(v, jnp.int32).reshape(1) for v in [inner, base] + list(places)]
    found, first = zip(*[places_of(m, n, stride) for m, n in zip(masks, slots)])
    info = jnp.concatenate(head + [v.reshape(-1) for v in found] + list(first)).astype(jnp.int32)
    flat = [v for choice in planes for v in choice]
    shape = (len(planes), wide, len(sources) * rows)
    flops = 2 * shape[0] * shape[1] * shape[2] * columns * blk
    size = columns * blk * (wide * len(planes) + rows * len(sources) // 2) * 2
    lists = max(1, sum(n is not None for n in slots))
    return pl.pallas_call(
        functools.partial(
            product_kernel, blk, row_blocks, stride, columns // stride, slots, [len(choice) - 1 for choice in planes]
        ),
        out_shape=jax.ShapeDtypeStruct(shape, jnp.float32),
        in_specs=[pl.BlockSpec(memory_space=pltpu.SMEM)]
        + [pl.BlockSpec(memory_space=pl.ANY)] * (len(sources) + len(flat)),
        out_specs=pl.BlockSpec(memory_space=pltpu.VMEM),
        scratch_shapes=[
            pltpu.VMEM((len(planes), len(sources) * rows, wide), jnp.float32),
            pltpu.VMEM((len(sources) * rows, stride * blk), dtype),
            pltpu.VMEM((2, rows, stride * blk), dtype),
            pltpu.VMEM((2, lists, stride * row_blocks, blk, blk), dtype),
            pltpu.VMEM((2, len(planes), stride * blk, wide), dtype),
            pltpu.SemaphoreType.DMA((2, len(sources))),
            pltpu.SemaphoreType.DMA((2,)),
        ],
        compiler_params=params(vmem_limit_bytes=48 << 20),
        cost_estimate=pl.CostEstimate(flops=flops, bytes_accessed=size, transcendentals=0),
        name="tiles_times_planes",
    )(info, *sources, *flat)


def dots_kernel(blk, count, ids, early, late, out):
    groups, share = early.shape[1] - 1, late.shape[1] - 8
    flag = jnp.sum(late[:, share : share + 1, :blk], axis=0)
    rest = jnp.zeros((out.shape[1] - blk - 3, blk), jnp.float32)

    def one(k, carry):
        def side(which):
            place, start = ids[which, 0, k], pl.multiple_of(ids[which, 1, k] * blk, blk)
            held = [early[place, g, :, pl.ds(start, blk)] for g in range(groups + 1)]
            held.append(late[place, :share, pl.ds(start, blk)])
            order = [ids[which, 2 + g, k] for g in range(groups + 2)]
            picked = []
            for g in range(groups + 2):
                part = held[0]
                for s in range(1, groups + 2):
                    part = jnp.where(order[g] == s, held[s], part)
                picked.append(part)
            return jnp.concatenate(picked)

        left, right = side(0), side(1)
        out[k, :blk, :] = lax.dot_general(
            left, right, (((0,), (0,)), ((), ())),
            precision=lax.Precision.HIGHEST, preferred_element_type=jnp.float32,
        )
        squares = [jnp.sum(v * v, axis=0, keepdims=True) for v in (left, right)]
        out[k, blk:, :] = jnp.concatenate(squares + [flag, rest])
        return carry

    lax.fori_loop(0, count, one, 0)


def pair_dots(early, late, ids, blk):
    count = ids.shape[2]
    return pl.pallas_call(
        functools.partial(dots_kernel, blk, count),
        out_shape=jax.ShapeDtypeStruct((count, blk + 8, blk), jnp.float32),
        in_specs=[pl.BlockSpec(memory_space=pltpu.SMEM)] + [pl.BlockSpec(memory_space=pltpu.VMEM)] * 2,
        out_specs=pl.BlockSpec(memory_space=pltpu.VMEM),
        compiler_params=params(vmem_limit_bytes=48 << 20),
        name="pair_dots",
    )(ids, early, late)


def turn(count, k):
    return [(d, (d + k) % count) for d in range(count)]


def scatter_sum(values, axis, dim):
    count = lax.axis_size(axis)
    here = lax.axis_index(axis)
    piece = values.shape[dim] // count

    def part(owner):
        return lax.dynamic_slice_in_dim(values, owner * piece, piece, dim)

    total = part(here)
    for k in range(1, count):
        total = total + lax.ppermute(part((here + k) % count), axis, turn(count, k))
    return total


def after(values, arrived):
    return lax.optimization_barrier((values, arrived))[0]


class Lane:
    def __init__(self, arrived=None):
        self.arrived = arrived

    def send(self, values, axis, routes):
        if self.arrived is not None:
            values = after(values, self.arrived)
        self.arrived = [lax.ppermute(v, axis, route) for v, route in zip(values, routes)]
        return self.arrived


def along_line(block, inner):
    near = lax.ppermute(block, "z", NEAR)
    middle = lax.ppermute(block, "z", MIDDLE)
    far = lax.ppermute(near, "z", MIDDLE)
    out1 = lax.ppermute(middle, "z", OUTWARD)
    out2 = lax.ppermute(far, "z", OUTWARD)
    return [block, near, jnp.where(inner, middle, out1), jnp.where(inner, far, out2)]


def dense(hist, tile_mask, planes, pairs):
    sess, act = ("z", "x"), ("y", "core")
    rows, acts = hist.shape
    row_blocks, act_blocks = tile_mask.shape
    blk = rows // row_blocks
    masked = (
        hist.reshape(row_blocks, blk, act_blocks, blk)
        * (tile_mask != 0).astype(jnp.bfloat16)[:, None, :, None]
    ).reshape(rows, acts)
    partial_proj = jnp.dot(
        masked, lax.all_gather(planes, sess, axis=1, tiled=True), preferred_element_type=jnp.float32
    )
    proj = lax.psum_scatter(partial_proj, act, scatter_dimension=1, tiled=True)
    own_count = pairs.shape[0] // lax.axis_size(act)
    place = lax.axis_index(act) * own_count
    sq = lax.psum(jnp.sum(proj * proj, axis=1), act)
    blocks = lax.all_gather(proj, sess, axis=0, tiled=True).reshape(-1, blk, proj.shape[1])
    norms = lax.all_gather(sq, sess, axis=0, tiled=True).reshape(-1, blk)
    dots = jnp.einsum(
        "kuc,kvc->kuv", blocks[pairs[:, 0]], blocks[pairs[:, 1]], precision=lax.Precision.HIGHEST
    )
    dots = lax.psum_scatter(dots, act, scatter_dimension=0, tiled=True)
    own = lax.dynamic_slice_in_dim(pairs, place, own_count, 0)
    scale = lax.rsqrt(norms[own] / P_SIZE + 1e-06)
    return dots / P_SIZE * scale[:, 0, :, None] * scale[:, 1, None, :]


def body(hist, tile_mask, planes, pairs):
    rows, acts = hist.shape
    row_blocks, act_blocks = tile_mask.shape
    blk = rows // row_blocks
    own_planes = planes.shape[1]
    wide = lax.axis_size("x")
    x, z = lax.axis_index("x"), lax.axis_index("z")
    inner = jnp.logical_or(z == 1, z == 2)
    columns = act_blocks // wide
    tile_mask = (tile_mask != 0).astype(jnp.int32)

    lent = columns * LENT[0] // LENT[1] // STRIDE * STRIDE
    kept = columns - lent
    cuts = [0, (kept // 3 + STRIDE // 2) // STRIDE * STRIDE, kept, columns]
    widths = [b - a for a, b in zip(cuts[:-1], cuts[1:])]
    slots = [room(w * row_blocks) for w in widths]

    def mask_of(owner):
        return lax.dynamic_slice_in_dim(tile_mask, owner * columns, columns, 1)

    def over_x(make):
        return [lax.ppermute(make((x + k) % wide), "x", turn(wide, k)) for k in range(1, wide)]

    others = [(x + k) % wide for k in range(1, wide)]
    row_routes = [turn(wide, k) for k in range(1, wide)]

    def in_row_order(parts, dim):
        ordered = []
        for owner in range(wide):
            chosen = parts[0]
            for k in range(1, wide):
                chosen = jnp.where((x - owner) % wide == k, parts[k], chosen)
            ordered.append(chosen)
        return jnp.concatenate(ordered, axis=dim)

    def planes_of(owner, c):
        return lax.dynamic_slice_in_dim(planes, (owner * columns + cuts[c]) * blk, widths[c] * blk, 0)

    def packed(owner, c, later):
        mask = after(mask_of(owner)[:, cuts[c] : cuts[c + 1]], later)
        return pack(hist, mask, owner * columns + cuts[c], slots[c])

    over_x = Lane()
    both_masks = jnp.stack([tile_mask, lax.ppermute(tile_mask, "z", INWARD)])

    def both_of(owner):
        return lax.dynamic_slice_in_dim(both_masks, owner * columns, columns, 2)

    known = [both_of(x)] + [lax.ppermute(both_of(o), "x", r) for o, r in zip(others, row_routes)]
    listed = [pairs] + [lax.ppermute(pairs, "x", route) for route in row_routes]
    masks, guest_masks = [m[0] for m in known], [m[1][:, kept:] for m in known]
    groups = []
    for c in range(3):
        got = over_x.send([planes_of(o, c) for o in others], "x", row_routes)
        groups.append(in_row_order([planes_of(x, c)] + got, 1))
        if c == 0:
            over_x.arrived = got + known[1:] + listed[1:]
    tiles = [None] * 3
    for c in (0, 2, 1):
        tiles[c] = over_x.send([packed(o, c, groups[0]) for o in others], "x", row_routes)

    ends, middle = Lane(), Lane()
    near, mid, far = [], [], []
    for c in range(2):
        near += ends.send([groups[c]], "z", [NEAR])
        mid += middle.send([groups[c]], "z", [MIDDLE])
    inward, outward = Lane(near[1:]), Lane(near[1:])
    for c in range(2):
        far += middle.send([near[c]], "z", [MIDDLE])
    loans = inward.send([packed(x, 2, near[0])], "z", [INWARD])
    near += inward.send([groups[2]], "z", [INWARD])
    mid += middle.send([groups[2]], "z", [MIDDLE])
    far += middle.send([near[2]], "z", [MIDDLE])
    outer = [outward.send([v], "z", [OUTWARD])[0] for v in mid[:2]]
    loans = loans + inward.send(tiles[2], "z", [INWARD] * len(others))
    over = jnp.int32(0)
    for c in range(3):
        for owner in range(wide):
            count = jnp.sum(tile_mask[:, owner * columns + cuts[c] : owner * columns + cuts[c + 1]])
            over = jnp.maximum(over, (count > slots[c]).astype(jnp.int32))
    row_places = [(x - k) % wide * rows for k in range(wide)]
    early_groups = [[[groups[c]], [near[c]], [mid[c], outer[c]]] for c in range(2)]

    def times(c, sources, which, held, places):
        own = [masks[k][:, cuts[c] : cuts[c + 1]] for k in which]
        return product(sources, own, held, inner, x * columns + cuts[c], places)

    every = range(wide)
    part0 = times(0, [hist] + tiles[0], every, early_groups[0], row_places)
    outer += outward.send([after(far[1], part0)], "z", [OUTWARD])
    part1 = [times(1, [hist], [0], early_groups[1], [0])]
    part2 = times(2, [hist] + tiles[2], every, [[groups[2]], [near[2]], [mid[2]]], row_places)
    guest = product([loans[0]], [guest_masks[0]], [[groups[2]], [mid[2]]], inner, 0, [0])
    outer += outward.send([after(far[0], [part1[0], part2, guest])], "z", [OUTWARD])
    part1 += [times(1, [tiles[1][k - 1]], [k], early_groups[1], [0]) for k in range(1, wide)]
    first_three = part0 + part2 + in_row_order(part1, 2)

    end2 = times(2, [hist] + tiles[2], every, [[far[2]]], row_places)
    first_three = scatter_sum(first_three, "core", 1)
    end1 = product(
        [hist] + tiles[1], [m[:, cuts[1] : cuts[2]] for m in masks], [[far[1], outer[2]]],
        after(inner, first_three), x * columns + cuts[1], row_places,
    )
    end0 = times(0, [hist] + tiles[0], every, [[far[0], outer[3]]], row_places)
    last_one = end0 + (end1 + end2)
    guest = jnp.concatenate([guest, product([loans[0]], [guest_masks[0]], [[far[2]]], inner, 0, [0])])
    visitors = in_row_order(
        [guest]
        + [
            product([t], [m], [[groups[2]], [mid[2]], [far[2]]], inner, 0, [0])
            for t, m in zip(loans[1:], guest_masks[1:])
        ],
        2,
    )

    def summed(totals):
        return scatter_sum(scatter_sum(scatter_sum(totals, "core", 1), "x", 1), "y", 1)

    first_three = scatter_sum(scatter_sum(first_three, "x", 1), "y", 1)
    visitors = lax.ppermute(summed(visitors), "z", OUTWARD)
    early = first_three.at[1:].add(visitors[:2])
    early = jnp.stack(along_line(early, inner))
    last_one = summed(last_one)[0] + visitors[2]
    flags = jnp.full((8, last_one.shape[1]), over.astype(jnp.float32))
    late = jnp.stack(along_line(jnp.concatenate([last_one, flags]), inner))

    order = (x - jnp.arange(wide)) % wide
    all_pairs = jnp.stack(listed)[order].reshape(-1, 2).T
    plane_blocks = wide * row_blocks
    of_plane = all_pairs // plane_blocks
    places = jnp.moveaxis(jnp.asarray(PLACE)[of_plane], 2, 1)
    ids = jnp.concatenate(
        [jnp.asarray(PLACE)[z][of_plane][:, None], (all_pairs % plane_blocks)[:, None], places], axis=1
    )
    sums = pair_dots(early, late, ids, blk)
    high, cores = lax.axis_size("y"), lax.axis_size("core")
    sums = sums.reshape((wide, high, cores, -1) + sums.shape[1:])
    sums = scatter_sum(sums, "core", 2)
    half = sums.shape[3] // 2
    by_x = scatter_sum(scatter_sum(sums[:, :, :, :half], "x", 0), "y", 1)
    by_y = scatter_sum(scatter_sum(sums[:, :, :, half:], "y", 1), "x", 0)
    sums = jnp.concatenate([by_x, by_y], axis=3)
    own = sums.reshape((-1,) + sums.shape[4:])
    scale = lax.rsqrt(own[:, blk : blk + 2] / P_SIZE + 1e-06)
    scores = own[:, :blk] / P_SIZE * scale[:, 0, :, None] * scale[:, 1, None, :]
    crowded = own[0, blk + 2, 0] > 0
    return lax.cond(crowded, lambda: dense(hist, tile_mask, planes, pairs), lambda: scores)


def solution(mesh):
    sess, act = mesh.shape["sess"], mesh.shape["act"]
    fine = Mesh(
        mesh.devices.reshape(DEPTH, sess // DEPTH, act // CORES, CORES), ("z", "x", "y", "core")
    )
    sess_axes, act_axes = ("z", "x"), ("y", "core")
    placed = (
        P(sess_axes, act_axes), P(sess_axes, act_axes), P(act_axes, sess_axes), P(sess_axes, None)
    )
    return jax.shard_map(
        body, mesh=fine, in_specs=placed, out_specs=P(sess_axes + act_axes, None, None), check_vma=False
    )
```
